32 devices in a mesh: dp: 8 (over y, x, core), mp: 4 (over z).
Axes of the slice: x: 2, y: 2, z: 4, core: 2. Of those that a mesh axis runs over, the one named last changes fastest.
Arguments:
- tokens: bfloat16 [16384, 768], P(('dp', 'mp')), may hold values from -6 to 6
- region_mask: int32 [128, 128], P('dp'), may hold values from 0 to 1, as said below
- attn_gain: bfloat16 [768], replicated, may hold values from 0.25 to 1.75
- self_qkv: bfloat16 [3, 768, 768], P(None, 'mp'), may hold values from -0.21875 to 0.21875
- cross_qkv: bfloat16 [3, 768, 768], P(None, 'mp'), may hold values from -0.21875 to 0.21875
- self_out: bfloat16 [768, 768], P('mp'), may hold values from -1.25 to 1.25
- cross_out: bfloat16 [768, 768], P('mp'), may hold values from -1.25 to 1.25
- gate_weight: bfloat16 [768, 768], replicated, may hold values from -0.21875 to 0.21875
- gate_bias: bfloat16 [768], replicated, may hold values from -4 to 4
- ffn_gain: bfloat16 [768], replicated, may hold values from 0.25 to 1.75
- up_weight: bfloat16 [768, 3072], P(None, 'mp'), may hold values from -0.21875 to 0.21875
- down_weight: bfloat16 [3072, 768], P('mp'), may hold values from -0.109375 to 0.109375
- out_grad: bfloat16 [16384, 768], P(('dp', 'mp')), may hold values from -6 to 6
Outputs:
- out: bfloat16 [16384, 768], P(('dp', 'mp'))
- tokens_grad: bfloat16 [16384, 768], P(('dp', 'mp'))
- attn_gain_grad: float32 [768], replicated
- self_qkv_grad: float32 [3, 768, 768], P(None, 'mp')
- cross_qkv_grad: float32 [3, 768, 768], P(None, 'mp')
- self_out_grad: float32 [768, 768], P('mp')
- cross_out_grad: float32 [768, 768], P('mp')
- gate_weight_grad: float32 [768, 768], replicated
- gate_bias_grad: float32 [768], replicated
- ffn_gain_grad: float32 [768], replicated
- up_weight_grad: float32 [768, 3072], P(None, 'mp')
- down_weight_grad: float32 [3072, 768], P('mp')
The draws below stay inside these ranges and needn't reach their ends.
Inputs may be any that keep to these rules, and one draw needn't show every extreme that they name: `region_mask`: in each page the real language regions fill the first of the 96 language slots and the real vision regions the first of the 32 vision slots; every page has one or more of each, and some page has all 128 slots real.
All inputs are finite; a program needn't handle non-finite values.
Results may differ from the reference program's by a relative error of at most 0.012.
The reference program's roundings to bfloat16 on the way count: a program that leaves them out, or rounds other values in their place, can miss the bound.
Values may be sent and summed in bfloat16 or wider, within the bound.
A program may use at most 192 MiB of HBM per device.

```python
import jax
import jax.numpy as jnp
from jax import lax

D = 768
HEADS = 12
HEAD_DIM = 64
FF = 3072
LANG = 96
VIS = 32
SLOTS = 128
PAGES_DEV = 16
PAGES = 128
TOKENS = 16384


def draw_region_mask(key, part):
    key = jax.random.fold_in(key, 11)
    subkeys = jax.random.split(key, 3)
    lang_count = jax.random.randint(subkeys[0], (PAGES, 1), 1, LANG + 1)
    vis_count = jax.random.randint(subkeys[1], (PAGES, 1), 1, VIS + 1)
    full_page = jax.random.randint(subkeys[2], (), 0, PAGES)
    page_ids = jnp.arange(PAGES)[:, None]
    lang_count = jnp.where(page_ids == full_page, LANG, lang_count)
    vis_count = jnp.where(page_ids == full_page, VIS, vis_count)
    slot_ids = jnp.arange(SLOTS)[None, :]
    live_slots = jnp.where(slot_ids < LANG, slot_ids < lang_count, slot_ids - LANG < vis_count)
    return live_slots.astype(jnp.int32)


def block_scale(key, extent, shards, low, high):
    level = 1.0
    for position, parts in shards:
        heights = jax.random.uniform(jax.random.fold_in(jax.random.fold_in(key, 6), position), (parts,), jnp.float32, low / len(shards), high / len(shards))
        level = level * jnp.repeat(jnp.exp(heights), extent[position] // parts).reshape((-1,) + (1,) * (len(extent) - 1 - position))
    return level


def gaussian(key, extent, scale, most, cuts=(), held_as=jnp.bfloat16):
    level = block_scale(key, extent, cuts, -0.22, 0.18) if cuts else 1.0
    values = jax.random.normal(key, extent, jnp.float32) * scale * level
    return jnp.minimum(jnp.maximum(values, -most), most).astype(held_as)


def setup_inputs(seed: int = 0) -> dict:
    keys = jax.random.split(jax.random.key(seed), 14)
    return {
        "tokens": gaussian(keys[0], (TOKENS, D), 1.0, 6.0, ((0, 32),)),
        "region_mask": draw_region_mask(jax.random.fold_in(keys[13], 71), 0),
        "attn_gain": jnp.clip(1.0 + 0.15 * jax.random.normal(keys[2], (D,), jnp.float32), 0.25, 1.75).astype(jnp.bfloat16),
        "self_qkv": gaussian(keys[3], (3, D, D), D ** -0.5, 0.21875, ((1, 4),)),
        "cross_qkv": gaussian(keys[4], (3, D, D), D ** -0.5, 0.21875, ((1, 4),)),
        "self_out": gaussian(keys[5], (D, D), (D // 32) ** -0.5, 1.25, ((0, 4),)),
        "cross_out": gaussian(keys[6], (D, D), (D // 32) ** -0.5, 1.25, ((0, 4),)),
        "gate_weight": gaussian(keys[7], (D, D), D ** -0.5, 0.21875),
        "gate_bias": gaussian(keys[8], (D,), 1.0, 4.0),
        "ffn_gain": jnp.clip(1.0 + 0.15 * jax.random.normal(keys[9], (D,), jnp.float32), 0.25, 1.75).astype(jnp.bfloat16),
        "up_weight": gaussian(keys[10], (D, FF), D ** -0.5, 0.21875, ((1, 4),)),
        "down_weight": gaussian(keys[11], (FF, D), FF ** -0.5, 0.109375, ((0, 4),)),
        "out_grad": gaussian(keys[12], (TOKENS, D), 1.0, 6.0, ((0, 32),)),
    }


@jax.custom_vjp
def low(v):
    return lax.optimization_barrier(v.astype(jnp.bfloat16)).astype(jnp.float32)

@jax.custom_vjp
def low_back(v):
    return v

def low_keep(v):
    return (low(v), None)

def low_pass(kept, grad):
    return (grad,)

def back_keep(v):
    return (v, None)

def back_low(kept, grad):
    return (low(grad),)
low.defvjp(low_keep, low_pass)
low_back.defvjp(back_keep, back_low)
highest = lax.Precision.HIGHEST
epsilon = 1e-05
neg_fill = -1e+30

def normalize(values, gain):
    centre = lax.optimization_barrier(jnp.mean(values, axis=-1, keepdims=True))
    offset = values - centre
    spread = lax.optimization_barrier(jnp.mean(offset * offset, axis=-1, keepdims=True))
    return offset * lax.rsqrt(spread + epsilon) * gain

def attend(normed, weight, allowed):
    page_count = normed.shape[0]
    triple = low(low_back(jnp.einsum('psd,cfd->pscf', normed, weight, precision=highest)))
    triple = triple.reshape(page_count, SLOTS, 3, HEADS, HEAD_DIM)
    queries = triple[:, :, 0]
    keys_all = triple[:, :, 1]
    values_all = triple[:, :, 2]
    scores = low_back(jnp.einsum('pqhe,pkhe->phqk', queries, keys_all, precision=highest) * HEAD_DIM ** (-0.5))
    scores = jnp.where(allowed[:, None], scores, neg_fill)
    attention = jax.nn.softmax(scores, axis=-1)
    mixture = jnp.einsum('phqk,pkhe->pqhe', low(attention), values_all, precision=highest)
    return low(low_back(mixture.reshape(page_count, SLOTS, D)))

def layer_block(params, row_block, mark_block):
    attn_gain, self_qkv, cross_qkv, self_out, cross_out, gate_weight, gate_bias, ffn_gain, up_weight, down_weight = params
    modality = jnp.arange(SLOTS) >= LANG
    same_kind = modality[:, None] == modality[None, :]
    real_key = mark_block[:, None, :] > 0
    allow_self = same_kind[None] & real_key
    allow_cross = jnp.logical_not(same_kind)[None] & real_key
    normed = low(normalize(row_block, attn_gain))
    self_mix = attend(normed, self_qkv, allow_self)
    cross_mix = attend(normed, cross_qkv, allow_cross)
    self_branch = low_back(jnp.einsum('psd,de->pse', self_mix, self_out, precision=highest))
    cross_branch = low_back(jnp.einsum('psd,de->pse', cross_mix, cross_out, precision=highest))
    gate_open = jax.nn.sigmoid(low_back(jnp.einsum('psd,de->pse', normed, gate_weight, precision=highest) + gate_bias))
    middle = row_block + gate_open * self_branch + (1.0 - gate_open) * cross_branch
    normed_two = low(normalize(middle, ffn_gain))
    inner_act = low_back(jnp.einsum('psd,df->psf', normed_two, up_weight, precision=highest))
    hidden = low(jax.nn.gelu(inner_act, approximate=True))
    return middle + jnp.einsum('psf,fd->psd', hidden, down_weight, precision=highest)

def reference(tokens, region_mask, attn_gain, self_qkv, cross_qkv, self_out, cross_out, gate_weight, gate_bias, ffn_gain, up_weight, down_weight, out_grad):
    params = tuple((weight.astype(jnp.float32) for weight in (attn_gain, self_qkv, cross_qkv, self_out, cross_out, gate_weight, gate_bias, ffn_gain, up_weight, down_weight)))
    groups = PAGES // PAGES_DEV
    row_groups = tokens.astype(jnp.float32).reshape(groups, PAGES_DEV, SLOTS, D)
    mark_groups = region_mask.reshape(groups, PAGES_DEV, SLOTS)
    checked = jax.checkpoint(layer_block)

    def forward(weights, row_data):

        def scan_step(scan_carry, page_pair):
            return (scan_carry, checked(weights, page_pair[0], page_pair[1]))
        _, outputs = lax.scan(scan_step, jnp.zeros((), jnp.float32), (row_data, mark_groups))
        return outputs
    result, pullback = jax.vjp(forward, params, row_groups)
    grad_params, grad_rows = pullback(out_grad.astype(jnp.float32).reshape(groups, PAGES_DEV, SLOTS, D))
    out = result.reshape(TOKENS, D).astype(jnp.bfloat16)
    tokens_grad = grad_rows.reshape(TOKENS, D).astype(jnp.bfloat16)
    return (out, tokens_grad, grad_params[0], grad_params[1], grad_params[2], grad_params[3], grad_params[4], grad_params[5], grad_params[6], grad_params[7], grad_params[8], grad_params[9])
```

```python
import functools

import jax
import jax.numpy as jnp
from jax import lax
from jax.experimental import pallas as pl
from jax.experimental.pallas import tpu as pltpu
from jax.sharding import PartitionSpec as P

HEAD = 64
LANG = 96
SLOTS = 128
EPS = 1e-5
NEG = -1e30
GC = 0.7978845608028654
GK = 0.044715
f32 = jnp.float32
bf16 = jnp.bfloat16
MESH = pl.DeviceIdType.MESH


def mm(lhs, rhs, form):
    dims = {"nn": ((1,), (0,)), "nt": ((1,), (1,)), "tn": ((0,), (0,))}[form]
    return lax.dot_general(lhs, rhs, (dims, ((), ())), preferred_element_type=f32)


def blk(start, size, align):
    return pl.ds(pl.multiple_of(start, align), size)


def standardize(rows):
    centre = jnp.mean(rows, axis=1, keepdims=True)
    offset = rows - centre
    spread = jnp.mean(offset * offset, axis=1, keepdims=True)
    inv = lax.rsqrt(spread + EPS)
    return offset * inv, inv


def layer_kernel(
    x_ref, og_ref, bias_ref, again_ref, fgain_ref, gate_ref, gbias_ref,
    sq_ref, cq_ref, so_ref, co_ref, up_ref, dn_ref,
    out_ref, tg_ref, fin, gout, vec_ref,
    buf, crecv, p1a, p1b, p2a, p2b, zrv, gg, gcr, gxr, gyr, gzr, vs, vr, vz,
    h, qkv, o, lse, sc, aa, mid, h2, acc, gh, eb, wb, gz,
    loc, az_s, az_r, a1_s, a1_r, a2_s, a2_r, ac_s, ac_r,
    rc_s, rc_r, r1_s, r1_r, r2_s, r2_r, rz_s, rz_r,
    f1_s, f1_r, f2_s, f2_r, fc_s, fc_r, fl,
    g_s, g_r, gz_s, gz_r, ga_s, ga_r, gl, v_s, v_r, vz_s, vz_r,
):
    R, D = x_ref.shape
    CH = buf.shape[3]
    XH, YH = CH // 2, D // 2
    AR = XH // 2
    QR = sq_ref.shape[0]
    F = QR // 3
    heads = F // HEAD
    pages = R // SLOTS
    GX = gg.shape[2] // 2

    dp = lax.axis_index("dp")
    z = lax.axis_index("mp")
    c = dp % 2
    x = (dp // 2) % 2
    y = (dp // 4) % 2
    s = z // 2
    ismid = (z + s) % 2
    dev_c = (dp + 1 - 2 * c, z)
    dev_x = (dp + 2 - 4 * x, z)
    dev_y = (dp + 4 - 8 * y, z)

    def zof(slot):
        b0, b1 = slot % 2, slot // 2
        near = (1 - b0) * z + b0 * (4 * s + 1 - z)
        far = (1 - b0) * (2 - s) + b0 * (3 - 3 * s)
        return (1 - b1) * near + b1 * far

    def seen_as(slot):
        is1 = 1 - slot // 2
        return is1 + (1 - is1) * (3 - ismid)

    def remote(src, dst, ss, rs, dev):
        return pltpu.make_async_remote_copy(
            src_ref=src, dst_ref=dst, send_sem=ss, recv_sem=rs, device_id=dev, device_id_type=MESH
        )

    bar = pltpu.get_barrier_semaphore()
    partners = (dev_c, dev_x, dev_y, (dp, zof(1)), (dp, zof(2)), (dp, zof(3)))
    for dev in partners:
        pl.semaphore_signal(bar, inc=1, device_id=dev, device_id_type=MESH)

    local = []
    for i, (src, g, cc, r0) in enumerate(
        (
            (sq_ref, 0, 0, 0), (so_ref, 0, 0, QR), (cq_ref, 0, 1, 0), (co_ref, 0, 1, QR),
            (up_ref, 1, 0, 0), (dn_ref, 1, 1, 0),
        )
    ):
        cp = pltpu.make_async_copy(src, buf.at[g, cc, z, pl.ds(r0, src.shape[0]), :], loc.at[i])
        cp.start()
        local.append(cp)

    def wpart(g, cc, zz, r0, nr, c0, nc):
        return buf.at[g, cc, zz, blk(r0, nr, 16), blk(c0, nc, 128)]

    def wquarter(g, zz):
        return wpart(g, c, zz, XH * x, XH, YH * y, YH)

    def z_copy(g, zz, slot_to, sidx, rslot):
        ref = wquarter(g, zz)
        return remote(ref, ref, az_s.at[g, sidx], az_r.at[g, rslot], (dp, zof(slot_to)))

    def ag_zsend(g):
        z_copy(g, z, 1, 0, 1).start()

        @pl.when(ismid == 1)
        def _():
            z_copy(g, z, 2, 1, 2).start()

    def ag_zsend_wait(g):
        z_copy(g, z, 1, 0, 1).wait_send()

        @pl.when(ismid == 1)
        def _():
            for i in range(1, 5):
                z_copy(g, z, 1, i, 1).wait_send()

    def ag_p1(g, j):
        zz = zof(j)
        ra = wpart(g, c, zz, XH * x, AR, YH * y, YH)
        rb = wpart(g, c, zz, XH * x + AR, AR, YH * y, YH)
        ia = wpart(g, c, zz, XH * (1 - x), AR, YH * y, YH)
        ib = wpart(g, c, zz, XH * x + AR, AR, YH * (1 - y), YH)
        return (
            (remote(ra, ra, a1_s.at[g, j, 0], a1_r.at[g, j, 0], dev_x),
             remote(rb, rb, a1_s.at[g, j, 1], a1_r.at[g, j, 1], dev_y)),
            (remote(ia, ia, a1_s.at[g, j, 0], a1_r.at[g, j, 0], dev_x),
             remote(ib, ib, a1_s.at[g, j, 1], a1_r.at[g, j, 1], dev_y)),
        )

    def ag_p2(g, j):
        zz = zof(j)
        outs, ins = [], []
        for xx in range(2):
            ra = wpart(g, c, zz, XH * xx, AR, YH * y, YH)
            ia = wpart(g, c, zz, XH * xx, AR, YH * (1 - y), YH)
            outs.append(remote(ra, ra, a2_s.at[g, j, xx], a2_r.at[g, j, xx], dev_y))
            ins.append(remote(ia, ia, a2_s.at[g, j, xx], a2_r.at[g, j, xx], dev_y))
        rb = wpart(g, c, zz, XH * x + AR, AR, 0, D)
        ib = wpart(g, c, zz, XH * (1 - x) + AR, AR, 0, D)
        outs.append(remote(rb, rb, a2_s.at[g, j, 2], a2_r.at[g, j, 2], dev_x))
        ins.append(remote(ib, ib, a2_s.at[g, j, 2], a2_r.at[g, j, 2], dev_x))
        return outs, ins

    def ag_c(g, j):
        zz = zof(j)
        mine, theirs = buf.at[g, c, zz], buf.at[g, 1 - c, zz]
        return (
            remote(mine, mine, ac_s.at[g, j], ac_r.at[g, j], dev_c),
            remote(theirs, theirs, ac_s.at[g, j], ac_r.at[g, j], dev_c),
        )

    def pump_ag(t):
        @pl.when(t < 6)
        def _():
            g, j = t // 3, t % 3 + 1
            z_copy(g, zof(j), 1, 0, j).wait_recv()

            @pl.when(ismid == 1)
            def _():
                is1 = 1 - j // 2
                z_copy(g, zof(j), 2 * is1 + 1 - is1, j + 1, 3 * is1 + j * (1 - is1)).start()

            for cp in ag_p1(g, j)[0]:
                cp.start()

        @pl.when((t >= 1) & (t < 7))
        def _():
            g, j = (t - 1) // 3, (t - 1) % 3 + 1
            outs, ins = ag_p1(g, j)
            for cp in ins:
                cp.wait_recv()
            for cp in ag_p2(g, j)[0]:
                cp.start()
            for cp in outs:
                cp.wait_send()

        @pl.when((t >= 2) & (t < 8))
        def _():
            g, j = (t - 2) // 3, (t - 2) % 3 + 1
            outs, ins = ag_p2(g, j)
            for cp in ins:
                cp.wait_recv()
            ag_c(g, j)[0].start()
            for cp in outs:
                cp.wait_send()

    def ag_done(g, j):
        mine, theirs = ag_c(g, j)
        theirs.wait_recv()
        mine.wait_send()

    def add_rows(dst, dst_idx, r0, nr, c0, nc, src, src_idx):
        step = 64 if nr % 64 == 0 else 48

        @pl.loop(0, nr // step)
        def _(i):
            rows = blk(r0 + i * step, step, 16)
            cols = blk(c0, nc, 128)
            d = dst[(*dst_idx, rows, cols)].astype(f32)
            t = src[(*src_idx, blk(i * step, step, 16), slice(None))].astype(f32)
            dst[(*dst_idx, rows, cols)] = (d + t).astype(bf16)

    def rs_c(n):
        return remote(buf.at[2 - n // 4, 1 - c, n % 4], crecv.at[n % 4], rc_s.at[n], rc_r.at[n], dev_c)

    def rs_p1(n):
        b, k = 2 - n // 4, n % 4
        cps = [remote(buf.at[b, c, k, blk(XH * (1 - x), AR, 16), :], p1a.at[k], r1_s.at[n, 0], r1_r.at[n, 0], dev_x)]
        for xx in range(2):
            cps.append(
                remote(
                    buf.at[b, c, k, pl.ds(XH * xx + AR, AR), blk(YH * (1 - y), YH, 128)],
                    p1b.at[k, xx], r1_s.at[n, 1 + xx], r1_r.at[n, 1 + xx], dev_y,
                )
            )
        return cps

    def rs_p2(n):
        b, k = 2 - n // 4, n % 4
        return [
            remote(
                buf.at[b, c, k, blk(XH * x, AR, 16), blk(YH * (1 - y), YH, 128)],
                p2a.at[k], r2_s.at[n, 0], r2_r.at[n, 0], dev_y,
            ),
            remote(
                buf.at[b, c, k, blk(XH * (1 - x) + AR, AR, 16), blk(YH * y, YH, 128)],
                p2b.at[k], r2_s.at[n, 1], r2_r.at[n, 1], dev_x,
            ),
        ]

    def rs_z(n, rslot):
        b, k, g = 2 - n // 4, n % 4, n // 4
        return remote(
            buf.at[b, c, k, blk(XH * x, XH, 16), blk(YH * y, YH, 128)],
            zrv.at[g, rslot - 1], rz_s.at[n], rz_r.at[g, rslot], (dp, zof(k)),
        )

    def pump_rs(t):
        def chunk(v):
            return v - v // 5

        def has(v):
            return (v >= 0) & (v < 9) & (v != 4)

        @pl.when(has(t))
        def _():
            rs_c(chunk(t)).start()

        @pl.when(has(t - 1))
        def _():
            n = chunk(t - 1)
            cp = rs_c(n)
            cp.wait_recv()
            add_rows(buf, (2 - n // 4, c, n % 4), 0, CH, 0, D, crecv, (n % 4,))
            for q in rs_p1(n):
                q.start()
            cp.wait_send()

        @pl.when(has(t - 2))
        def _():
            n = chunk(t - 2)
            idx = (2 - n // 4, c, n % 4)
            cps = rs_p1(n)
            for q in cps:
                q.wait_recv()
            add_rows(buf, idx, XH * x, AR, 0, D, p1a, (n % 4,))
            for xx in range(2):
                add_rows(buf, idx, XH * xx + AR, AR, YH * y, YH, p1b, (n % 4, xx))
            for q in rs_p2(n):
                q.start()
            for q in cps:
                q.wait_send()

        @pl.when(has(t - 3))
        def _():
            n = chunk(t - 3)
            idx = (2 - n // 4, c, n % 4)
            cps = rs_p2(n)
            for q in cps:
                q.wait_recv()
            add_rows(buf, idx, XH * x, AR, YH * y, YH, p2a, (n % 4,))
            add_rows(buf, idx, XH * x + AR, AR, YH * y, YH, p2b, (n % 4,))

            @pl.when(n % 4 != 0)
            def _():
                rs_z(n, seen_as(n % 4)).start()

            for q in cps:
                q.wait_send()

    def fin_part(g, r0, nr, c0, nc):
        return fin.at[g, c, blk(r0, nr, 16), blk(c0, nc, 128)]

    def fin_p1(g):
        b = 2 - g
        return [
            remote(
                buf.at[b, c, 0, blk(XH * x, AR, 16), blk(YH * y, YH, 128)],
                fin_part(g, XH * x, AR, YH * y, YH), f1_s.at[g, 0], f1_r.at[g, 0], dev_x,
            ),
            remote(
                buf.at[b, c, 0, blk(XH * x + AR, AR, 16), blk(YH * y, YH, 128)],
                fin_part(g, XH * x + AR, AR, YH * y, YH), f1_s.at[g, 1], f1_r.at[g, 1], dev_y,
            ),
        ]

    def fin_local(g):
        return pltpu.make_async_copy(
            buf.at[2 - g, c, 0, blk(XH * x, XH, 16), blk(YH * y, YH, 128)],
            fin_part(g, XH * x, XH, YH * y, YH), fl.at[g],
        )

    def fin_p2(g):
        cps = []
        for xx in range(2):
            ref = fin_part(g, XH * xx, AR, YH * y, YH)
            cps.append(remote(ref, ref, f2_s.at[g, xx], f2_r.at[g, xx], dev_y))
        ref = fin_part(g, XH * x + AR, AR, 0, D)
        cps.append(remote(ref, ref, f2_s.at[g, 2], f2_r.at[g, 2], dev_x))
        return cps

    def fin_c(g):
        return remote(fin.at[g, c], fin.at[g, c], fc_s.at[g], fc_r.at[g], dev_c)

    def fin_step0(g):
        b = 2 - g
        for slot in range(1, 4):
            rs_z(4 * g + slot, slot).wait_recv()
        for i in range(XH // 64):
            rows = blk(XH * x + 64 * i, 64, 16)
            cols = blk(YH * y, YH, 128)
            t = buf[b, c, 0, rows, cols].astype(f32)
            for slot in range(3):
                t = t + zrv[g, slot, pl.ds(64 * i, 64), :].astype(f32)
            buf[b, c, 0, rows, cols] = t.astype(bf16)
        fin_local(g).start()
        for q in fin_p1(g):
            q.start()
        for slot in range(1, 4):
            rs_z(4 * g + slot, slot).wait_send()

    def fin_step1(g):
        for q in fin_p1(g):
            q.wait_recv()
        fin_local(g).wait()
        for q in fin_p2(g):
            q.start()
        for q in fin_p1(g):
            q.wait_send()

    def fin_step2(g):
        for q in fin_p2(g):
            q.wait_recv()
        fin_c(g).start()
        for q in fin_p2(g):
            q.wait_send()

    def fin_step3(g):
        fin_c(g).wait_recv()
        fin_c(g).wait_send()

    def g_copy(i):
        xs, xo = blk(GX * x, GX, 16), blk(GX * (1 - x), GX, 16)
        ys, yo = blk(YH * y, YH, 128), blk(YH * (1 - y), YH, 128)
        src, dst, dev = {
            0: lambda: (gg.at[:, 1 - c], gcr, dev_c),
            1: lambda: (gg.at[:, c, xo, :], gxr, dev_x),
            2: lambda: (gg.at[:, c, xs, yo], gyr, dev_y),
            3: lambda: (gout.at[:, c, xs, ys], gout.at[:, c, xs, ys], dev_y),
            4: lambda: (gout.at[:, c, xs, :], gout.at[:, c, xs, :], dev_x),
            5: lambda: (gout.at[:, c], gout.at[:, c], dev_c),
        }[i]()
        return remote(src, dst, g_s.at[i], g_r.at[i], dev)

    def g_z(slot, rslot):
        src = gg.at[zof(slot), c, blk(GX * x, GX, 16), blk(YH * y, YH, 128)]
        return remote(src, gzr.at[rslot - 1], gz_s.at[slot], gz_r.at[rslot], (dp, zof(slot)))

    def g_za(slot, rslot):
        src = gg.at[z, c, blk(GX * x, GX, 16), blk(YH * y, YH, 128)]
        dst = gout.at[z, c, blk(GX * x, GX, 16), blk(YH * y, YH, 128)]
        return remote(src, dst, ga_s.at[slot], ga_r.at[rslot], (dp, zof(slot)))

    def g_local():
        src = gg.at[z, c, blk(GX * x, GX, 16), blk(YH * y, YH, 128)]
        dst = gout.at[z, c, blk(GX * x, GX, 16), blk(YH * y, YH, 128)]
        return pltpu.make_async_copy(src, dst, gl.at[0])

    def g_step(i):
        xs, ys = blk(GX * x, GX, 16), blk(YH * y, YH, 128)
        if i == 0:
            g_copy(0).start()
        if i == 1:
            g_copy(0).wait_recv()
            for q in range(4):
                add_rows(gg, (q, c), 0, 2 * GX, 0, D, gcr, (q,))
            g_copy(1).start()
            g_copy(0).wait_send()
        if i == 2:
            g_copy(1).wait_recv()
            for q in range(4):
                add_rows(gg, (q, c), GX * x, GX, 0, D, gxr, (q,))
            g_copy(2).start()
            g_copy(1).wait_send()
        if i == 3:
            g_copy(2).wait_recv()
            for q in range(4):
                add_rows(gg, (q, c), GX * x, GX, YH * y, YH, gyr, (q,))
            for slot in range(1, 4):
                g_z(slot, seen_as(slot)).start()
            g_copy(2).wait_send()
        if i == 4:
            for slot in range(1, 4):
                g_z(slot, slot).wait_recv()
            t = gg[z, c, xs, ys].astype(f32)
            for slot in range(3):
                t = t + gzr[slot].astype(f32)
            gg[z, c, xs, ys] = t.astype(bf16)
            g_local().start()
            for slot in range(1, 4):
                g_za(slot, seen_as(slot)).start()
            for slot in range(1, 4):
                g_z(slot, slot).wait_send()
        if i == 5:
            for slot in range(1, 4):
                g_za(slot, slot).wait_recv()
            g_local().wait()
            g_copy(3).start()
            for slot in range(1, 4):
                g_za(slot, slot).wait_send()
        if i == 6:
            g_copy(3).wait_recv()
            g_copy(4).start()
            g_copy(3).wait_send()
        if i == 7:
            g_copy(4).wait_recv()
            g_copy(5).start()
            g_copy(4).wait_send()
        if i == 8:
            g_copy(5).wait_recv()
            g_copy(5).wait_send()

    def v_copy(i):
        return remote(vs.at[i], vr.at[i], v_s.at[i], v_r.at[i], (dev_c, dev_x, dev_y)[i])

    def v_z(slot, zz_dst, rslot):
        return remote(vz.at[z], vz.at[zz_dst], vz_s.at[slot], vz_r.at[rslot], (dp, zof(slot)))

    def v_step(i):
        if i == 0:
            v_copy(0).start()
        if i in (1, 2):
            v_copy(i - 1).wait_recv()
            vs[i] = vs[i - 1] + vr[i - 1]
            v_copy(i).start()
            v_copy(i - 1).wait_send()
        if i == 3:
            v_copy(2).wait_recv()
            vz[z] = vs[2] + vr[2]
            for slot in range(1, 4):
                v_z(slot, z, seen_as(slot)).start()
            v_copy(2).wait_send()
        if i == 4:
            for slot in range(1, 4):
                v_z(slot, z, slot).wait_recv()
            vec_ref[...] = (vz[0] + vz[1]) + (vz[2] + vz[3])
            for slot in range(1, 4):
                v_z(slot, z, slot).wait_send()

    pl.semaphore_wait(bar, 6)
    for cp in local[:4]:
        cp.wait()
    ag_zsend(0)

    TR = 64
    again = again_ref[...].astype(f32)
    fgain = fgain_ref[...].astype(f32)
    gbias = gbias_ref[...].astype(f32)

    @pl.loop(0, R // TR)
    def _(i):
        rows = blk(i * TR, TR, 16)
        u, _inv = standardize(x_ref[rows, :].astype(f32))
        h[rows, :] = (u * again).astype(bf16)
        sc[rows, :] = jnp.zeros((TR, D), f32)
        mid[rows, :] = jnp.zeros((TR, D), f32)
        gh[rows, :] = jnp.zeros((TR, D), f32)

    vs[...] = jnp.zeros_like(vs)
    for cp in local[4:]:
        cp.wait()
    ag_zsend(1)
    pump_ag(0)

    @pl.loop(0, R // 128)
    def _(i):
        rows = blk(i * 128, 128, 16)
        aa[rows, :] = jax.nn.sigmoid(mm(h[rows, :], gate_ref[...], "nn") + gbias)

    pump_ag(1)

    @pl.loop(0, 4)
    def _(k):
        zz = zof(k)

        @pl.when(k > 0)
        def _():
            ag_done(0, k)

        for at in range(2):
            qkv[at, k] = mm(buf[0, at, zz, 0:QR, :], h[...], "nt").astype(bf16)

        @pl.loop(0, pages)
        def _(p):
            cols = blk(p * SLOTS, SLOTS, 128)
            for at in range(2):
                for hh in range(heads):
                    qt = qkv[at, k, HEAD * hh : HEAD * (hh + 1), cols]
                    kt = qkv[at, k, F + HEAD * hh : F + HEAD * (hh + 1), cols]
                    vt = qkv[at, k, 2 * F + HEAD * hh : 2 * F + HEAD * (hh + 1), cols]
                    st = mm(kt, qt, "tn") * HEAD ** (-0.5) + bias_ref[at, p]
                    top = jnp.max(st, axis=0, keepdims=True)
                    ex = jnp.exp(st - top)
                    tot = jnp.sum(ex, axis=0, keepdims=True)
                    pt = (ex * (1.0 / tot)).astype(bf16)
                    lse[at, k, hh : hh + 1, cols] = top + jnp.log(tot)
                    o[at, k, HEAD * hh : HEAD * (hh + 1), cols] = mm(vt, pt, "nn").astype(bf16)

        for at, dst in ((0, sc), (1, mid)):
            dst[...] += mm(o[at, k], buf[0, at, zz, QR:CH, :], "tn")
        pump_ag(k + 2)

    ag_zsend_wait(0)

    @pl.loop(0, R // TR)
    def _(i):
        rows = blk(i * TR, TR, 16)
        a = aa[rows, :]
        sv, cv = sc[rows, :], mid[rows, :]
        mv = x_ref[rows, :].astype(f32) + a * sv + (1.0 - a) * cv
        sc[rows, :] = sv - cv
        mid[rows, :] = mv
        acc[rows, :] = mv
        u, _inv = standardize(mv)
        h2[rows, :] = (u * fgain).astype(bf16)

    @pl.loop(0, 4)
    def _(k):
        zz = zof(k)

        @pl.when(k > 0)
        def _():
            ag_done(1, k)

        MT = 256

        @pl.loop(0, R // MT)
        def _(i):
            rows = blk(i * MT, MT, 16)
            w = mm(h2[rows, :], buf[1, 0, zz], "nn")
            ge = mm(og_ref[rows, :], buf[1, 1, zz], "nt")
            w2 = w * w
            th = jnp.tanh(GC * w * (1.0 + GK * w2))
            half = 0.5 * (1.0 + th)
            eb[rows, :] = (w * half).astype(bf16)
            dg = half + 0.5 * w * (1.0 - th * th) * (GC * (1.0 + 3.0 * GK * w2))
            wb[rows, :] = (dg * ge).astype(bf16)

        @pl.loop(0, R // MT)
        def _(i):
            rows = blk(i * MT, MT, 16)
            acc[rows, :] += mm(eb[rows, :], buf[1, 1, zz], "nn")
            gh[rows, :] += mm(wb[rows, :], buf[1, 0, zz], "nt")

        @pl.loop(0, CH // 256)
        def _(i):
            cols = blk(i * 256, 256, 128)
            buf[2, 1, k, blk(i * 256, 256, 16), :] = mm(eb[:, cols], og_ref[...], "tn").astype(bf16)
            buf[2, 0, k, blk(i * 256, 256, 16), :] = mm(h2[:, cols], wb[...], "tn").astype(bf16)

        pump_rs(k)

        @pl.when(k < 2)
        def _():
            pump_ag(k + 6)

    ag_zsend_wait(1)

    TS = 32
    zero_row = jnp.zeros((1, D), f32)

    def mid_back(i, sums):
        gain_sum, bias_sum = sums
        rows = blk(i * TS, TS, 16)
        ov = acc[rows, :]
        out_ref[rows, :] = ov.astype(bf16)
        u, inv = standardize(mid[rows, :])
        gy = gh[rows, :]
        gain_sum = gain_sum + jnp.sum(gy * u, axis=0, keepdims=True)
        sy = gy * fgain
        m1 = jnp.mean(sy, axis=1, keepdims=True)
        m2 = jnp.mean(sy * u, axis=1, keepdims=True)
        gm = og_ref[rows, :].astype(f32) + inv * (sy - m1 - u * m2)
        acc[rows, :] = gm
        gh[rows, :] = jnp.zeros((TS, D), f32)
        a = aa[rows, :]
        eb[rows, :] = (a * gm).astype(bf16)
        wb[rows, :] = ((1.0 - a) * gm).astype(bf16)
        gzv = (gm * sc[rows, :] * a * (1.0 - a)).astype(bf16)
        gz[rows, :] = gzv
        bias_sum = bias_sum + jnp.sum(gzv.astype(f32), axis=0, keepdims=True)
        return gain_sum, bias_sum

    gain_sum, bias_sum = lax.fori_loop(0, R // TS, mid_back, (zero_row, zero_row))
    vs[0, 1:2, :] = bias_sum
    vs[0, 2:3, :] = gain_sum
    pump_rs(4)

    for i in range(4):
        t = mm(h[:, F * i : F * (i + 1)], gz[...], "tn").astype(bf16)
        gg[i, 0] = t[: F // 2]
        gg[i, 1] = t[F // 2 :]
    g_step(0)

    @pl.loop(0, 4)
    def _(k):
        zz = zof(k)
        for at, gref in ((0, eb), (1, wb)):
            buf[1, at, k, QR:CH, :] = mm(o[at, k], gref[...], "nn").astype(bf16)
            o[at, k] = mm(buf[0, at, zz, QR:CH, :], gref[...], "nt").astype(bf16)

        @pl.loop(0, pages)
        def _(p):
            cols = blk(p * SLOTS, SLOTS, 128)
            for at in range(2):
                for hh in range(heads):
                    qs = slice(HEAD * hh, HEAD * (hh + 1))
                    ks = slice(F + HEAD * hh, F + HEAD * (hh + 1))
                    vsl = slice(2 * F + HEAD * hh, 2 * F + HEAD * (hh + 1))
                    qt = qkv[at, k, qs, cols]
                    kt = qkv[at, k, ks, cols]
                    vt = qkv[at, k, vsl, cols]
                    go = o[at, k, qs, cols]
                    st = mm(kt, qt, "tn") * HEAD ** (-0.5) + bias_ref[at, p]
                    pt = jnp.exp(st - lse[at, k, hh : hh + 1, cols])
                    gvt = mm(go, pt.astype(bf16), "nt")
                    gpt = mm(vt, go, "tn")
                    pg = pt * gpt
                    gst = (pg - pt * jnp.sum(pg, axis=0, keepdims=True)).astype(bf16)
                    gqt = mm(kt, gst, "nn") * HEAD ** (-0.5)
                    gkt = mm(qt, gst, "nt") * HEAD ** (-0.5)
                    qkv[at, k, qs, cols] = gqt.astype(bf16)
                    qkv[at, k, ks, cols] = gkt.astype(bf16)
                    qkv[at, k, vsl, cols] = gvt.astype(bf16)

        for at in range(2):
            buf[1, at, k, 0:QR, :] = mm(qkv[at, k], h[...], "nn").astype(bf16)
        pump_rs(5 + k)
        for i in range(4):

            @pl.when(k == i)
            def _():
                g_step(i + 1)

        for at in range(2):
            gh[...] += mm(qkv[at, k], buf[0, at, zz, 0:QR, :], "tn")

    @pl.loop(0, R // 128)
    def _(i):
        rows = blk(i * 128, 128, 16)
        gh[rows, :] += mm(gz[rows, :], gate_ref[...], "nt")

    def first_back(i, gain_sum):
        rows = blk(i * TS, TS, 16)
        u, inv = standardize(x_ref[rows, :].astype(f32))
        gy = gh[rows, :]
        gain_sum = gain_sum + jnp.sum(gy * u, axis=0, keepdims=True)
        sy = gy * again
        m1 = jnp.mean(sy, axis=1, keepdims=True)
        m2 = jnp.mean(sy * u, axis=1, keepdims=True)
        tg_ref[rows, :] = (acc[rows, :] + inv * (sy - m1 - u * m2)).astype(bf16)
        return gain_sum

    vs[0, 0:1, :] = lax.fori_loop(0, R // TS, first_back, zero_row)
    v_step(0)
    pump_rs(9)
    g_step(5)
    fin_step0(0)
    v_step(1)
    pump_rs(10)
    g_step(6)
    fin_step1(0)
    v_step(2)
    pump_rs(11)
    g_step(7)
    fin_step2(0)
    v_step(3)
    fin_step0(1)
    g_step(8)
    fin_step3(0)
    v_step(4)
    fin_step1(1)
    fin_step2(1)
    fin_step3(1)


def body(
    tokens, region_mask, attn_gain, self_qkv, cross_qkv, self_out, cross_out, gate_weight, gate_bias,
    ffn_gain, up_weight, down_weight, out_grad, *, outer,
):
    R, D = tokens.shape
    F = self_out.shape[0]
    QR = 3 * F
    CH = QR + F
    pages = R // SLOTS
    marks = lax.dynamic_slice_in_dim(region_mask, lax.axis_index("mp") * pages, pages, 0)
    lang = jnp.arange(SLOTS) < LANG
    same = lang[:, None] == lang[None, :]
    real = (marks > 0)[:, :, None]
    bias = jnp.stack([jnp.where(same[None] & real, 0.0, NEG), jnp.where(~same[None] & real, 0.0, NEG)]).astype(f32)

    vm = pl.BlockSpec(memory_space=pltpu.VMEM)
    hb = pl.BlockSpec(memory_space=pl.ANY)
    dma = pltpu.SemaphoreType.DMA
    XH, YH, AR, GX = CH // 2, D // 2, CH // 4, D // 16
    scratch = [
        pltpu.VMEM((3, 2, 4, CH, D), bf16),
        pltpu.VMEM((4, CH, D), bf16),
        pltpu.VMEM((4, AR, D), bf16),
        pltpu.VMEM((4, 2, AR, YH), bf16),
        pltpu.VMEM((4, AR, YH), bf16),
        pltpu.VMEM((4, AR, YH), bf16),
        pltpu.VMEM((2, 3, XH, YH), bf16),
        pltpu.VMEM((4, 2, 2 * GX, D), bf16),
        pltpu.VMEM((4, 2 * GX, D), bf16),
        pltpu.VMEM((4, GX, D), bf16),
        pltpu.VMEM((4, GX, YH), bf16),
        pltpu.VMEM((3, GX, YH), bf16),
        pltpu.VMEM((3, 8, D), f32),
        pltpu.VMEM((3, 8, D), f32),
        pltpu.VMEM((4, 8, D), f32),
        pltpu.VMEM((R, D), bf16),
        pltpu.VMEM((2, 4, QR, R), bf16),
        pltpu.VMEM((2, 4, F, R), bf16),
        pltpu.VMEM((2, 4, 8, R), f32),
        pltpu.VMEM((R, D), f32),
        pltpu.VMEM((R, D), f32),
        pltpu.VMEM((R, D), f32),
        pltpu.VMEM((R, D), bf16),
        pltpu.VMEM((R, D), f32),
        pltpu.VMEM((R, D), f32),
        pltpu.VMEM((R, D), bf16),
        pltpu.VMEM((R, D), bf16),
        pltpu.VMEM((R, D), bf16),
        dma((6,)), dma((2, 5)), dma((2, 4)), dma((2, 4, 2)), dma((2, 4, 2)), dma((2, 4, 3)), dma((2, 4, 3)),
        dma((2, 4)), dma((2, 4)),
        dma((8,)), dma((8,)), dma((8, 3)), dma((8, 3)), dma((8, 2)), dma((8, 2)), dma((8,)), dma((2, 4)),
        dma((2, 2)), dma((2, 2)), dma((2, 3)), dma((2, 3)), dma((2,)), dma((2,)), dma((2,)),
        dma((6,)), dma((6,)), dma((4,)), dma((4,)), dma((4,)), dma((4,)), dma((1,)),
        dma((3,)), dma((3,)), dma((4,)), dma((4,)),
    ]
    out, tg, fin, gout, vec = pl.pallas_call(
        layer_kernel,
        out_shape=(
            jax.ShapeDtypeStruct((R, D), bf16),
            jax.ShapeDtypeStruct((R, D), bf16),
            jax.ShapeDtypeStruct((2, 2, CH, D), bf16),
            jax.ShapeDtypeStruct((4, 2, 2 * GX, D), bf16),
            jax.ShapeDtypeStruct((8, D), f32),
        ),
        in_specs=[vm] * 7 + [hb] * 6,
        out_specs=(vm, vm, hb, hb, vm),
        scratch_shapes=scratch,
        compiler_params=pltpu.CompilerParams(
            collective_id=1, has_side_effects=True, vmem_limit_bytes=64 * 2**20 - 2**17
        ),
    )(
        tokens, out_grad, bias, attn_gain.reshape(1, D), ffn_gain.reshape(1, D), gate_weight, gate_bias.reshape(1, D),
        self_qkv.reshape(QR, D), cross_qkv.reshape(QR, D), self_out, cross_out, up_weight, down_weight,
    )
    grads = (
        vec[0], fin[1, 0, :QR].reshape(3, F, D), fin[1, 1, :QR].reshape(3, F, D), fin[1, 0, QR:], fin[1, 1, QR:],
        gout.reshape(D, D), vec[1], vec[2], fin[0, 0], fin[0, 1],
    )
    grads = tuple(g.astype(f32) for g in grads)
    if outer > 1:
        first = (lax.axis_index("dp") % 8 == 0).astype(f32)
        grads = lax.psum(tuple(g * first for g in grads), "dp")
    return (out, tg) + tuple(grads)


def solution(mesh):
    rows = P(("dp", "mp"), None)
    weights = (P(), P(None, "mp", None), P(None, "mp", None), P("mp", None), P("mp", None), P(), P(), P(), P(None, "mp"), P("mp", None))
    return jax.shard_map(
        functools.partial(body, outer=mesh.shape["dp"] // 8),
        mesh=mesh,
        in_specs=(rows, P("dp", None)) + weights + (rows,),
        out_specs=(rows, rows) + weights,
        check_vma=False,
    )
```

```python
import functools

import jax
import jax.numpy as jnp
from jax import lax
from jax.experimental import pallas as pl
from jax.experimental.pallas import tpu as pltpu
from jax.sharding import PartitionSpec as P

HEAD = 64
LANG = 96
SLOTS = 128
EPS = 1e-5
NEG = -1e30
GC = 0.7978845608028654
GK = 0.044715
f32 = jnp.float32
bf16 = jnp.bfloat16
MESH = pl.DeviceIdType.MESH

AFTER = {
    "A0p1": (("zw", 0, 1), ("ag1", 0), ("zw", 0, 2),),
    "A0p2": (("ag2", 0), ("zw", 0, 3), ("ag1", 1), ("ag3", 0), ("zs", 1),),
    "A0p3": (("ag1", 2),),
    "A0s": (("ag2", 1),),
    "gate": (("ag2", 2),),
    "A1p0": (("zw", 1, 1),),
    "A1p1": (("zw", 1, 2), ("ag1", 3),),
    "A1p3": (("ag3", 1),),
    "A2q": (("zw", 1, 3), ("ag1", 4),),
    "A2p0": (("ag3", 2),),
    "A2s": (("ag2", 3),),
    "A3p3": (("ag1", 5), ("ag2", 4),),
    "F0a": (("ag3", 3),),
    "F1a": (("rs0", 0), ("ag2", 5),),
    "F1b": (("ag3", 4),),
    "F1c": (("rs0", 1), ("rs1", 0),),
    "F2a": (("rs1", 1), ("ag3", 5),),
    "F3a": (("rs0", 2),),
    "F3c": (("rs0", 3), ("rs1", 2),),
    "mid2": (("rs1", 3),),
    "ggrad": (("rs2", 0), ("rs2", 2), ("g", 0), ("rs0", 4),),
    "B0p3": (("rs1", 4),),
    "B1o": (("rs2", 3),),
    "B1p0": (("rs3", 0), ("rs0", 5),),
    "B1p2": (("rs3", 2), ("rs1", 5),),
    "B1p3": (("rs2", 1),),
    "B2o": (("rs3", 3), ("rs0", 6),),
    "B2p0": (("rs2", 4), ("zza", 0, 2),),
    "B2p2": (("rs3", 1), ("rs1", 6),),
    "B2g": (("zza", 0, 3), ("g", 1), ("rs0", 7), ("rs2", 5),),
    "B2h": (("rs1", 7), ("rs3", 4),),
    "B3p1": (("rs3", 5), ("g", 2), ("rs2", 6),),
    "B3p3": (("fin0", 0),),
    "B3g": (("rs0", 8), ("zza", 1, 3), ("rs2", 7), ("g", 3), ("rs3", 6), ("zza", 2, 3), ("rs1", 8), ("fin1", 0), ("zza", 1, 2),),
    "B3h": (("g", 4),),
    "tail": (("g", 5), ("zza", 2, 2), ("rs3", 7), ("rs2", 8), ("v", 0), ("fin2", 0), ("v", 1), ("fin0", 1), ("g", 6), ("rs3", 8), ("fin0", 2), ("v", 2), ("fin1", 1), ("fin1", 2), ("v", 3), ("v", 4), ("fin3", 0), ("fin2", 1), ("g", 7), ("fin2", 2), ("g", 8), ("fin3", 1), ("fin3", 2),),
}


def mm(lhs, rhs, form):
    dims = {"nn": ((1,), (0,)), "nt": ((1,), (1,)), "tn": ((0,), (0,))}[form]
    return lax.dot_general(lhs, rhs, (dims, ((), ())), preferred_element_type=f32)


def blk(start, size, align):
    return pl.ds(pl.multiple_of(start, align), size)


def standardize(rows):
    centre = jnp.mean(rows, axis=1, keepdims=True)
    offset = rows - centre
    spread = jnp.mean(offset * offset, axis=1, keepdims=True)
    inv = lax.rsqrt(spread + EPS)
    return offset * inv, inv


def layer_kernel(
    x_hbm, og_hbm, gate_hbm, marks_ref, again_ref, fgain_ref, gbias_ref,
    sq_ref, cq_ref, so_ref, co_ref, up_ref, dn_ref,
    out_hbm, tg_hbm, fin, gout, vec_ref,
    buf, crecv, p1a, p1b, p2a, p2b, cr_o, p1a_o, p1b_o, p2a_o, p2b_o,
    z_f, z_o, z_q, e_f, e_o, e_q, gg, gcr, gxr, gyr, gzr, vs, vr, vz,
    og_ref, bias_ref, h, qkv, o, lse, sc, aa, mid, h2, acc, gh, eb, wb,
    io, loc, az_s, az_r, a1_s, a1_r, a2_s, a2_r, ac_s, ac_r,
    rc_s, rc_r, r1_s, r1_r, r2_s, r2_r, rz_s, rz_r, re_r,
    f1_s, f1_r, f2_s, f2_r, fc_s, fc_r, fl,
    g_s, g_r, gz_s, gz_r, ga_s, ga_r, gl, v_s, v_r, vz_s, vz_r,
):
    R, D = x_hbm.shape
    gate_ref = buf.at[2, 0, 0]
    x_ref = eb
    gz = og_ref
    CH = buf.shape[3]
    XH, YH = CH // 2, D // 2
    AR = XH // 2
    QR = sq_ref.shape[0]
    F = QR // 3
    heads = F // HEAD
    pages = R // SLOTS
    GX = gg.shape[2] // 2

    dp = lax.axis_index("dp")
    z = lax.axis_index("mp")
    c = dp % 2
    x = (dp // 2) % 2
    y = (dp // 4) % 2
    s = z // 2
    ismid = (z + s) % 2
    dev_c = (dp + 1 - 2 * c, z)
    dev_x = (dp + 2 - 4 * x, z)
    dev_y = (dp + 4 - 8 * y, z)

    def zof(slot):
        b0, b1 = slot % 2, slot // 2
        near = (1 - b0) * z + b0 * (4 * s + 1 - z)
        far = (1 - b0) * (2 - s) + b0 * (3 - 3 * s)
        return (1 - b1) * near + b1 * far

    def seen_as(slot):
        is1 = 1 - slot // 2
        return is1 + (1 - is1) * (3 - ismid)

    def remote(src, dst, ss, rs, dev):
        return pltpu.make_async_remote_copy(
            src_ref=src, dst_ref=dst, send_sem=ss, recv_sem=rs, device_id=dev, device_id_type=MESH
        )

    bar = pltpu.get_barrier_semaphore()
    partners = (dev_c, dev_x, dev_y, (dp, zof(1)), (dp, zof(2)), (dp, zof(3)))
    for dev in partners:
        pl.semaphore_signal(bar, inc=1, device_id=dev, device_id_type=MESH)

    ins = [
        pltpu.make_async_copy(src, dst, io.at[i])
        for i, (src, dst) in enumerate(((x_hbm, x_ref), (gate_hbm, gate_ref), (og_hbm, og_ref)))
    ]
    ins[0].start()
    local = []
    for i, (src, g, cc, r0) in enumerate(
        (
            (sq_ref, 0, 0, 0), (so_ref, 0, 0, QR), (cq_ref, 0, 1, 0), (co_ref, 0, 1, QR),
            (up_ref, 1, 0, 0), (dn_ref, 1, 1, 0),
        )
    ):
        cp = pltpu.make_async_copy(src, buf.at[g, cc, z, pl.ds(r0, src.shape[0]), :], loc.at[i])
        cp.start()
        local.append(cp)
    ins[1].start()
    ins[2].start()

    def wpart(g, cc, zz, r0, nr, c0, nc):
        return buf.at[g, cc, zz, blk(r0, nr, 16), blk(c0, nc, 128)]

    def wquarter(g, zz):
        return wpart(g, c, zz, XH * x, XH, YH * y, YH)

    def z_copy(g, zz, slot_to, sidx, rslot):
        ref = wquarter(g, zz)
        return remote(ref, ref, az_s.at[g, sidx], az_r.at[g, rslot], (dp, zof(slot_to)))

    def ag_zsend(g):
        z_copy(g, z, 1, 0, 1).start()

        @pl.when(ismid == 1)
        def _():
            z_copy(g, z, 2, 1, 2).start()

    def ag_zsend_wait(g):
        z_copy(g, z, 1, 0, 1).wait_send()

        @pl.when(ismid == 1)
        def _():
            for i in range(1, 5):
                z_copy(g, z, 1, i, 1).wait_send()

    def ag_p1(g, j):
        zz = zof(j)
        ra = wpart(g, c, zz, XH * x, AR, YH * y, YH)
        rb = wpart(g, c, zz, XH * x + AR, AR, YH * y, YH)
        ia = wpart(g, c, zz, XH * (1 - x), AR, YH * y, YH)
        ib = wpart(g, c, zz, XH * x + AR, AR, YH * (1 - y), YH)
        return (
            (remote(ra, ra, a1_s.at[g, j, 0], a1_r.at[g, j, 0], dev_x),
             remote(rb, rb, a1_s.at[g, j, 1], a1_r.at[g, j, 1], dev_y)),
            (remote(ia, ia, a1_s.at[g, j, 0], a1_r.at[g, j, 0], dev_x),
             remote(ib, ib, a1_s.at[g, j, 1], a1_r.at[g, j, 1], dev_y)),
        )

    def ag_p2(g, j):
        zz = zof(j)
        outs, ins = [], []
        for xx in range(2):
            ra = wpart(g, c, zz, XH * xx, AR, YH * y, YH)
            ia = wpart(g, c, zz, XH * xx, AR, YH * (1 - y), YH)
            outs.append(remote(ra, ra, a2_s.at[g, j, xx], a2_r.at[g, j, xx], dev_y))
            ins.append(remote(ia, ia, a2_s.at[g, j, xx], a2_r.at[g, j, xx], dev_y))
        rb = wpart(g, c, zz, XH * x + AR, AR, 0, D)
        ib = wpart(g, c, zz, XH * (1 - x) + AR, AR, 0, D)
        outs.append(remote(rb, rb, a2_s.at[g, j, 2], a2_r.at[g, j, 2], dev_x))
        ins.append(remote(ib, ib, a2_s.at[g, j, 2], a2_r.at[g, j, 2], dev_x))
        return outs, ins

    def ag_c(g, j):
        zz = zof(j)
        mine, theirs = buf.at[g, c, zz], buf.at[g, 1 - c, zz]
        return (
            remote(mine, mine, ac_s.at[g, j], ac_r.at[g, j], dev_c),
            remote(theirs, theirs, ac_s.at[g, j], ac_r.at[g, j], dev_c),
        )

    def ag_forward(g, j):
        @pl.when(ismid == 1)
        def _():
            z_copy(g, zof(j), 1, 0, j).wait_recv()
            if j == 1:
                z_copy(g, zof(1), 2, 2, 3).start()
            else:
                z_copy(g, zof(j), 1, j + 1, j).start()

    def ag_1(t):
        g, j = t // 3, t % 3 + 1

        @pl.when(ismid == 0)
        def _():
            z_copy(g, zof(j), 1, 0, j).wait_recv()

        for cp in ag_p1(g, j)[0]:
            cp.start()

    def ag_2(t):
        g, j = t // 3, t % 3 + 1
        outs, arrivals = ag_p1(g, j)
        for cp in arrivals:
            cp.wait_recv()
        for cp in ag_p2(g, j)[0]:
            cp.start()
        for cp in outs:
            cp.wait_send()

    def ag_3(t):
        g, j = t // 3, t % 3 + 1
        outs, arrivals = ag_p2(g, j)
        for cp in arrivals:
            cp.wait_recv()
        ag_c(g, j)[0].start()
        for cp in outs:
            cp.wait_send()

    def ag_done(g, j):
        mine, theirs = ag_c(g, j)
        theirs.wait_recv()
        mine.wait_send()

    def add_rows(dst, dst_idx, r0, nr, c0, nc, src, src_idx):
        step = next(n for n in (64, 48) if nr % n == 0)

        @pl.loop(0, nr // step)
        def _(i):
            rows = blk(r0 + i * step, step, 16)
            cols = blk(c0, nc, 128)
            d = dst[(*dst_idx, rows, cols)].astype(f32)
            t = src[(*src_idx, blk(i * step, step, 16), slice(None))].astype(f32)
            dst[(*dst_idx, rows, cols)] = (d + t).astype(bf16)

    def single(b, nr, ha, kq, slot, sem):
        def reg(cc, r0, n, c0, w):
            return buf.at[b, cc, kq, blk(r0, n, 16), blk(c0, w, 128)]

        def add(r0, n, c0, w, src, idx):
            add_rows(buf, (b, c, kq), r0, n, c0, w, src, idx)

        return dict(
            reg=reg, add=add, nr=nr, ha=ha, sem=sem,
            cr=(crecv, (slot,), pl.ds(0, nr)), a1=(p1a, (slot,), pl.ds(0, ha)),
            b1=[(p1b, (slot, xx), pl.ds(0, ha)) for xx in range(2)],
            a2=(p2a, (slot,), pl.ds(0, ha)), b2=(p2b, (slot,), pl.ds(0, ha)),
        )

    def k_ffn(k):
        return single(2, CH, AR, k, k, k)

    def k_qkv(i):
        return single(1, QR, QR // 4, 3 - i, i, 5 + i)

    def k_out():
        def reg(cc, r0, n, c0, w):
            return buf.at[1, cc, :, blk(QR + r0, n, 16), blk(c0, w, 128)]

        def add(r0, n, c0, w, src, idx):
            for q in range(4):
                add_rows(buf, (1, c, q), QR + r0, n, c0, w, src, (*idx, q))

        every = slice(None)
        return dict(
            reg=reg, add=add, nr=F, ha=F // 4, sem=4,
            cr=(cr_o, (), every), a1=(p1a_o, (), every), b1=[(p1b_o, (xx,), every) for xx in range(2)],
            a2=(p2a_o, (), every), b2=(p2b_o, (), every),
        )

    def land(part):
        ref, idx, rows = part
        return ref.at[(*idx, rows)]

    def rs_c(kd):
        n = kd["sem"]
        return remote(kd["reg"](1 - c, 0, kd["nr"], 0, D), land(kd["cr"]), rc_s.at[n], rc_r.at[n], dev_c)

    def rs_p1(kd):
        n, half, ha, reg = kd["sem"], kd["nr"] // 2, kd["ha"], kd["reg"]
        cps = [remote(reg(c, half * (1 - x), ha, 0, D), land(kd["a1"]), r1_s.at[n, 0], r1_r.at[n, 0], dev_x)]
        for xx in range(2):
            src = reg(c, half * xx + ha, ha, YH * (1 - y), YH)
            cps.append(remote(src, land(kd["b1"][xx]), r1_s.at[n, 1 + xx], r1_r.at[n, 1 + xx], dev_y))
        return cps

    def rs_p2(kd):
        n, half, ha, reg = kd["sem"], kd["nr"] // 2, kd["ha"], kd["reg"]
        return [
            remote(reg(c, half * x, ha, YH * (1 - y), YH), land(kd["a2"]), r2_s.at[n, 0], r2_r.at[n, 0], dev_y),
            remote(
                reg(c, half * (1 - x) + ha, ha, YH * y, YH), land(kd["b2"]), r2_s.at[n, 1], r2_r.at[n, 1], dev_x
            ),
        ]

    def rs_0(kd):
        rs_c(kd).start()

    def rs_1(kd, between=None):
        cp = rs_c(kd)
        cp.wait_recv()
        kd["add"](0, kd["nr"], 0, D, kd["cr"][0], kd["cr"][1])
        if between is not None:
            between()
        for q in rs_p1(kd):
            q.start()
        cp.wait_send()

    def rs_2(kd):
        half, ha = kd["nr"] // 2, kd["ha"]
        cps = rs_p1(kd)
        for q in cps:
            q.wait_recv()
        kd["add"](half * x, ha, 0, D, kd["a1"][0], kd["a1"][1])
        for xx in range(2):
            kd["add"](half * xx + ha, ha, YH * y, YH, kd["b1"][xx][0], kd["b1"][xx][1])
        for q in rs_p2(kd):
            q.start()
        for q in cps:
            q.wait_send()

    def rs_3(kd, after=None):
        half, ha = kd["nr"] // 2, kd["ha"]
        cps = rs_p2(kd)
        for q in cps:
            q.wait_recv()
        kd["add"](half * x, ha, YH * y, YH, kd["a2"][0], kd["a2"][1])
        kd["add"](half * x + ha, ha, YH * y, YH, kd["b2"][0], kd["b2"][1])
        if after is not None:
            after()
        for q in cps:
            q.wait_send()

    groups = ((2, 0, XH, z_f, e_f), (1, QR, F // 2, z_o, e_o), (1, 0, QR // 2, z_q, e_q))

    def z_part(gi, k):
        b, r0, half = groups[gi][:3]
        return buf.at[b, c, k, blk(r0 + half * x, half, 16), blk(YH * y, YH, 128)]

    def z_out(gi, k):
        return remote(z_part(gi, k), groups[gi][3].at[0 if k == 1 else 1], rz_s.at[gi, k], rz_r.at[gi, 0 if k == 1 else 1], (dp, zof(k)))

    def z_hop(gi, k):
        return remote(z_part(gi, k), groups[gi][4].at[k - 2], rz_s.at[gi, k], re_r.at[gi, k - 2], (dp, zof(1)))

    def z_start(gi, k):
        if k == 1:
            z_out(gi, 1).start()
        if k > 1:

            @pl.when(ismid == 0)
            def _():
                z_hop(gi, k).start()

    def z_join(gi, k):
        b, r0, half, _to, mid_buf = groups[gi]

        @pl.when(ismid == 1)
        def _():
            z_hop(gi, k).wait_recv()
            add_rows(buf, (b, c, k), r0 + half * x, half, YH * y, YH, mid_buf, (k - 2,))
            z_out(gi, k).start()

    def fin_part(gi, r, n, c0, w):
        r0 = groups[gi][1]
        return fin.at[0 if gi == 0 else 1, c, blk(r0 + r, n, 16), blk(c0, w, 128)]

    def own_part(gi, r, n):
        b, r0 = groups[gi][:2]
        return buf.at[b, c, 0, blk(r0 + r, n, 16), blk(YH * y, YH, 128)]

    def fin_p1(gi):
        half = groups[gi][2]
        q = half // 2
        return [
            remote(
                own_part(gi, half * x + q * i, q), fin_part(gi, half * x + q * i, q, YH * y, YH),
                f1_s.at[gi, i], f1_r.at[gi, i], dev,
            )
            for i, dev in enumerate((dev_x, dev_y))
        ]

    def fin_local(gi):
        half = groups[gi][2]
        return pltpu.make_async_copy(
            own_part(gi, half * x, half), fin_part(gi, half * x, half, YH * y, YH), fl.at[gi]
        )

    def fin_p2(gi):
        half = groups[gi][2]
        q = half // 2
        cps = []
        for xx in range(2):
            ref = fin_part(gi, half * xx, q, YH * y, YH)
            cps.append(remote(ref, ref, f2_s.at[gi, xx], f2_r.at[gi, xx], dev_y))
        ref = fin_part(gi, half * x + q, q, 0, D)
        cps.append(remote(ref, ref, f2_s.at[gi, 2], f2_r.at[gi, 2], dev_x))
        return cps

    def fin_c(gi):
        ref = fin_part(gi, 0, 2 * groups[gi][2], 0, D)
        return remote(ref, ref, fc_s.at[gi], fc_r.at[gi], dev_c)

    def fin_0(gi):
        b, r0, half, part, _mid = groups[gi]
        for k in (1, 2):
            z_out(gi, k).wait_recv()
        for slot in range(2):
            add_rows(buf, (b, c, 0), r0 + half * x, half, YH * y, YH, part, (slot,))
        for q in fin_p1(gi):
            q.start()
        fin_local(gi).start()
        for k in (1, 2, 3):
            z_out(gi, k).wait_send()

    def fin_1(gi):
        for q in fin_p1(gi):
            q.wait_recv()
        fin_local(gi).wait()
        for q in fin_p2(gi):
            q.start()
        for q in fin_p1(gi):
            q.wait_send()

    def fin_2(gi):
        for q in fin_p2(gi):
            q.wait_recv()
        fin_c(gi).start()
        for q in fin_p2(gi):
            q.wait_send()

    def fin_3(gi):
        fin_c(gi).wait_recv()
        fin_c(gi).wait_send()

    def g_copy(i):
        xs, xo = blk(GX * x, GX, 16), blk(GX * (1 - x), GX, 16)
        ys, yo = blk(YH * y, YH, 128), blk(YH * (1 - y), YH, 128)
        src, dst, dev = {
            0: lambda: (gg.at[:, 1 - c], gcr, dev_c),
            1: lambda: (gg.at[:, c, xo, :], gxr, dev_x),
            2: lambda: (gg.at[:, c, xs, yo], gyr, dev_y),
            3: lambda: (gout.at[:, c, xs, ys], gout.at[:, c, xs, ys], dev_y),
            4: lambda: (gout.at[:, c, xs, :], gout.at[:, c, xs, :], dev_x),
            5: lambda: (gout.at[:, c], gout.at[:, c], dev_c),
        }[i]()
        return remote(src, dst, g_s.at[i], g_r.at[i], dev)

    def g_z(slot, rslot):
        src = gg.at[zof(slot), c, blk(GX * x, GX, 16), blk(YH * y, YH, 128)]
        return remote(src, gzr.at[rslot - 1], gz_s.at[slot], gz_r.at[rslot], (dp, zof(slot)))

    def g_za(slot, rslot):
        src = gg.at[z, c, blk(GX * x, GX, 16), blk(YH * y, YH, 128)]
        dst = gout.at[z, c, blk(GX * x, GX, 16), blk(YH * y, YH, 128)]
        return remote(src, dst, ga_s.at[slot], ga_r.at[rslot], (dp, zof(slot)))

    def g_local():
        src = gg.at[z, c, blk(GX * x, GX, 16), blk(YH * y, YH, 128)]
        dst = gout.at[z, c, blk(GX * x, GX, 16), blk(YH * y, YH, 128)]
        return pltpu.make_async_copy(src, dst, gl.at[0])

    def g_step(i):
        xs, ys = blk(GX * x, GX, 16), blk(YH * y, YH, 128)
        if i == 0:
            g_copy(0).start()
        if i == 1:
            g_copy(0).wait_recv()
            for q in range(4):
                add_rows(gg, (q, c), 0, 2 * GX, 0, D, gcr, (q,))
            g_copy(1).start()
            g_copy(0).wait_send()
        if i == 2:
            g_copy(1).wait_recv()
            for q in range(4):
                add_rows(gg, (q, c), GX * x, GX, 0, D, gxr, (q,))
            g_copy(2).start()
            g_copy(1).wait_send()
        if i == 3:
            g_copy(2).wait_recv()
            for q in range(4):
                add_rows(gg, (q, c), GX * x, GX, YH * y, YH, gyr, (q,))
            for slot in range(1, 4):
                g_z(slot, seen_as(slot)).start()
            g_copy(2).wait_send()
        if i == 4:
            for slot in range(1, 4):
                g_z(slot, slot).wait_recv()
            t = gg[z, c, xs, ys].astype(f32)
            for slot in range(3):
                t = t + gzr[slot].astype(f32)
            gg[z, c, xs, ys] = t.astype(bf16)
            g_local().start()
            for slot in range(1, 4):
                g_za(slot, seen_as(slot)).start()
            for slot in range(1, 4):
                g_z(slot, slot).wait_send()
        if i == 5:
            for slot in range(1, 4):
                g_za(slot, slot).wait_recv()
            g_local().wait()
            g_copy(3).start()
            for slot in range(1, 4):
                g_za(slot, slot).wait_send()
        if i == 6:
            g_copy(3).wait_recv()
            g_copy(4).start()
            g_copy(3).wait_send()
        if i == 7:
            g_copy(4).wait_recv()
            g_copy(5).start()
            g_copy(4).wait_send()
        if i == 8:
            g_copy(5).wait_recv()
            g_copy(5).wait_send()

    def v_copy(i):
        return remote(vs.at[i], vr.at[i], v_s.at[i], v_r.at[i], (dev_c, dev_x, dev_y)[i])

    def v_z(slot, zz_dst, rslot):
        return remote(vz.at[z], vz.at[zz_dst], vz_s.at[slot], vz_r.at[rslot], (dp, zof(slot)))

    def v_step(i):
        if i == 0:
            v_copy(0).start()
        if i in (1, 2):
            v_copy(i - 1).wait_recv()
            vs[i] = vs[i - 1] + vr[i - 1]
            v_copy(i).start()
            v_copy(i - 1).wait_send()
        if i == 3:
            v_copy(2).wait_recv()
            vz[z] = vs[2] + vr[2]
            for slot in range(1, 4):
                v_z(slot, z, seen_as(slot)).start()
            v_copy(2).wait_send()
        if i == 4:
            for slot in range(1, 4):
                v_z(slot, z, slot).wait_recv()
            vec_ref[...] = (vz[0] + vz[1]) + (vz[2] + vz[3])
            for slot in range(1, 4):
                v_z(slot, z, slot).wait_send()

    def kind(n):
        return k_ffn(n) if n < 4 else k_out() if n == 4 else k_qkv(n - 5)

    def third(n):
        if n < 4:
            rs_3(kind(n), lambda: z_start(0, n))
        elif n == 4:
            rs_3(kind(n), lambda: [z_start(1, q) for q in range(1, 4)])
        else:
            rs_3(kind(n), lambda: z_start(2, 8 - n))

    events = {
        "zs": ag_zsend, "zw": ag_forward, "ag1": ag_1, "ag2": ag_2, "ag3": ag_3,
        "rs0": lambda n: rs_0(kind(n)), "rs1": lambda n: rs_1(kind(n)), "rs2": lambda n: rs_2(kind(n)), "rs3": third,
        "zza": z_join, "g": g_step, "v": v_step, "fin0": fin_0, "fin1": fin_1, "fin2": fin_2, "fin3": fin_3,
    }

    def after(name, k=None, p=None):
        if k is None:
            for ev in AFTER.get(name, ()):
                events[ev[0]](*ev[1:])
            return
        for kk in range(4):
            for pp in range(1 if p is None else 4):
                found = AFTER.get(name[0] + str(kk) + name[1:] + ("" if p is None else str(pp)), ())
                if found:

                    @pl.when((k == kk) if p is None else (k == kk) & (p == pp))
                    def _():
                        for ev in found:
                            events[ev[0]](*ev[1:])

    TR = 64
    again = again_ref[...].astype(f32).reshape(1, D)
    fgain = fgain_ref[...].astype(f32).reshape(1, D)
    gbias = gbias_ref[...].astype(f32).reshape(1, D)

    pl.semaphore_wait(bar, 6)
    for cp in local[:4]:
        cp.wait()
    ag_zsend(0)

    key_id = lax.broadcasted_iota(jnp.int32, (SLOTS, SLOTS), 0)
    query_id = lax.broadcasted_iota(jnp.int32, (SLOTS, SLOTS), 1)
    key_kind = jnp.where(key_id < LANG, 1, 0)
    query_kind = jnp.where(query_id < LANG, 1, 0)
    for p in range(pages):
        row = marks_ref[pl.ds(pages * z + p, 1), :]
        real = jnp.broadcast_to(jnp.where(row > 0, 0.0, NEG), (SLOTS, SLOTS)).T
        bias_ref[0, p] = jnp.where(key_kind == query_kind, real, NEG).astype(bf16)
        bias_ref[1, p] = jnp.where(key_kind == query_kind, NEG, real).astype(bf16)

    ins[0].wait()

    @pl.loop(0, R // TR)
    def _(i):
        rows = blk(i * TR, TR, 16)
        u, _inv = standardize(x_ref[rows, :].astype(f32))
        h[rows, :] = (u * again).astype(bf16)
        sc[rows, :] = jnp.zeros((TR, D), f32)
        mid[rows, :] = jnp.zeros((TR, D), f32)
        gh[rows, :] = jnp.zeros((TR, D), f32)

    vs[...] = jnp.zeros_like(vs)
    for cp in local[4:] + ins[1:]:
        cp.wait()
    after("norm")

    @pl.loop(0, 4)
    def _(k):
        zz = zof(k)

        @pl.when(k > 0)
        def _():
            ag_done(0, k)

        for at in range(2):
            qkv[at, k] = mm(buf[0, at, zz, 0:QR, :], h[...], "nt").astype(bf16)
        after("Aq", k)

        @pl.loop(0, pages)
        def _(p):
            cols = blk(p * SLOTS, SLOTS, 128)
            for at in range(2):
                for hh in range(heads):
                    qt = qkv[at, k, HEAD * hh : HEAD * (hh + 1), cols]
                    kt = qkv[at, k, F + HEAD * hh : F + HEAD * (hh + 1), cols]
                    vt = qkv[at, k, 2 * F + HEAD * hh : 2 * F + HEAD * (hh + 1), cols]
                    st = mm(kt, qt, "tn") * HEAD ** (-0.5) + bias_ref[at, p].astype(f32)
                    top = jnp.max(st, axis=0, keepdims=True)
                    ex = jnp.exp(st - top)
                    tot = jnp.sum(ex, axis=0, keepdims=True)
                    pt = (ex * (1.0 / tot)).astype(bf16)
                    lse[at, k, hh : hh + 1, cols] = top + jnp.log(tot)
                    o[at, k, HEAD * hh : HEAD * (hh + 1), cols] = mm(vt, pt, "nn").astype(bf16)
            after("Ap", k, p)

        @pl.loop(0, pages)
        def _(p):
            cols = blk(p * SLOTS, SLOTS, 128)
            for at, dst in ((0, sc), (1, mid)):
                dst[cols, :] += mm(o[at, k, :, cols], buf[0, at, zz, QR:CH, :], "tn")

        after("As", k)

        @pl.when(k == 0)
        def _():
            @pl.loop(0, R // 128)
            def _(i):
                rows = blk(i * 128, 128, 16)
                aa[rows, :] = jax.nn.sigmoid(mm(h[rows, :], gate_ref[...], "nn") + gbias)

            after("gate")

    ag_zsend_wait(0)

    @pl.loop(0, R // TR)
    def _(i):
        rows = blk(i * TR, TR, 16)
        a = aa[rows, :]
        sv, cv = sc[rows, :], mid[rows, :]
        mv = x_ref[rows, :].astype(f32) + a * sv + (1.0 - a) * cv
        sc[rows, :] = sv - cv
        mid[rows, :] = mv
        acc[rows, :] = mv
        u, _inv = standardize(mv)
        h2[rows, :] = (u * fgain).astype(bf16)

    after("join")

    @pl.loop(0, 4)
    def _(k):
        zz = zof(k)

        @pl.when(k > 0)
        def _():
            ag_done(1, k)

        MT = 256

        @pl.loop(0, R // MT)
        def _(i):
            rows = blk(i * MT, MT, 16)
            w = mm(h2[rows, :], buf[1, 0, zz], "nn")
            ge = mm(og_ref[rows, :], buf[1, 1, zz], "nt")
            w2 = w * w
            th = jnp.tanh(GC * w * (1.0 + GK * w2))
            half = 0.5 * (1.0 + th)
            eb[rows, :] = (w * half).astype(bf16)
            dg = half + 0.5 * w * (1.0 - th * th) * (GC * (1.0 + 3.0 * GK * w2))
            wb[rows, :] = (dg * ge).astype(bf16)

        after("Fa", k)

        @pl.loop(0, R // MT)
        def _(i):
            rows = blk(i * MT, MT, 16)
            acc[rows, :] += mm(eb[rows, :], buf[1, 1, zz], "nn")
            gh[rows, :] += mm(wb[rows, :], buf[1, 0, zz], "nt")

        after("Fb", k)

        @pl.loop(0, CH // 256)
        def _(i):
            cols = blk(i * 256, 256, 128)
            buf[2, 1, k, blk(i * 256, 256, 16), :] = mm(eb[:, cols], og_ref[...], "tn").astype(bf16)
            buf[2, 0, k, blk(i * 256, 256, 16), :] = mm(h2[:, cols], wb[...], "tn").astype(bf16)

        after("Fc", k)

    ag_zsend_wait(1)

    TS = 32
    zero_row = jnp.zeros((1, D), f32)

    def mid_back(i, sums):
        gain_sum, bias_sum = sums
        rows = blk(i * TS, TS, 16)
        h2[rows, :] = acc[rows, :].astype(bf16)
        u, inv = standardize(mid[rows, :])
        gy = gh[rows, :]
        gain_sum = gain_sum + jnp.sum(gy * u, axis=0, keepdims=True)
        sy = gy * fgain
        m1 = jnp.mean(sy, axis=1, keepdims=True)
        m2 = jnp.mean(sy * u, axis=1, keepdims=True)
        gm = og_ref[rows, :].astype(f32) + inv * (sy - m1 - u * m2)
        acc[rows, :] = gm
        a = aa[rows, :]
        eb[rows, :] = (a * gm).astype(bf16)
        wb[rows, :] = ((1.0 - a) * gm).astype(bf16)
        gzv = (gm * sc[rows, :] * a * (1.0 - a)).astype(bf16)
        gz[rows, :] = gzv
        bias_sum = bias_sum + jnp.sum(gzv.astype(f32), axis=0, keepdims=True)
        return gain_sum, bias_sum

    gain_sum, bias_sum = lax.fori_loop(0, R // TS, mid_back, (zero_row, zero_row))
    vs[0, 1:2, :] = bias_sum
    vs[0, 2:3, :] = gain_sum
    out_copy = pltpu.make_async_copy(h2, out_hbm, io.at[3])
    out_copy.start()
    after("mid2")
    gate_again = buf.at[2, 1 - c, 1]
    gate_load = pltpu.make_async_copy(gate_hbm, gate_again, io.at[5])
    gate_load.start()

    for k in range(4):
        for at, gref in ((0, eb), (1, wb)):
            buf[1, at, k, QR:CH, :] = mm(o[at, k], gref[...], "nn").astype(bf16)
    after("outmm")
    for i in range(4):
        t = mm(h[:, F * i : F * (i + 1)], gz[...], "tn").astype(bf16)
        gg[i, 0] = t[: F // 2]
        gg[i, 1] = t[F // 2 :]
    after("ggrad")

    x_again = wb
    x_load = pltpu.make_async_copy(x_hbm, x_again, io.at[6])

    @pl.loop(0, 4)
    def _(i):
        k = 3 - i
        zz = zof(k)
        for at, gref in ((0, eb), (1, wb)):
            o[at, k] = mm(buf[0, at, zz, QR:CH, :], gref[...], "nt").astype(bf16)

        @pl.when(i == 3)
        def _():
            x_load.start()

        after("Bo", i)

        @pl.loop(0, pages)
        def _(p):
            cols = blk(p * SLOTS, SLOTS, 128)
            for at in range(2):
                for hh in range(heads):
                    qs = slice(HEAD * hh, HEAD * (hh + 1))
                    ks = slice(F + HEAD * hh, F + HEAD * (hh + 1))
                    vsl = slice(2 * F + HEAD * hh, 2 * F + HEAD * (hh + 1))
                    qt = qkv[at, k, qs, cols]
                    kt = qkv[at, k, ks, cols]
                    vt = qkv[at, k, vsl, cols]
                    go = o[at, k, qs, cols]
                    st = mm(kt, qt, "tn") * HEAD ** (-0.5) + bias_ref[at, p].astype(f32)
                    pt = jnp.exp(st - lse[at, k, hh : hh + 1, cols])
                    gvt = mm(go, pt.astype(bf16), "nt")
                    gpt = mm(vt, go, "tn")
                    pg = pt * gpt
                    gst = (pg - pt * jnp.sum(pg, axis=0, keepdims=True)).astype(bf16)
                    gqt = mm(kt, gst, "nn") * HEAD ** (-0.5)
                    gkt = mm(qt, gst, "nt") * HEAD ** (-0.5)
                    qkv[at, k, qs, cols] = gqt.astype(bf16)
                    qkv[at, k, ks, cols] = gkt.astype(bf16)
                    qkv[at, k, vsl, cols] = gvt.astype(bf16)
            after("Bp", i, p)

        for at in range(2):
            for q in range(3):
                part = slice(F * q, F * (q + 1))
                buf[1, at, k, part, :] = mm(qkv[at, k, part, :], h[...], "nn").astype(bf16)
        after("Bg", i)

        @pl.loop(0, pages)
        def _(p):
            cols = blk(p * SLOTS, SLOTS, 128)
            t = mm(qkv[0, k, :, cols], buf[0, 0, zz, 0:QR, :], "tn") + mm(qkv[1, k, :, cols], buf[0, 1, zz, 0:QR, :], "tn")

            @pl.when(i == 0)
            def _():
                gh[cols, :] = t

            @pl.when(i > 0)
            def _():
                gh[cols, :] += t

        after("Bh", i)

    gate_load.wait()

    @pl.loop(0, R // 128)
    def _(i):
        rows = blk(i * 128, 128, 16)
        gh[rows, :] += mm(gz[rows, :], gate_again[...], "nt")

    def first_back(i, gain_sum):
        rows = blk(i * TS, TS, 16)
        u, inv = standardize(x_again[rows, :].astype(f32))
        gy = gh[rows, :]
        gain_sum = gain_sum + jnp.sum(gy * u, axis=0, keepdims=True)
        sy = gy * again
        m1 = jnp.mean(sy, axis=1, keepdims=True)
        m2 = jnp.mean(sy * u, axis=1, keepdims=True)
        eb[rows, :] = (acc[rows, :] + inv * (sy - m1 - u * m2)).astype(bf16)
        return gain_sum

    x_load.wait()
    vs[0, 0:1, :] = lax.fori_loop(0, R // TS, first_back, zero_row)
    tg_copy = pltpu.make_async_copy(eb, tg_hbm, io.at[4])
    tg_copy.start()
    after("tail")
    out_copy.wait()
    tg_copy.wait()


def widen_kernel(
    out_in, tg_in, fin, gout, vec_in,
    out_o, tg_o, ag_o, sq_o, cq_o, so_o, co_o, gw_o, gb_o, fg_o, up_o, dn_o,
    narrow, wide, whole, sem_in, sem_out, sem_pass,
):
    F = so_o.shape[0]
    QR = 3 * F
    passes = []
    for i, (src, dst) in enumerate(((out_in, out_o), (tg_in, tg_o))):
        load = pltpu.make_async_copy(src, whole.at[i], sem_pass.at[i])
        passes.append((load, pltpu.make_async_copy(whole.at[i], dst, sem_pass.at[2 + i])))
    parts = [(fin.at[0, 0], up_o), (fin.at[0, 1], dn_o), (gout, gw_o)]
    for cc, (a, b) in enumerate(((sq_o, so_o), (cq_o, co_o))):
        parts += [(fin.at[1, cc, pl.ds(0, QR)], a), (fin.at[1, cc, pl.ds(QR, F)], b)]
    r0 = 0
    jobs = []
    for i, (src, dst) in enumerate(parts):
        n = src.shape[0]
        load = pltpu.make_async_copy(src, narrow.at[pl.ds(r0, n)], sem_in.at[i])
        save = pltpu.make_async_copy(wide.at[pl.ds(r0, n)], dst, sem_out.at[i])
        load.start()
        jobs.append((r0, n, load, save))
        r0 += n
    for load, _ in passes:
        load.start()
    ag_o[...] = vec_in[0, :]
    gb_o[...] = vec_in[1, :]
    fg_o[...] = vec_in[2, :]
    for load, save in passes:
        load.wait()
        save.start()
    for r0, n, load, save in jobs:
        load.wait()

        @pl.loop(0, n // 64)
        def _(i):
            rows = blk(r0 + 64 * i, 64, 16)
            wide[rows, :] = narrow[rows, :].astype(f32)

        save.start()
    for _, _, _, save in jobs:
        save.wait()
    for _, save in passes:
        save.wait()


def body(
    tokens, region_mask, attn_gain, self_qkv, cross_qkv, self_out, cross_out, gate_weight, gate_bias,
    ffn_gain, up_weight, down_weight, out_grad, *, outer,
):
    R, D = tokens.shape
    F = self_out.shape[0]
    QR = 3 * F
    CH = QR + F
    pages = R // SLOTS

    vm = pl.BlockSpec(memory_space=pltpu.VMEM)
    hb = pl.BlockSpec(memory_space=pl.ANY)
    dma = pltpu.SemaphoreType.DMA
    XH, YH, AR, GX, OR = CH // 2, D // 2, CH // 4, D // 16, F // 4
    scratch = [
        pltpu.VMEM((3, 2, 4, CH, D), bf16),
        pltpu.VMEM((4, CH, D), bf16),
        pltpu.VMEM((4, AR, D), bf16),
        pltpu.VMEM((4, 2, AR, YH), bf16),
        pltpu.VMEM((4, AR, YH), bf16),
        pltpu.VMEM((4, AR, YH), bf16),
        pltpu.VMEM((4, F, D), bf16),
        pltpu.VMEM((4, OR, D), bf16),
        pltpu.VMEM((2, 4, OR, YH), bf16),
        pltpu.VMEM((4, OR, YH), bf16),
        pltpu.VMEM((4, OR, YH), bf16),
        pltpu.VMEM((2, XH, YH), bf16),
        pltpu.VMEM((2, F // 2, YH), bf16),
        pltpu.VMEM((2, QR // 2, YH), bf16),
        pltpu.VMEM((2, XH, YH), bf16),
        pltpu.VMEM((2, F // 2, YH), bf16),
        pltpu.VMEM((2, QR // 2, YH), bf16),
        pltpu.VMEM((4, 2, 2 * GX, D), bf16),
        pltpu.VMEM((4, 2 * GX, D), bf16),
        pltpu.VMEM((4, GX, D), bf16),
        pltpu.VMEM((4, GX, YH), bf16),
        pltpu.VMEM((3, GX, YH), bf16),
        pltpu.VMEM((3, 8, D), f32),
        pltpu.VMEM((3, 8, D), f32),
        pltpu.VMEM((4, 8, D), f32),
        pltpu.VMEM((R, D), bf16),
        pltpu.VMEM((2, pages, SLOTS, SLOTS), bf16),
        pltpu.VMEM((R, D), bf16),
        pltpu.VMEM((2, 4, QR, R), bf16),
        pltpu.VMEM((2, 4, F, R), bf16),
        pltpu.VMEM((2, 4, 8, R), f32),
        pltpu.VMEM((R, D), f32),
        pltpu.VMEM((R, D), f32),
        pltpu.VMEM((R, D), f32),
        pltpu.VMEM((R, D), bf16),
        pltpu.VMEM((R, D), f32),
        pltpu.VMEM((R, D), f32),
        pltpu.VMEM((R, D), bf16),
        pltpu.VMEM((R, D), bf16),
        dma((7,)),
        dma((6,)), dma((2, 5)), dma((2, 4)), dma((2, 4, 2)), dma((2, 4, 2)), dma((2, 4, 3)), dma((2, 4, 3)),
        dma((2, 4)), dma((2, 4)),
        dma((9,)), dma((9,)), dma((9, 3)), dma((9, 3)), dma((9, 2)), dma((9, 2)), dma((3, 4)), dma((3, 2)),
        dma((3, 2)),
        dma((3, 2)), dma((3, 2)), dma((3, 3)), dma((3, 3)), dma((3,)), dma((3,)), dma((3,)),
        dma((6,)), dma((6,)), dma((4,)), dma((4,)), dma((4,)), dma((4,)), dma((1,)),
        dma((3,)), dma((3,)), dma((4,)), dma((4,)),
    ]
    mid_out = pl.pallas_call(
        layer_kernel,
        out_shape=(
            jax.ShapeDtypeStruct((R, D), bf16),
            jax.ShapeDtypeStruct((R, D), bf16),
            jax.ShapeDtypeStruct((2, 2, CH, D), bf16),
            jax.ShapeDtypeStruct((4, 2, 2 * GX, D), bf16),
            jax.ShapeDtypeStruct((8, D), f32),
        ),
        in_specs=[hb] * 3 + [vm] * 4 + [hb] * 6,
        out_specs=(hb, hb, hb, hb, vm),
        scratch_shapes=scratch,
        compiler_params=pltpu.CompilerParams(
            collective_id=1, has_side_effects=True, vmem_limit_bytes=64 * 2**20 - 2**17
        ),
    )(
        tokens, out_grad, gate_weight, region_mask, attn_gain, ffn_gain, gate_bias,
        self_qkv.reshape(QR, D), cross_qkv.reshape(QR, D), self_out, cross_out, up_weight, down_weight,
    )
    out, tg, fin, gout, vec = mid_out
    total = 4 * CH + D
    wide = lambda *shape: jax.ShapeDtypeStruct(shape, f32)
    res = pl.pallas_call(
        widen_kernel,
        out_shape=(
            jax.ShapeDtypeStruct((R, D), bf16), jax.ShapeDtypeStruct((R, D), bf16),
            wide(D), wide(QR, D), wide(QR, D), wide(F, D), wide(F, D), wide(D, D), wide(D), wide(D),
            wide(CH, D), wide(CH, D),
        ),
        in_specs=[hb] * 4 + [vm],
        out_specs=(hb, hb, vm, hb, hb, hb, hb, hb, vm, vm, hb, hb),
        scratch_shapes=[
            pltpu.VMEM((total, D), bf16), pltpu.VMEM((total, D), f32), pltpu.VMEM((2, R, D), bf16),
            dma((7,)), dma((7,)), dma((4,)),
        ],
        compiler_params=pltpu.CompilerParams(vmem_limit_bytes=60 * 2**20),
    )(out, tg, fin, gout.reshape(D, D), vec)
    out, tg, again, sq, cq, so, co, gw, gb, fg, up, dn = res
    grads = (again, sq.reshape(3, F, D), cq.reshape(3, F, D), so, co, gw, gb, fg, up, dn)
    if outer > 1:
        first = (lax.axis_index("dp") % 8 == 0).astype(f32)
        grads = lax.psum(tuple(g * first for g in grads), "dp")
    return (out, tg) + tuple(grads)


def solution(mesh):
    rows = P(("dp", "mp"), None)
    weights = (P(), P(None, "mp", None), P(None, "mp", None), P("mp", None), P("mp", None), P(), P(), P(), P(None, "mp"), P("mp", None))
    return jax.shard_map(
        functools.partial(body, outer=mesh.shape["dp"] // 8),
        mesh=mesh,
        in_specs=(rows, P("dp", None)) + weights + (rows,),
        out_specs=(rows, rows) + weights,
        check_vma=False,
    )
```

```python
import functools

import jax
import jax.numpy as jnp
from jax import lax
from jax.experimental import pallas as pl
from jax.experimental.pallas import tpu as pltpu
from jax.sharding import PartitionSpec as P

HEAD = 64
LANG = 96
SLOTS = 128
EPS = 1e-5
NEG = -1e30
GC = 0.7978845608028654
GK = 0.044715
f32 = jnp.float32
bf16 = jnp.bfloat16
MESH = pl.DeviceIdType.MESH

AFTER = {
    "A0p1": (("zw", 0, 1), ("ag1", 0), ("zw", 0, 2), ("zs", 1), ("ag2", 0), ("ag1", 1), ("zw", 1, 1), ("zw", 0, 3),),
    "A0p2": (("zw", 1, 2), ("ag1", 3),),
    "A0p3": (("ag3", 0), ("ag2", 1),),
    "A1q": (("ag1", 2), ("ag3", 1), ("zw", 1, 3), ("ag1", 4),),
    "A1p1": (("ag2", 2),),
    "A2p1": (("ag1", 5),),
    "A2s": (("ag2", 3), ("ag2", 4), ("ag3", 2), ("ag2", 5),),
    "F0a": (("ag3", 3),),
    "F0c": (("rs0", 0),),
    "F1a": (("ag3", 4),),
    "F1c": (("rs1", 0), ("rs0", 1),),
    "F2a": (("ag3", 5),),
    "F2b": (("rs1", 1),),
    "F2c": (("rs0", 2),),
    "F3a": (("rs2", 0),),
    "F3b": (("rs1", 2),),
    "F3c": (("rs0", 3), ("rs2", 1),),
    "mid2": (("rs1", 3),),
    "outmm": (("rs0", 4), ("rs2", 2),),
    "B0o": (("g", 0),),
    "B0p1": (("rs1", 4),),
    "B0p2": (("rs3", 0), ("zfa", 0, 2), ("g", 1),),
    "B0h": (("rs0", 5), ("rs2", 3),),
    "B1p1": (("rs1", 5),),
    "B1p3": (("zfa", 0, 3), ("rs3", 1),),
    "B1g": (("rs0", 6), ("rs2", 4),),
    "B1h": (("g", 2),),
    "B2o": (("rs3", 3), ("rs2", 5), ("rs1", 6), ("rs3", 2),),
    "B2g": (("rs0", 7), ("zza", 0, 3), ("g", 3), ("rs1", "z0"),),
    "B2h": (("rs1", 7), ("rs3", 5), ("rs2", 6),),
    "B3p0": (("rs2", "z0"), ("zza", 0, 2), ("rs3", 4),),
    "B3g": (("rs0", 8), ("rs2", 7), ("rs1", 8), ("zza", 1, 2), ("rs3", 6),),
    "B3h": (("rs3", "z0"), ("zza", 1, 3), ("zza", 2, 3), ("fin0", 0),),
    "tail": (("g", 4), ("rs2", 8), ("zza", 2, 2), ("v", 0), ("rs3", 7), ("fin0", 1), ("fin1", 0), ("rs3", 8), ("g", 5), ("v", 1), ("fin0", 2), ("fin2", 0), ("fin1", 1), ("g", 6), ("v", 2), ("fin1", 2), ("v", 3), ("fin2", 1), ("fin3", 1), ("g", 7), ("v", 4), ("fin2", 2), ("g", 8), ("fin3", 0), ("fin3", 2),),
}


def mm(lhs, rhs, form):
    dims = {"nn": ((1,), (0,)), "nt": ((1,), (1,)), "tn": ((0,), (0,))}[form]
    return lax.dot_general(lhs, rhs, (dims, ((), ())), preferred_element_type=f32)


def blk(start, size, align):
    return pl.ds(pl.multiple_of(start, align), size)


def standardize(rows):
    centre = jnp.mean(rows, axis=1, keepdims=True)
    offset = rows - centre
    spread = jnp.mean(offset * offset, axis=1, keepdims=True)
    inv = lax.rsqrt(spread + EPS)
    return offset * inv, inv


def layer_kernel(
    x_hbm, og_hbm, gate_hbm, marks_ref, again_ref, fgain_ref, gbias_ref,
    sq_ref, cq_ref, so_ref, co_ref, up_ref, dn_ref,
    out_hbm, tg_hbm, fin, gout, vec_ref,
    buf, crecv, p1a, p1b, p2a, p2b, cr_o, p1a_o, p1b_o, p2a_o, p2b_o,
    z_f, z_o, z_q, e_f, e_o, e_q, zr, ze, p1a_z, p1b_z, p2a_z, p2b_z, gg, gcr, gxr, gyr, gzr, vs, vr, vz,
    og_ref, bias_ref, h, qkv, o, lse, sc, aa, mid, h2, acc, gh, eb, wb,
    io, loc, az_s, az_r, a1_s, a1_r, a2_s, a2_r, ac_s, ac_r,
    rc_s, rc_r, r1_s, r1_r, r2_s, r2_r, rz_s, rz_r, re_r, zf_s, zf_r, zfe_r,
    f1_s, f1_r, f2_s, f2_r, fc_s, fc_r, fl,
    g_s, g_r, gz_s, gz_r, ga_s, ga_r, gl, v_s, v_r, vz_s, vz_r,
):
    R, D = x_hbm.shape
    gate_ref = buf.at[2, 0, 0]
    x_ref = eb
    gz = og_ref
    CH = buf.shape[3]
    XH, YH = CH // 2, D // 2
    ZF = zr.shape[2]
    AR = XH // 2
    QR = sq_ref.shape[0]
    F = QR // 3
    heads = F // HEAD
    pages = R // SLOTS
    GX = gg.shape[2] // 2

    dp = lax.axis_index("dp")
    z = lax.axis_index("mp")
    c = dp % 2
    x = (dp // 2) % 2
    y = (dp // 4) % 2
    s = z // 2
    ismid = (z + s) % 2
    dev_c = (dp + 1 - 2 * c, z)
    dev_x = (dp + 2 - 4 * x, z)
    dev_y = (dp + 4 - 8 * y, z)

    def zof(slot):
        b0, b1 = slot % 2, slot // 2
        near = (1 - b0) * z + b0 * (4 * s + 1 - z)
        far = (1 - b0) * (2 - s) + b0 * (3 - 3 * s)
        return (1 - b1) * near + b1 * far

    def seen_as(slot):
        is1 = 1 - slot // 2
        return is1 + (1 - is1) * (3 - ismid)

    def remote(src, dst, ss, rs, dev):
        return pltpu.make_async_remote_copy(
            src_ref=src, dst_ref=dst, send_sem=ss, recv_sem=rs, device_id=dev, device_id_type=MESH
        )

    bar = pltpu.get_barrier_semaphore()
    partners = (dev_c, dev_x, dev_y, (dp, zof(1)), (dp, zof(2)), (dp, zof(3)))
    for dev in partners:
        pl.semaphore_signal(bar, inc=1, device_id=dev, device_id_type=MESH)

    ins = [
        pltpu.make_async_copy(src, dst, io.at[i])
        for i, (src, dst) in enumerate(((x_hbm, x_ref), (gate_hbm, gate_ref), (og_hbm, og_ref)))
    ]
    ins[0].start()
    local = []
    for i, (src, g, cc, r0) in enumerate(
        (
            (sq_ref, 0, 0, 0), (so_ref, 0, 0, QR), (cq_ref, 0, 1, 0), (co_ref, 0, 1, QR),
            (up_ref, 1, 0, 0), (dn_ref, 1, 1, 0),
        )
    ):
        cp = pltpu.make_async_copy(src, buf.at[g, cc, z, pl.ds(r0, src.shape[0]), :], loc.at[i])
        cp.start()
        local.append(cp)
    ins[1].start()
    ins[2].start()

    def wpart(g, cc, zz, r0, nr, c0, nc):
        return buf.at[g, cc, zz, blk(r0, nr, 16), blk(c0, nc, 128)]

    def wquarter(g, zz):
        return wpart(g, c, zz, XH * x, XH, YH * y, YH)

    def z_copy(g, zz, slot_to, sidx, rslot):
        ref = wquarter(g, zz)
        return remote(ref, ref, az_s.at[g, sidx], az_r.at[g, rslot], (dp, zof(slot_to)))

    def ag_zsend(g):
        z_copy(g, z, 1, 0, 1).start()

        @pl.when(ismid == 1)
        def _():
            z_copy(g, z, 2, 1, 2).start()

    def ag_zsend_wait(g):
        z_copy(g, z, 1, 0, 1).wait_send()

        @pl.when(ismid == 1)
        def _():
            for i in range(1, 5):
                z_copy(g, z, 1, i, 1).wait_send()

    def ag_p1(g, j):
        zz = zof(j)
        ra = wpart(g, c, zz, XH * x, AR, YH * y, YH)
        rb = wpart(g, c, zz, XH * x + AR, AR, YH * y, YH)
        ia = wpart(g, c, zz, XH * (1 - x), AR, YH * y, YH)
        ib = wpart(g, c, zz, XH * x + AR, AR, YH * (1 - y), YH)
        return (
            (remote(ra, ra, a1_s.at[g, j, 0], a1_r.at[g, j, 0], dev_x),
             remote(rb, rb, a1_s.at[g, j, 1], a1_r.at[g, j, 1], dev_y)),
            (remote(ia, ia, a1_s.at[g, j, 0], a1_r.at[g, j, 0], dev_x),
             remote(ib, ib, a1_s.at[g, j, 1], a1_r.at[g, j, 1], dev_y)),
        )

    def ag_p2(g, j):
        zz = zof(j)
        outs, ins = [], []
        for xx in range(2):
            ra = wpart(g, c, zz, XH * xx, AR, YH * y, YH)
            ia = wpart(g, c, zz, XH * xx, AR, YH * (1 - y), YH)
            outs.append(remote(ra, ra, a2_s.at[g, j, xx], a2_r.at[g, j, xx], dev_y))
            ins.append(remote(ia, ia, a2_s.at[g, j, xx], a2_r.at[g, j, xx], dev_y))
        rb = wpart(g, c, zz, XH * x + AR, AR, 0, D)
        ib = wpart(g, c, zz, XH * (1 - x) + AR, AR, 0, D)
        outs.append(remote(rb, rb, a2_s.at[g, j, 2], a2_r.at[g, j, 2], dev_x))
        ins.append(remote(ib, ib, a2_s.at[g, j, 2], a2_r.at[g, j, 2], dev_x))
        return outs, ins

    def ag_c(g, j):
        zz = zof(j)
        mine, theirs = buf.at[g, c, zz], buf.at[g, 1 - c, zz]
        return (
            remote(mine, mine, ac_s.at[g, j], ac_r.at[g, j], dev_c),
            remote(theirs, theirs, ac_s.at[g, j], ac_r.at[g, j], dev_c),
        )

    def ag_forward(g, j):
        @pl.when(ismid == 1)
        def _():
            z_copy(g, zof(j), 1, 0, j).wait_recv()
            if j == 1:
                z_copy(g, zof(1), 2, 2, 3).start()
            else:
                z_copy(g, zof(j), 1, j + 1, j).start()

    def ag_1(t):
        g, j = t // 3, t % 3 + 1

        @pl.when(ismid == 0)
        def _():
            z_copy(g, zof(j), 1, 0, j).wait_recv()

        for cp in ag_p1(g, j)[0]:
            cp.start()

    def ag_2(t):
        g, j = t // 3, t % 3 + 1
        outs, arrivals = ag_p1(g, j)
        for cp in arrivals:
            cp.wait_recv()
        for cp in ag_p2(g, j)[0]:
            cp.start()
        for cp in outs:
            cp.wait_send()

    def ag_3(t):
        g, j = t // 3, t % 3 + 1
        outs, arrivals = ag_p2(g, j)
        for cp in arrivals:
            cp.wait_recv()
        ag_c(g, j)[0].start()
        for cp in outs:
            cp.wait_send()

    def ag_done(g, j):
        mine, theirs = ag_c(g, j)
        theirs.wait_recv()
        mine.wait_send()

    def add_rows(dst, dst_idx, r0, nr, c0, nc, src, src_idx):
        step = next(n for n in (64, 48) if nr % n == 0)

        @pl.loop(0, nr // step)
        def _(i):
            rows = blk(r0 + i * step, step, 16)
            cols = blk(c0, nc, 128)
            d = dst[(*dst_idx, rows, cols)].astype(f32)
            t = src[(*src_idx, blk(i * step, step, 16), slice(None))].astype(f32)
            dst[(*dst_idx, rows, cols)] = (d + t).astype(bf16)

    def single(b, nr, ha, kq, slot, sem):
        def reg(cc, r0, n, c0, w):
            return buf.at[b, cc, kq, blk(r0, n, 16), blk(c0, w, 128)]

        def add(r0, n, c0, w, src, idx):
            add_rows(buf, (b, c, kq), r0, n, c0, w, src, idx)

        return dict(
            reg=reg, add=add, nr=nr, ha=ha, off=0, sem=sem,
            cr=(crecv, (slot,), pl.ds(0, nr)), a1=(p1a, (slot,), pl.ds(0, ha)),
            b1=[(p1b, (slot, xx), pl.ds(0, ha)) for xx in range(2)],
            a2=(p2a, (slot,), pl.ds(0, ha)), b2=(p2b, (slot,), pl.ds(0, ha)),
        )

    def k_ffn(k):
        return single(2, CH, (XH - ZF) // 2, k, k, k)

    def k_first():
        kd = k_ffn(0)
        every = slice(None)
        kd.update(
            off=XH - ZF, ha=ZF // 2, sem=9, a1=(p1a_z, (), every), b1=[(p1b_z, (xx,), every) for xx in range(2)],
            a2=(p2a_z, (), every), b2=(p2b_z, (), every),
        )
        return kd

    def k_qkv(i):
        return single(1, QR, QR // 4, 3 - i, i, 5 + i)

    def k_out():
        def reg(cc, r0, n, c0, w):
            return buf.at[1, cc, :, blk(QR + r0, n, 16), blk(c0, w, 128)]

        def add(r0, n, c0, w, src, idx):
            for q in range(4):
                add_rows(buf, (1, c, q), QR + r0, n, c0, w, src, (*idx, q))

        every = slice(None)
        return dict(
            reg=reg, add=add, nr=F, ha=F // 4, off=0, sem=4,
            cr=(cr_o, (), every), a1=(p1a_o, (), every), b1=[(p1b_o, (xx,), every) for xx in range(2)],
            a2=(p2a_o, (), every), b2=(p2b_o, (), every),
        )

    def land(part):
        ref, idx, rows = part
        return ref.at[(*idx, rows)]

    def rs_c(kd):
        n = kd["sem"]
        return remote(kd["reg"](1 - c, 0, kd["nr"], 0, D), land(kd["cr"]), rc_s.at[n], rc_r.at[n], dev_c)

    def rs_p1(kd):
        n, half, ha, reg, off = kd["sem"], kd["nr"] // 2, kd["ha"], kd["reg"], kd["off"]
        cps = [remote(reg(c, half * (1 - x) + off, ha, 0, D), land(kd["a1"]), r1_s.at[n, 0], r1_r.at[n, 0], dev_x)]
        for xx in range(2):
            src = reg(c, half * xx + off + ha, ha, YH * (1 - y), YH)
            cps.append(remote(src, land(kd["b1"][xx]), r1_s.at[n, 1 + xx], r1_r.at[n, 1 + xx], dev_y))
        return cps

    def rs_p2(kd):
        n, half, ha, reg, off = kd["sem"], kd["nr"] // 2, kd["ha"], kd["reg"], kd["off"]
        return [
            remote(reg(c, half * x + off, ha, YH * (1 - y), YH), land(kd["a2"]), r2_s.at[n, 0], r2_r.at[n, 0], dev_y),
            remote(
                reg(c, half * (1 - x) + off + ha, ha, YH * y, YH), land(kd["b2"]), r2_s.at[n, 1], r2_r.at[n, 1], dev_x
            ),
        ]

    def rs_0(kd):
        rs_c(kd).start()

    def rs_1(kd, between=None):
        cp = rs_c(kd)
        cp.wait_recv()
        kd["add"](0, kd["nr"], 0, D, kd["cr"][0], kd["cr"][1])
        if between is not None:
            between()
        for q in rs_p1(kd):
            q.start()
        cp.wait_send()

    def rs_2(kd):
        half, ha, off = kd["nr"] // 2, kd["ha"], kd["off"]
        cps = rs_p1(kd)
        for q in cps:
            q.wait_recv()
        kd["add"](half * x + off, ha, 0, D, kd["a1"][0], kd["a1"][1])
        for xx in range(2):
            kd["add"](half * xx + off + ha, ha, YH * y, YH, kd["b1"][xx][0], kd["b1"][xx][1])
        for q in rs_p2(kd):
            q.start()
        for q in cps:
            q.wait_send()

    def rs_3(kd, after=None):
        half, ha, off = kd["nr"] // 2, kd["ha"], kd["off"]
        cps = rs_p2(kd)
        for q in cps:
            q.wait_recv()
        kd["add"](half * x + off, ha, YH * y, YH, kd["a2"][0], kd["a2"][1])
        kd["add"](half * x + off + ha, ha, YH * y, YH, kd["b2"][0], kd["b2"][1])
        if after is not None:
            after()
        for q in cps:
            q.wait_send()

    groups = (
        (2, 0, XH, XH - ZF, z_f, e_f),
        (1, QR, F // 2, F // 2, z_o, e_o),
        (1, 0, QR // 2, QR // 2, z_q, e_q),
    )

    def z_part(gi, k):
        b, r0, half, n = groups[gi][:4]
        return buf.at[b, c, k, blk(r0 + half * x, n, 16), blk(YH * y, YH, 128)]

    def z_out(gi, k):
        return remote(z_part(gi, k), groups[gi][4].at[0 if k == 1 else 1], rz_s.at[gi, k], rz_r.at[gi, 0 if k == 1 else 1], (dp, zof(k)))

    def z_hop(gi, k):
        return remote(z_part(gi, k), groups[gi][5].at[k - 2], rz_s.at[gi, k], re_r.at[gi, k - 2], (dp, zof(1)))

    def z_start(gi, k):
        if k == 1:
            z_out(gi, 1).start()
        if k > 1:

            @pl.when(ismid == 0)
            def _():
                z_hop(gi, k).start()

    def z_join(gi, k):
        b, r0, half, n, _to, mid_buf = groups[gi]

        @pl.when(ismid == 1)
        def _():
            z_hop(gi, k).wait_recv()
            add_rows(buf, (b, c, k), r0 + half * x, n, YH * y, YH, mid_buf, (k - 2,))
            z_out(gi, k).start()

    def zf_rows(k, xx):
        return buf.at[2, c, k, pl.ds(XH * (xx + 1) - ZF, ZF), :]

    def zf_out(k, xx):
        to = 0 if k == 1 else 1
        return remote(zf_rows(k, xx), zr.at[to, xx], zf_s.at[k, xx], zf_r.at[to, xx], (dp, zof(k)))

    def zf_hop(k, xx):
        return remote(zf_rows(k, xx), ze.at[k - 2, xx], zf_s.at[k, xx], zfe_r.at[k - 2, xx], (dp, zof(1)))

    def zf_start(k):
        if k == 1:
            for xx in range(2):
                zf_out(1, xx).start()
        if k > 1:

            @pl.when(ismid == 0)
            def _():
                for xx in range(2):
                    zf_hop(k, xx).start()

    def zf_join(_gi, k):
        @pl.when(ismid == 1)
        def _():
            for xx in range(2):
                zf_hop(k, xx).wait_recv()
                add_rows(buf, (2, c, k), XH * (xx + 1) - ZF, ZF, 0, D, ze, (k - 2, xx))
                zf_out(k, xx).start()

    def zf_sum():
        for xx in range(2):
            for slot in range(2):
                zf_out(1 + slot, xx).wait_recv()
                add_rows(buf, (2, c, 0), XH * (xx + 1) - ZF, ZF, 0, D, zr, (slot, xx))
        for q in rs_p1(k_first()):
            q.start()

    def fin_part(gi, r, n, c0, w):
        r0 = groups[gi][1]
        return fin.at[0 if gi == 0 else 1, c, blk(r0 + r, n, 16), blk(c0, w, 128)]

    def own_part(gi, r, n):
        b, r0 = groups[gi][:2]
        return buf.at[b, c, 0, blk(r0 + r, n, 16), blk(YH * y, YH, 128)]

    def fin_p1(gi):
        half = groups[gi][2]
        q = half // 2
        return [
            remote(
                own_part(gi, half * x + q * i, q), fin_part(gi, half * x + q * i, q, YH * y, YH),
                f1_s.at[gi, i], f1_r.at[gi, i], dev,
            )
            for i, dev in enumerate((dev_x, dev_y))
        ]

    def fin_local(gi):
        half = groups[gi][2]
        return pltpu.make_async_copy(
            own_part(gi, half * x, half), fin_part(gi, half * x, half, YH * y, YH), fl.at[gi]
        )

    def fin_p2(gi):
        half = groups[gi][2]
        q = half // 2
        cps = []
        for xx in range(2):
            ref = fin_part(gi, half * xx, q, YH * y, YH)
            cps.append(remote(ref, ref, f2_s.at[gi, xx], f2_r.at[gi, xx], dev_y))
        ref = fin_part(gi, half * x + q, q, 0, D)
        cps.append(remote(ref, ref, f2_s.at[gi, 2], f2_r.at[gi, 2], dev_x))
        return cps

    def fin_c(gi):
        ref = fin_part(gi, 0, 2 * groups[gi][2], 0, D)
        return remote(ref, ref, fc_s.at[gi], fc_r.at[gi], dev_c)

    def fin_0(gi):
        b, r0, half, n, part, _mid = groups[gi]
        for k in (1, 2):
            z_out(gi, k).wait_recv()
        for slot in range(2):
            add_rows(buf, (b, c, 0), r0 + half * x, n, YH * y, YH, part, (slot,))
        for q in fin_p1(gi):
            q.start()
        fin_local(gi).start()
        for k in (1, 2, 3):
            z_out(gi, k).wait_send()
            if gi == 0:
                for xx in range(2):
                    zf_out(k, xx).wait_send()

    def fin_1(gi):
        for q in fin_p1(gi):
            q.wait_recv()
        fin_local(gi).wait()
        for q in fin_p2(gi):
            q.start()
        for q in fin_p1(gi):
            q.wait_send()

    def fin_2(gi):
        for q in fin_p2(gi):
            q.wait_recv()
        fin_c(gi).start()
        for q in fin_p2(gi):
            q.wait_send()

    def fin_3(gi):
        fin_c(gi).wait_recv()
        fin_c(gi).wait_send()

    def g_copy(i):
        xs, xo = blk(GX * x, GX, 16), blk(GX * (1 - x), GX, 16)
        ys, yo = blk(YH * y, YH, 128), blk(YH * (1 - y), YH, 128)
        src, dst, dev = {
            0: lambda: (gg.at[:, 1 - c], gcr, dev_c),
            1: lambda: (gg.at[:, c, xo, :], gxr, dev_x),
            2: lambda: (gg.at[:, c, xs, yo], gyr, dev_y),
            3: lambda: (gout.at[:, c, xs, ys], gout.at[:, c, xs, ys], dev_y),
            4: lambda: (gout.at[:, c, xs, :], gout.at[:, c, xs, :], dev_x),
            5: lambda: (gout.at[:, c], gout.at[:, c], dev_c),
        }[i]()
        return remote(src, dst, g_s.at[i], g_r.at[i], dev)

    def g_z(slot, rslot):
        src = gg.at[zof(slot), c, blk(GX * x, GX, 16), blk(YH * y, YH, 128)]
        return remote(src, gzr.at[rslot - 1], gz_s.at[slot], gz_r.at[rslot], (dp, zof(slot)))

    def g_za(slot, rslot):
        src = gg.at[z, c, blk(GX * x, GX, 16), blk(YH * y, YH, 128)]
        dst = gout.at[z, c, blk(GX * x, GX, 16), blk(YH * y, YH, 128)]
        return remote(src, dst, ga_s.at[slot], ga_r.at[rslot], (dp, zof(slot)))

    def g_local():
        src = gg.at[z, c, blk(GX * x, GX, 16), blk(YH * y, YH, 128)]
        dst = gout.at[z, c, blk(GX * x, GX, 16), blk(YH * y, YH, 128)]
        return pltpu.make_async_copy(src, dst, gl.at[0])

    def g_step(i):
        xs, ys = blk(GX * x, GX, 16), blk(YH * y, YH, 128)
        if i == 0:
            g_copy(0).start()
        if i == 1:
            g_copy(0).wait_recv()
            for q in range(4):
                add_rows(gg, (q, c), 0, 2 * GX, 0, D, gcr, (q,))
            g_copy(1).start()
            g_copy(0).wait_send()
        if i == 2:
            g_copy(1).wait_recv()
            for q in range(4):
                add_rows(gg, (q, c), GX * x, GX, 0, D, gxr, (q,))
            g_copy(2).start()
            g_copy(1).wait_send()
        if i == 3:
            g_copy(2).wait_recv()
            for q in range(4):
                add_rows(gg, (q, c), GX * x, GX, YH * y, YH, gyr, (q,))
            for slot in range(1, 4):
                g_z(slot, seen_as(slot)).start()
            g_copy(2).wait_send()
        if i == 4:
            for slot in range(1, 4):
                g_z(slot, slot).wait_recv()
            t = gg[z, c, xs, ys].astype(f32)
            for slot in range(3):
                t = t + gzr[slot].astype(f32)
            gg[z, c, xs, ys] = t.astype(bf16)
            g_local().start()
            for slot in range(1, 4):
                g_za(slot, seen_as(slot)).start()
            for slot in range(1, 4):
                g_z(slot, slot).wait_send()
        if i == 5:
            for slot in range(1, 4):
                g_za(slot, slot).wait_recv()
            g_local().wait()
            g_copy(3).start()
            for slot in range(1, 4):
                g_za(slot, slot).wait_send()
        if i == 6:
            g_copy(3).wait_recv()
            g_copy(4).start()
            g_copy(3).wait_send()
        if i == 7:
            g_copy(4).wait_recv()
            g_copy(5).start()
            g_copy(4).wait_send()
        if i == 8:
            g_copy(5).wait_recv()
            g_copy(5).wait_send()

    def v_copy(i):
        return remote(vs.at[i], vr.at[i], v_s.at[i], v_r.at[i], (dev_c, dev_x, dev_y)[i])

    def v_z(slot, zz_dst, rslot):
        return remote(vz.at[z], vz.at[zz_dst], vz_s.at[slot], vz_r.at[rslot], (dp, zof(slot)))

    def v_step(i):
        if i == 0:
            v_copy(0).start()
        if i in (1, 2):
            v_copy(i - 1).wait_recv()
            vs[i] = vs[i - 1] + vr[i - 1]
            v_copy(i).start()
            v_copy(i - 1).wait_send()
        if i == 3:
            v_copy(2).wait_recv()
            vz[z] = vs[2] + vr[2]
            for slot in range(1, 4):
                v_z(slot, z, seen_as(slot)).start()
            v_copy(2).wait_send()
        if i == 4:
            for slot in range(1, 4):
                v_z(slot, z, slot).wait_recv()
            vec_ref[...] = (vz[0] + vz[1]) + (vz[2] + vz[3])
            for slot in range(1, 4):
                v_z(slot, z, slot).wait_send()

    def kind(n):
        if n == "z0":
            return k_first()
        return k_ffn(n) if n < 4 else k_out() if n == 4 else k_qkv(n - 5)

    def first(n):
        if n == "z0":
            zf_sum()
        else:
            rs_1(kind(n), lambda: zf_start(n) if n < 4 else None)

    def third(n):
        if n == "z0":
            rs_3(kind(n))
        elif n < 4:
            rs_3(kind(n), lambda: z_start(0, n))
        elif n == 4:
            rs_3(kind(n), lambda: [z_start(1, q) for q in range(1, 4)])
        else:
            rs_3(kind(n), lambda: z_start(2, 8 - n))

    events = {
        "zs": ag_zsend, "zw": ag_forward, "ag1": ag_1, "ag2": ag_2, "ag3": ag_3,
        "rs0": lambda n: rs_0(kind(n)), "rs1": first, "rs2": lambda n: rs_2(kind(n)), "rs3": third,
        "zza": z_join, "zfa": zf_join, "g": g_step, "v": v_step, "fin0": fin_0, "fin1": fin_1, "fin2": fin_2, "fin3": fin_3,
    }

    def after(name, k=None, p=None):
        if k is None:
            for ev in AFTER.get(name, ()):
                events[ev[0]](*ev[1:])
            return
        for kk in range(4):
            for pp in range(1 if p is None else 4):
                found = AFTER.get(name[0] + str(kk) + name[1:] + ("" if p is None else str(pp)), ())
                if found:

                    @pl.when((k == kk) if p is None else (k == kk) & (p == pp))
                    def _():
                        for ev in found:
                            events[ev[0]](*ev[1:])

    TR = 128
    again = again_ref[...].astype(f32).reshape(1, D)
    fgain = fgain_ref[...].astype(f32).reshape(1, D)
    gbias = gbias_ref[...].astype(f32).reshape(1, D)

    pl.semaphore_wait(bar, 6)
    for cp in local[:4]:
        cp.wait()
    ag_zsend(0)

    after("start")

    key_id = lax.broadcasted_iota(jnp.int32, (SLOTS, SLOTS), 0)
    query_id = lax.broadcasted_iota(jnp.int32, (SLOTS, SLOTS), 1)
    key_kind = jnp.where(key_id < LANG, 1, 0)
    query_kind = jnp.where(query_id < LANG, 1, 0)
    for p in range(pages):
        row = marks_ref[pl.ds(pages * z + p, 1), :]
        real = jnp.broadcast_to(jnp.where(row > 0, 0.0, NEG), (SLOTS, SLOTS)).T
        bias_ref[0, p] = jnp.where(key_kind == query_kind, real, NEG).astype(bf16)
        bias_ref[1, p] = jnp.where(key_kind == query_kind, NEG, real).astype(bf16)

    ins[0].wait()

    @pl.loop(0, R // TR)
    def _(i):
        rows = blk(i * TR, TR, 16)
        u, _inv = standardize(x_ref[rows, :].astype(f32))
        h[rows, :] = (u * again).astype(bf16)
        sc[rows, :] = jnp.zeros((TR, D), f32)
        mid[rows, :] = jnp.zeros((TR, D), f32)
        gh[rows, :] = jnp.zeros((TR, D), f32)

    vs[...] = jnp.zeros_like(vs)
    for cp in local[4:] + ins[1:]:
        cp.wait()
    after("norm")

    @pl.loop(0, 4)
    def _(k):
        zz = zof(k)

        @pl.when(k > 0)
        def _():
            ag_done(0, k)

        for at in range(2):
            qkv[at, k] = mm(buf[0, at, zz, 0:QR, :], h[...], "nt").astype(bf16)
        after("Aq", k)

        @pl.loop(0, pages)
        def _(p):
            cols = blk(p * SLOTS, SLOTS, 128)
            units = [(at, hh) for at in range(2) for hh in range(heads)]
            scores = []
            for at, hh in units:
                qt = qkv[at, k, HEAD * hh : HEAD * (hh + 1), cols]
                kt = qkv[at, k, F + HEAD * hh : F + HEAD * (hh + 1), cols]
                scores.append(mm(kt, qt, "tn"))
            probs = []
            for (at, hh), st in zip(units, scores):
                st = st * HEAD ** (-0.5) + bias_ref[at, p].astype(f32)
                top = jnp.max(st, axis=0, keepdims=True)
                ex = jnp.exp(st - top)
                tot = jnp.sum(ex, axis=0, keepdims=True)
                probs.append((ex * (1.0 / tot)).astype(bf16))
                lse[at, k, hh : hh + 1, cols] = top + jnp.log(tot)
            for (at, hh), pt in zip(units, probs):
                vt = qkv[at, k, 2 * F + HEAD * hh : 2 * F + HEAD * (hh + 1), cols]
                o[at, k, HEAD * hh : HEAD * (hh + 1), cols] = mm(vt, pt, "nn").astype(bf16)
            after("Ap", k, p)

        @pl.loop(0, 2)
        def _(p):
            cols = blk(p * 256, 256, 128)
            for at, dst in ((0, sc), (1, mid)):
                dst[cols, :] += mm(o[at, k, :, cols], buf[0, at, zz, QR:CH, :], "tn")

        after("As", k)

        @pl.when(k == 0)
        def _():
            @pl.loop(0, R // 256)
            def _(i):
                rows = blk(i * 256, 256, 16)
                aa[rows, :] = jax.nn.sigmoid(mm(h[rows, :], gate_ref[...], "nn") + gbias)

            after("gate")

    ag_zsend_wait(0)

    @pl.loop(0, R // TR)
    def _(i):
        rows = blk(i * TR, TR, 16)
        a = aa[rows, :]
        sv, cv = sc[rows, :], mid[rows, :]
        mv = x_ref[rows, :].astype(f32) + a * sv + (1.0 - a) * cv
        sc[rows, :] = sv - cv
        mid[rows, :] = mv
        acc[rows, :] = mv
        u, _inv = standardize(mv)
        h2[rows, :] = (u * fgain).astype(bf16)

    after("join")

    @pl.loop(0, 4)
    def _(k):
        zz = zof(k)

        @pl.when(k > 0)
        def _():
            ag_done(1, k)

        MT = 256

        @pl.loop(0, 2 * (R // MT))
        def _(i):
            rows = blk((i // 2) * MT, MT, 16)
            cols = blk((i % 2) * XH, XH, 128)
            w = mm(h2[rows, :], buf[1, 0, zz, :, cols], "nn")
            ge = mm(og_ref[rows, :], buf[1, 1, zz, blk((i % 2) * XH, XH, 16), :], "nt")
            w2 = w * w
            th = jnp.tanh(GC * w * (1.0 + GK * w2))
            half = 0.5 * (1.0 + th)
            eb[rows, cols] = (w * half).astype(bf16)
            dg = half + 0.5 * w * (1.0 - th * th) * (GC * (1.0 + 3.0 * GK * w2))
            wb[rows, cols] = (dg * ge).astype(bf16)

        after("Fa", k)

        @pl.loop(0, R // MT)
        def _(i):
            rows = blk(i * MT, MT, 16)
            acc[rows, :] += mm(eb[rows, :], buf[1, 1, zz], "nn")
            gh[rows, :] += mm(wb[rows, :], buf[1, 0, zz], "nt")

        after("Fb", k)

        @pl.loop(0, CH // 384)
        def _(i):
            cols = blk(i * 384, 384, 128)
            buf[2, 1, k, blk(i * 384, 384, 16), :] = mm(eb[:, cols], og_ref[...], "tn").astype(bf16)
            buf[2, 0, k, blk(i * 384, 384, 16), :] = mm(h2[:, cols], wb[...], "tn").astype(bf16)

        after("Fc", k)

    ag_zsend_wait(1)

    TS = 128
    zero_row = jnp.zeros((1, D), f32)

    def mid_back(i, sums):
        gain_sum, bias_sum = sums
        rows = blk(i * TS, TS, 16)
        h2[rows, :] = acc[rows, :].astype(bf16)
        u, inv = standardize(mid[rows, :])
        gy = gh[rows, :]
        gain_sum = gain_sum + jnp.sum(gy * u, axis=0, keepdims=True)
        sy = gy * fgain
        m1 = jnp.mean(sy, axis=1, keepdims=True)
        m2 = jnp.mean(sy * u, axis=1, keepdims=True)
        gm = og_ref[rows, :].astype(f32) + inv * (sy - m1 - u * m2)
        acc[rows, :] = gm
        a = aa[rows, :]
        eb[rows, :] = (a * gm).astype(bf16)
        wb[rows, :] = ((1.0 - a) * gm).astype(bf16)
        gzv = (gm * sc[rows, :] * a * (1.0 - a)).astype(bf16)
        gz[rows, :] = gzv
        bias_sum = bias_sum + jnp.sum(gzv.astype(f32), axis=0, keepdims=True)
        return gain_sum, bias_sum

    gain_sum, bias_sum = lax.fori_loop(0, R // TS, mid_back, (zero_row, zero_row))
    vs[0, 1:2, :] = bias_sum
    vs[0, 2:3, :] = gain_sum
    out_copy = pltpu.make_async_copy(h2, out_hbm, io.at[3])
    out_copy.start()
    after("mid2")
    gate_again = buf.at[2, 1 - c, 1]
    gate_load = pltpu.make_async_copy(gate_hbm, gate_again, io.at[5])
    gate_load.start()

    for k in range(4):
        for at, gref in ((0, eb), (1, wb)):
            buf[1, at, k, QR:CH, :] = mm(o[at, k], gref[...], "nn").astype(bf16)
    after("outmm")
    for i in range(4):
        t = mm(h[:, F * i : F * (i + 1)], gz[...], "tn").astype(bf16)
        gg[i, 0] = t[: F // 2]
        gg[i, 1] = t[F // 2 :]
    after("ggrad")

    x_again = wb
    x_load = pltpu.make_async_copy(x_hbm, x_again, io.at[6])

    @pl.loop(0, 4)
    def _(i):
        k = 3 - i
        zz = zof(k)
        for at, gref in ((0, eb), (1, wb)):
            o[at, k] = mm(buf[0, at, zz, QR:CH, :], gref[...], "nt").astype(bf16)

        @pl.when(i == 3)
        def _():
            x_load.start()

        after("Bo", i)

        @pl.loop(0, pages)
        def _(p):
            cols = blk(p * SLOTS, SLOTS, 128)
            units = [(at, hh) for at in range(2) for hh in range(heads)]
            for grp in (units,):
                rd = []
                for at, hh in grp:
                    qs = slice(HEAD * hh, HEAD * (hh + 1))
                    ks = slice(F + HEAD * hh, F + HEAD * (hh + 1))
                    vsl = slice(2 * F + HEAD * hh, 2 * F + HEAD * (hh + 1))
                    qt, kt, vt, go = qkv[at, k, qs, cols], qkv[at, k, ks, cols], qkv[at, k, vsl, cols], o[at, k, qs, cols]
                    rd.append((at, hh, qs, ks, vsl, qt, kt, vt, go, mm(kt, qt, "tn"), mm(vt, go, "tn")))
                ps = []
                for at, hh, qs, ks, vsl, qt, kt, vt, go, st, gpt in rd:
                    pt = jnp.exp(st * HEAD ** (-0.5) + bias_ref[at, p].astype(f32) - lse[at, k, hh : hh + 1, cols])
                    pg = pt * gpt
                    gst = (pg - pt * jnp.sum(pg, axis=0, keepdims=True)).astype(bf16)
                    ps.append((pt.astype(bf16), gst))
                for (at, hh, qs, ks, vsl, qt, kt, vt, go, st, gpt), (pb, gst) in zip(rd, ps):
                    qkv[at, k, vsl, cols] = mm(go, pb, "nt").astype(bf16)
                    qkv[at, k, qs, cols] = (mm(kt, gst, "nn") * HEAD ** (-0.5)).astype(bf16)
                    qkv[at, k, ks, cols] = (mm(qt, gst, "nt") * HEAD ** (-0.5)).astype(bf16)
            after("Bp", i, p)

        for at in range(2):
            for q in range(3):
                part = slice(F * q, F * (q + 1))
                buf[1, at, k, part, :] = mm(qkv[at, k, part, :], h[...], "nn").astype(bf16)
        after("Bg", i)

        @pl.loop(0, 2)
        def _(p):
            cols = blk(p * 256, 256, 128)
            t = mm(qkv[0, k, :, cols], buf[0, 0, zz, 0:QR, :], "tn") + mm(qkv[1, k, :, cols], buf[0, 1, zz, 0:QR, :], "tn")

            @pl.when(i == 0)
            def _():
                gh[cols, :] = t

            @pl.when(i > 0)
            def _():
                gh[cols, :] += t

        after("Bh", i)

    gate_load.wait()

    @pl.loop(0, R // 256)
    def _(i):
        rows = blk(i * 256, 256, 16)
        gh[rows, :] += mm(gz[rows, :], gate_again[...], "nt")

    def first_back(i, gain_sum):
        rows = blk(i * TS, TS, 16)
        u, inv = standardize(x_again[rows, :].astype(f32))
        gy = gh[rows, :]
        gain_sum = gain_sum + jnp.sum(gy * u, axis=0, keepdims=True)
        sy = gy * again
        m1 = jnp.mean(sy, axis=1, keepdims=True)
        m2 = jnp.mean(sy * u, axis=1, keepdims=True)
        eb[rows, :] = (acc[rows, :] + inv * (sy - m1 - u * m2)).astype(bf16)
        return gain_sum

    x_load.wait()
    vs[0, 0:1, :] = lax.fori_loop(0, R // TS, first_back, zero_row)
    tg_copy = pltpu.make_async_copy(eb, tg_hbm, io.at[4])
    tg_copy.start()
    after("tail")
    out_copy.wait()
    tg_copy.wait()


def widen_kernel(
    out_in, tg_in, fin, gout, vec_in,
    out_o, tg_o, ag_o, sq_o, cq_o, so_o, co_o, gw_o, gb_o, fg_o, up_o, dn_o,
    narrow, wide, whole, sem_in, sem_out, sem_pass,
):
    F = so_o.shape[0]
    QR = 3 * F
    passes = []
    for i, (src, dst) in enumerate(((out_in, out_o), (tg_in, tg_o))):
        load = pltpu.make_async_copy(src, whole.at[i], sem_pass.at[i])
        passes.append((load, pltpu.make_async_copy(whole.at[i], dst, sem_pass.at[2 + i])))
    parts = []
    for src, dst in ((fin.at[0, 0], up_o), (fin.at[0, 1], dn_o), (gout, gw_o)):
        n = src.shape[0] // 3
        parts += [(src.at[pl.ds(n * q, n)], dst.at[pl.ds(n * q, n)]) for q in range(3)]
    for cc, (a, b) in enumerate(((sq_o, so_o), (cq_o, co_o))):
        parts += [(fin.at[1, cc, pl.ds(QR, F)], b)]
        parts += [(fin.at[1, cc, pl.ds(F * q, F)], a.at[pl.ds(F * q, F)]) for q in range(3)]
    r0 = 0
    jobs = []
    for i, (src, dst) in enumerate(parts):
        n = src.shape[0]
        load = pltpu.make_async_copy(src, narrow.at[pl.ds(r0, n)], sem_in.at[i])
        save = pltpu.make_async_copy(wide.at[pl.ds(r0, n)], dst, sem_out.at[i])
        load.start()
        jobs.append((r0, n, load, save))
        r0 += n
    for load, _ in passes:
        load.start()
    ag_o[...] = vec_in[0, :]
    gb_o[...] = vec_in[1, :]
    fg_o[...] = vec_in[2, :]
    for load, save in passes:
        load.wait()
        save.start()
    for r0, n, load, save in jobs:
        load.wait()

        @pl.loop(0, n // 64)
        def _(i):
            rows = blk(r0 + 64 * i, 64, 16)
            wide[rows, :] = narrow[rows, :].astype(f32)

        save.start()
    for _, _, _, save in jobs:
        save.wait()
    for _, save in passes:
        save.wait()


def body(
    tokens, region_mask, attn_gain, self_qkv, cross_qkv, self_out, cross_out, gate_weight, gate_bias,
    ffn_gain, up_weight, down_weight, out_grad, *, outer,
):
    R, D = tokens.shape
    F = self_out.shape[0]
    QR = 3 * F
    CH = QR + F
    pages = R // SLOTS

    vm = pl.BlockSpec(memory_space=pltpu.VMEM)
    hb = pl.BlockSpec(memory_space=pl.ANY)
    dma = pltpu.SemaphoreType.DMA
    XH, YH, GX, OR, ZF = CH // 2, D // 2, D // 16, F // 4, CH // 6
    scratch = [
        pltpu.VMEM((3, 2, 4, CH, D), bf16),
        pltpu.VMEM((4, CH, D), bf16),
        pltpu.VMEM((4, QR // 4, D), bf16),
        pltpu.VMEM((4, 2, QR // 4, YH), bf16),
        pltpu.VMEM((4, QR // 4, YH), bf16),
        pltpu.VMEM((4, QR // 4, YH), bf16),
        pltpu.VMEM((4, F, D), bf16),
        pltpu.VMEM((4, OR, D), bf16),
        pltpu.VMEM((2, 4, OR, YH), bf16),
        pltpu.VMEM((4, OR, YH), bf16),
        pltpu.VMEM((4, OR, YH), bf16),
        pltpu.VMEM((2, XH - ZF, YH), bf16),
        pltpu.VMEM((2, F // 2, YH), bf16),
        pltpu.VMEM((2, QR // 2, YH), bf16),
        pltpu.VMEM((2, XH - ZF, YH), bf16),
        pltpu.VMEM((2, F // 2, YH), bf16),
        pltpu.VMEM((2, QR // 2, YH), bf16),
        pltpu.VMEM((2, 2, ZF, D), bf16),
        pltpu.VMEM((2, 2, ZF, D), bf16),
        pltpu.VMEM((ZF // 2, D), bf16),
        pltpu.VMEM((2, ZF // 2, YH), bf16),
        pltpu.VMEM((ZF // 2, YH), bf16),
        pltpu.VMEM((ZF // 2, YH), bf16),
        pltpu.VMEM((4, 2, 2 * GX, D), bf16),
        pltpu.VMEM((4, 2 * GX, D), bf16),
        pltpu.VMEM((4, GX, D), bf16),
        pltpu.VMEM((4, GX, YH), bf16),
        pltpu.VMEM((3, GX, YH), bf16),
        pltpu.VMEM((3, 8, D), f32),
        pltpu.VMEM((3, 8, D), f32),
        pltpu.VMEM((4, 8, D), f32),
        pltpu.VMEM((R, D), bf16),
        pltpu.VMEM((2, pages, SLOTS, SLOTS), bf16),
        pltpu.VMEM((R, D), bf16),
        pltpu.VMEM((2, 4, QR, R), bf16),
        pltpu.VMEM((2, 4, F, R), bf16),
        pltpu.VMEM((2, 4, 8, R), f32),
        pltpu.VMEM((R, D), f32),
        pltpu.VMEM((R, D), f32),
        pltpu.VMEM((R, D), f32),
        pltpu.VMEM((R, D), bf16),
        pltpu.VMEM((R, D), f32),
        pltpu.VMEM((R, D), f32),
        pltpu.VMEM((R, D), bf16),
        pltpu.VMEM((R, D), bf16),
        dma((7,)),
        dma((6,)), dma((2, 5)), dma((2, 4)), dma((2, 4, 2)), dma((2, 4, 2)), dma((2, 4, 3)), dma((2, 4, 3)),
        dma((2, 4)), dma((2, 4)),
        dma((9,)), dma((9,)), dma((10, 3)), dma((10, 3)), dma((10, 2)), dma((10, 2)), dma((3, 4)), dma((3, 2)),
        dma((3, 2)), dma((4, 2)), dma((2, 2)), dma((2, 2)),
        dma((3, 2)), dma((3, 2)), dma((3, 3)), dma((3, 3)), dma((3,)), dma((3,)), dma((3,)),
        dma((6,)), dma((6,)), dma((4,)), dma((4,)), dma((4,)), dma((4,)), dma((1,)),
        dma((3,)), dma((3,)), dma((4,)), dma((4,)),
    ]
    mid_out = pl.pallas_call(
        layer_kernel,
        out_shape=(
            jax.ShapeDtypeStruct((R, D), bf16),
            jax.ShapeDtypeStruct((R, D), bf16),
            jax.ShapeDtypeStruct((2, 2, CH, D), bf16),
            jax.ShapeDtypeStruct((4, 2, 2 * GX, D), bf16),
            jax.ShapeDtypeStruct((8, D), f32),
        ),
        in_specs=[hb] * 3 + [vm] * 4 + [hb] * 6,
        out_specs=(hb, hb, hb, hb, vm),
        scratch_shapes=scratch,
        compiler_params=pltpu.CompilerParams(
            collective_id=1, has_side_effects=True, vmem_limit_bytes=64 * 2**20 - 2**17
        ),
    )(
        tokens, out_grad, gate_weight, region_mask, attn_gain, ffn_gain, gate_bias,
        self_qkv.reshape(QR, D), cross_qkv.reshape(QR, D), self_out, cross_out, up_weight, down_weight,
    )
    out, tg, fin, gout, vec = mid_out
    total = 4 * CH + D
    wide = lambda *shape: jax.ShapeDtypeStruct(shape, f32)
    res = pl.pallas_call(
        widen_kernel,
        out_shape=(
            jax.ShapeDtypeStruct((R, D), bf16), jax.ShapeDtypeStruct((R, D), bf16),
            wide(D), wide(QR, D), wide(QR, D), wide(F, D), wide(F, D), wide(D, D), wide(D), wide(D),
            wide(CH, D), wide(CH, D),
        ),
        in_specs=[hb] * 4 + [vm],
        out_specs=(hb, hb, vm, hb, hb, hb, hb, hb, vm, vm, hb, hb),
        scratch_shapes=[
            pltpu.VMEM((total, D), bf16), pltpu.VMEM((total, D), f32), pltpu.VMEM((2, R, D), bf16),
            dma((17,)), dma((17,)), dma((4,)),
        ],
        compiler_params=pltpu.CompilerParams(vmem_limit_bytes=60 * 2**20),
    )(out, tg, fin, gout.reshape(D, D), vec)
    out, tg, again, sq, cq, so, co, gw, gb, fg, up, dn = res
    grads = (again, sq.reshape(3, F, D), cq.reshape(3, F, D), so, co, gw, gb, fg, up, dn)
    if outer > 1:
        first = (lax.axis_index("dp") % 8 == 0).astype(f32)
        grads = lax.psum(tuple(g * first for g in grads), "dp")
    return (out, tg) + tuple(grads)


def solution(mesh):
    rows = P(("dp", "mp"), None)
    weights = (P(), P(None, "mp", None), P(None, "mp", None), P("mp", None), P("mp", None), P(), P(), P(), P(None, "mp"), P("mp", None))
    return jax.shard_map(
        functools.partial(body, outer=mesh.shape["dp"] // 8),
        mesh=mesh,
        in_specs=(rows, P("dp", None)) + weights + (rows,),
        out_specs=(rows, rows) + weights,
        check_vma=False,
    )
```

```python
import functools

import jax
import jax.numpy as jnp
from jax import lax
from jax.experimental import pallas as pl
from jax.experimental.pallas import tpu as pltpu
from jax.sharding import PartitionSpec as P

HEAD = 64
LANG = 96
SLOTS = 128
EPS = 1e-5
NEG = -1e30
GC = 0.7978845608028654
GK = 0.044715
f32 = jnp.float32
bf16 = jnp.bfloat16
MESH = pl.DeviceIdType.MESH

AFTER = {
    "norm": (("agp", 1), ("agp", 0), ("agp", 2), ("agp", 3), ("zw", 0, 1), ("zw", 0, 2), ("ag2", 0),),
    "A0p0": (("ag1", 1), ("zw", 0, 3), ("zs", 1),),
    "A0p2": (("ag3", 0),),
    "A0p3": (("ag2", 1),),
    "A0s": (("zw", 1, 1),),
    "gate": (("zw", 1, 2), ("ag1", 2),),
    "A1p0": (("ag1", 3),),
    "A1p1": (("zw", 1, 3), ("ag2", 2),),
    "A1p3": (("ag3", 1),),
    "A2q": (("ag1", 4),),
    "A2p0": (("ag2", 3),),
    "A2p1": (("ag3", 2), ("ag1", 5),),
    "A2s": (("ag2", 4),),
    "F0a": (("ag3", 3),),
    "F0b": (("ag2", 5),),
    "F1a": (("rs0", 0),),
    "F1b": (("ag3", 4),),
    "F1c": (("rs0", 1), ("rs1", 0),),
    "F2a": (("rs1", 1), ("ag3", 5),),
    "F2c": (("rs0", 2),),
    "F3a": (("rs2", 0),),
    "F3b": (("rs1", 2),),
    "F3c": (("rs0", 3), ("rs2", 1),),
    "mid2": (("rs1", 3),),
    "outmm": (("rs0", 4),),
    "B0o": (("rs3", 1), ("rs2", 2),),
    "B0p0": (("rs3", 0),),
    "B0p1": (("rs1", 4), ("zfa", 0, 2),),
    "B0g": (("rs0", 5),),
    "B1o": (("rs2", 3), ("g", 0), ("rs1", 5),),
    "B1p2": (("zfa", 0, 3), ("g", 1),),
    "B1g": (("rs0", 6), ("rs2", 4), ("rs3", 2),),
    "B2o": (("rs2", 5), ("rs1", 6),),
    "B2p0": (("g", 2),),
    "B2p1": (("rs3", 3),),
    "B2g": (("rs0", 7), ("rs3", 5), ("rs1", "z0"),),
    "B2h": (("rs1", 7),),
    "B3o": (("rs2", 6), ("zza", 0, 3),),
    "B3p1": (("rs3", 4), ("rs2", "z0"),),
    "B3p2": (("zza", 0, 2),),
    "B3g": (("rs0", 8), ("g", 3), ("rs2", 7), ("zza", 2, 3), ("rs3", 6), ("rs1", 8), ("rs3", "z0"), ("zza", 1, 2),),
    "B3h": (("fin0", 0), ("g", 4),),
    "tail": (("v", 0), ("rs2", 8), ("zza", 2, 2), ("rs3", 7), ("g", 5), ("v", 1), ("fin1", 0), ("rs3", 8), ("zza", 1, 3), ("fin0", 2), ("g", 6), ("v", 2), ("fin0", 1), ("fin1", 2), ("g", 7), ("fin1", 1), ("v", 3), ("fin2", 0), ("fin2", 2), ("fin2", 1), ("fin3", 0), ("v", 4), ("fin3", 2), ("g", 8), ("fin3", 1),),
}


def mm(lhs, rhs, form):
    dims = {"nn": ((1,), (0,)), "nt": ((1,), (1,)), "tn": ((0,), (0,))}[form]
    return lax.dot_general(lhs, rhs, (dims, ((), ())), preferred_element_type=f32)


def blk(start, size, align):
    return pl.ds(pl.multiple_of(start, align), size)


def standardize(rows):
    centre = jnp.mean(rows, axis=1, keepdims=True)
    offset = rows - centre
    spread = jnp.mean(offset * offset, axis=1, keepdims=True)
    inv = lax.rsqrt(spread + EPS)
    return offset * inv, inv


def layer_kernel(
    x_hbm, og_hbm, gate_hbm, marks_ref, again_ref, fgain_ref, gbias_ref,
    sq_ref, cq_ref, so_ref, co_ref, up_ref, dn_ref,
    out_hbm, tg_hbm, fin, gout, vec_ref,
    buf, crecv, p1a, p1b, p2a, p2b, cr_o, p1a_o, p1b_o, p2a_o, p2b_o,
    z_f, z_o, z_q, e_f, e_o, e_q, zr, ze, p1a_z, p1b_z, p2a_z, p2b_z, gg, gcr, gxr, gyr, gzr, vs, vr, vz,
    og_ref, bias_ref, h, qkv, o, lse, sc, aa, mid, h2, acc, gh, eb, wb,
    io, loc, ap_s, ap_r, a0_s, a0_r, az_s, az_r, a1_s, a1_r, a2_s, a2_r, ac_s, ac_r,
    rc_s, rc_r, r1_s, r1_r, r2_s, r2_r, rz_s, rz_r, re_r, zf_s, zf_r, zfe_r,
    f1_s, f1_r, f2_s, f2_r, fc_s, fc_r, fl,
    g_s, g_r, gz_s, gz_r, ga_s, ga_r, gl, v_s, v_r, vz_s, vz_r,
):
    R, D = x_hbm.shape
    gate_ref = buf.at[2, 0, 0]
    x_ref = eb
    gz = og_ref
    CH = buf.shape[3]
    XH, YH = CH // 2, D // 2
    ZF = zr.shape[2]
    AR = XH // 2
    QR = sq_ref.shape[0]
    F = QR // 3
    heads = F // HEAD
    pages = R // SLOTS
    GX = gg.shape[2] // 2

    dp = lax.axis_index("dp")
    z = lax.axis_index("mp")
    c = dp % 2
    x = (dp // 2) % 2
    y = (dp // 4) % 2
    s = z // 2
    ismid = (z + s) % 2
    dev_c = (dp + 1 - 2 * c, z)
    dev_x = (dp + 2 - 4 * x, z)
    dev_y = (dp + 4 - 8 * y, z)

    def zof(slot):
        b0, b1 = slot % 2, slot // 2
        near = (1 - b0) * z + b0 * (4 * s + 1 - z)
        far = (1 - b0) * (2 - s) + b0 * (3 - 3 * s)
        return (1 - b1) * near + b1 * far

    def seen_as(slot):
        is1 = 1 - slot // 2
        return is1 + (1 - is1) * (3 - ismid)

    def remote(src, dst, ss, rs, dev):
        return pltpu.make_async_remote_copy(
            src_ref=src, dst_ref=dst, send_sem=ss, recv_sem=rs, device_id=dev, device_id_type=MESH
        )

    bar = pltpu.get_barrier_semaphore()
    partners = (dev_c, dev_x, dev_y, (dp, zof(1)), (dp, zof(2)), (dp, zof(3)))
    for dev in partners:
        pl.semaphore_signal(bar, inc=1, device_id=dev, device_id_type=MESH)

    ins = [
        pltpu.make_async_copy(src, dst, io.at[i])
        for i, (src, dst) in enumerate(((x_hbm, x_ref), (gate_hbm, gate_ref), (og_hbm, og_ref)))
    ]
    ins[0].start()
    local = []
    for i, (src, g, cc, r0) in enumerate(
        (
            (sq_ref, 0, 0, 0), (so_ref, 0, 0, QR), (cq_ref, 0, 1, 0), (co_ref, 0, 1, QR),
            (up_ref, 1, 0, 0), (dn_ref, 1, 1, 0),
        )
    ):
        cp = pltpu.make_async_copy(src, buf.at[g, cc, z, pl.ds(r0, src.shape[0]), :], loc.at[i])
        cp.start()
        local.append(cp)
    ins[1].start()
    ins[2].start()

    def wpart(g, cc, zz, r0, nr, c0, nc):
        return buf.at[g, cc, zz, blk(r0, nr, 16), blk(c0, nc, 128)]

    def wquarter(g, zz):
        return wpart(g, c, zz, XH * x, XH, YH * y, YH)

    def z_copy(g, zz, slot_to, sidx, rslot):
        ref = wquarter(g, zz)
        return remote(ref, ref, az_s.at[g, sidx], az_r.at[g, rslot], (dp, zof(slot_to)))

    PIECES = 4

    def piece(zz, q):
        n = AR // PIECES
        out = []
        for i in range(2):
            ref = wpart(0, c, zz, XH * x + AR * i + n * q, n, YH * y, YH)
            out.append(remote(ref, ref, ap_s.at[q, i], ap_r.at[q, i], (dp, zof(1))))
        return out

    def piece_p1(zz, xx, yy, q):
        n = AR // PIECES
        ra = wpart(0, c, zz, XH * xx + n * q, n, YH * y, YH)
        rb = wpart(0, c, zz, XH * x + AR + n * q, n, YH * yy, YH)
        return (
            remote(ra, ra, a0_s.at[q, 0], a0_r.at[q, 0], dev_x), remote(rb, rb, a0_s.at[q, 1], a0_r.at[q, 1], dev_y)
        )

    def ag_piece(q):
        for cp in piece(zof(1), q):
            cp.wait_recv()
        for cp in piece_p1(zof(1), x, y, q):
            cp.start()

    def ag_zsend(g):
        if g == 0:
            for q in range(PIECES):
                for cp in piece(z, q):
                    cp.start()
        else:
            z_copy(g, z, 1, 0, 1).start()

        @pl.when(ismid == 1)
        def _():
            z_copy(g, z, 2, 1, 2).start()

    def ag_zsend_wait(g):
        if g == 0:
            for q in range(PIECES):
                for cp in piece(z, q):
                    cp.wait_send()
        else:
            z_copy(g, z, 1, 0, 1).wait_send()

        @pl.when(ismid == 1)
        def _():
            for i in range(1, 5):
                z_copy(g, z, 1, i, 1).wait_send()

    def ag_p1(g, j):
        zz = zof(j)
        ra = wpart(g, c, zz, XH * x, AR, YH * y, YH)
        rb = wpart(g, c, zz, XH * x + AR, AR, YH * y, YH)
        ia = wpart(g, c, zz, XH * (1 - x), AR, YH * y, YH)
        ib = wpart(g, c, zz, XH * x + AR, AR, YH * (1 - y), YH)
        return (
            (remote(ra, ra, a1_s.at[g, j, 0], a1_r.at[g, j, 0], dev_x),
             remote(rb, rb, a1_s.at[g, j, 1], a1_r.at[g, j, 1], dev_y)),
            (remote(ia, ia, a1_s.at[g, j, 0], a1_r.at[g, j, 0], dev_x),
             remote(ib, ib, a1_s.at[g, j, 1], a1_r.at[g, j, 1], dev_y)),
        )

    def ag_p2(g, j):
        zz = zof(j)
        outs, ins = [], []
        for xx in range(2):
            ra = wpart(g, c, zz, XH * xx, AR, YH * y, YH)
            ia = wpart(g, c, zz, XH * xx, AR, YH * (1 - y), YH)
            outs.append(remote(ra, ra, a2_s.at[g, j, xx], a2_r.at[g, j, xx], dev_y))
            ins.append(remote(ia, ia, a2_s.at[g, j, xx], a2_r.at[g, j, xx], dev_y))
        rb = wpart(g, c, zz, XH * x + AR, AR, 0, D)
        ib = wpart(g, c, zz, XH * (1 - x) + AR, AR, 0, D)
        outs.append(remote(rb, rb, a2_s.at[g, j, 2], a2_r.at[g, j, 2], dev_x))
        ins.append(remote(ib, ib, a2_s.at[g, j, 2], a2_r.at[g, j, 2], dev_x))
        return outs, ins

    def ag_c(g, j):
        zz = zof(j)
        mine, theirs = buf.at[g, c, zz], buf.at[g, 1 - c, zz]
        return (
            remote(mine, mine, ac_s.at[g, j], ac_r.at[g, j], dev_c),
            remote(theirs, theirs, ac_s.at[g, j], ac_r.at[g, j], dev_c),
        )

    def ag_forward(g, j):
        @pl.when(ismid == 1)
        def _():
            if g == 1 or j > 1:
                z_copy(g, zof(j), 1, 0, j).wait_recv()
            if j == 1:
                z_copy(g, zof(1), 2, 2, 3).start()
            else:
                z_copy(g, zof(j), 1, j + 1, j).start()

    def ag_1(t):
        g, j = t // 3, t % 3 + 1

        @pl.when(ismid == 0)
        def _():
            z_copy(g, zof(j), 1, 0, j).wait_recv()

        for cp in ag_p1(g, j)[0]:
            cp.start()

    def ag_2(t):
        g, j = t // 3, t % 3 + 1
        if t == 0:
            outs = [cp for q in range(PIECES) for cp in piece_p1(zof(1), x, y, q)]
            arrivals = [cp for q in range(PIECES) for cp in piece_p1(zof(1), 1 - x, 1 - y, q)]
        else:
            outs, arrivals = ag_p1(g, j)
        for cp in arrivals:
            cp.wait_recv()
        for cp in ag_p2(g, j)[0]:
            cp.start()
        for cp in outs:
            cp.wait_send()

    def ag_3(t):
        g, j = t // 3, t % 3 + 1
        outs, arrivals = ag_p2(g, j)
        for cp in arrivals:
            cp.wait_recv()
        ag_c(g, j)[0].start()
        for cp in outs:
            cp.wait_send()

    def ag_done(g, j):
        mine, theirs = ag_c(g, j)
        theirs.wait_recv()
        mine.wait_send()

    def add_rows(dst, dst_idx, r0, nr, c0, nc, src, src_idx):
        step = next(n for n in (64, 48) if nr % n == 0)

        @pl.loop(0, nr // step)
        def _(i):
            rows = blk(r0 + i * step, step, 16)
            cols = blk(c0, nc, 128)
            d = dst[(*dst_idx, rows, cols)].astype(f32)
            t = src[(*src_idx, blk(i * step, step, 16), slice(None))].astype(f32)
            dst[(*dst_idx, rows, cols)] = (d + t).astype(bf16)

    def single(b, nr, ha, kq, slot, sem):
        def reg(cc, r0, n, c0, w):
            return buf.at[b, cc, kq, blk(r0, n, 16), blk(c0, w, 128)]

        def add(r0, n, c0, w, src, idx):
            add_rows(buf, (b, c, kq), r0, n, c0, w, src, idx)

        return dict(
            reg=reg, add=add, nr=nr, ha=ha, off=0, sem=sem,
            cr=(crecv, (slot,), pl.ds(0, nr)), a1=(p1a, (slot,), pl.ds(0, ha)),
            b1=[(p1b, (slot, xx), pl.ds(0, ha)) for xx in range(2)],
            a2=(p2a, (slot,), pl.ds(0, ha)), b2=(p2b, (slot,), pl.ds(0, ha)),
        )

    def k_ffn(k):
        return single(2, CH, (XH - ZF) // 2, k, k, k)

    def k_first():
        kd = k_ffn(0)
        every = slice(None)
        kd.update(
            off=XH - ZF, ha=ZF // 2, sem=9, a1=(p1a_z, (), every), b1=[(p1b_z, (xx,), every) for xx in range(2)],
            a2=(p2a_z, (), every), b2=(p2b_z, (), every),
        )
        return kd

    def k_qkv(i):
        return single(1, QR, QR // 4, 3 - i, i, 5 + i)

    def k_out():
        def reg(cc, r0, n, c0, w):
            return buf.at[1, cc, :, blk(QR + r0, n, 16), blk(c0, w, 128)]

        def add(r0, n, c0, w, src, idx):
            for q in range(4):
                add_rows(buf, (1, c, q), QR + r0, n, c0, w, src, (*idx, q))

        every = slice(None)
        return dict(
            reg=reg, add=add, nr=F, ha=F // 4, off=0, sem=4,
            cr=(cr_o, (), every), a1=(p1a_o, (), every), b1=[(p1b_o, (xx,), every) for xx in range(2)],
            a2=(p2a_o, (), every), b2=(p2b_o, (), every),
        )

    def land(part):
        ref, idx, rows = part
        return ref.at[(*idx, rows)]

    def rs_c(kd):
        n = kd["sem"]
        return remote(kd["reg"](1 - c, 0, kd["nr"], 0, D), land(kd["cr"]), rc_s.at[n], rc_r.at[n], dev_c)

    def rs_p1(kd):
        n, half, ha, reg, off = kd["sem"], kd["nr"] // 2, kd["ha"], kd["reg"], kd["off"]
        cps = [remote(reg(c, half * (1 - x) + off, ha, 0, D), land(kd["a1"]), r1_s.at[n, 0], r1_r.at[n, 0], dev_x)]
        for xx in range(2):
            src = reg(c, half * xx + off + ha, ha, YH * (1 - y), YH)
            cps.append(remote(src, land(kd["b1"][xx]), r1_s.at[n, 1 + xx], r1_r.at[n, 1 + xx], dev_y))
        return cps

    def rs_p2(kd):
        n, half, ha, reg, off = kd["sem"], kd["nr"] // 2, kd["ha"], kd["reg"], kd["off"]
        return [
            remote(reg(c, half * x + off, ha, YH * (1 - y), YH), land(kd["a2"]), r2_s.at[n, 0], r2_r.at[n, 0], dev_y),
            remote(
                reg(c, half * (1 - x) + off + ha, ha, YH * y, YH), land(kd["b2"]), r2_s.at[n, 1], r2_r.at[n, 1], dev_x
            ),
        ]

    def rs_0(kd):
        rs_c(kd).start()

    def rs_1(kd, between=None):
        cp = rs_c(kd)
        cp.wait_recv()
        kd["add"](0, kd["nr"], 0, D, kd["cr"][0], kd["cr"][1])
        if between is not None:
            between()
        for q in rs_p1(kd):
            q.start()
        cp.wait_send()

    def rs_2(kd):
        half, ha, off = kd["nr"] // 2, kd["ha"], kd["off"]
        cps = rs_p1(kd)
        for q in cps:
            q.wait_recv()
        kd["add"](half * x + off, ha, 0, D, kd["a1"][0], kd["a1"][1])
        for xx in range(2):
            kd["add"](half * xx + off + ha, ha, YH * y, YH, kd["b1"][xx][0], kd["b1"][xx][1])
        for q in rs_p2(kd):
            q.start()
        for q in cps:
            q.wait_send()

    def rs_3(kd, after=None):
        half, ha, off = kd["nr"] // 2, kd["ha"], kd["off"]
        cps = rs_p2(kd)
        for q in cps:
            q.wait_recv()
        kd["add"](half * x + off, ha, YH * y, YH, kd["a2"][0], kd["a2"][1])
        kd["add"](half * x + off + ha, ha, YH * y, YH, kd["b2"][0], kd["b2"][1])
        if after is not None:
            after()
        for q in cps:
            q.wait_send()

    groups = (
        (2, 0, XH, XH - ZF, z_f, e_f),
        (1, QR, F // 2, F // 2, z_o, e_o),
        (1, 0, QR // 2, QR // 2, z_q, e_q),
    )

    def z_part(gi, k):
        b, r0, half, n = groups[gi][:4]
        return buf.at[b, c, k, blk(r0 + half * x, n, 16), blk(YH * y, YH, 128)]

    def z_out(gi, k):
        return remote(z_part(gi, k), groups[gi][4].at[0 if k == 1 else 1], rz_s.at[gi, k], rz_r.at[gi, 0 if k == 1 else 1], (dp, zof(k)))

    def z_hop(gi, k):
        return remote(z_part(gi, k), groups[gi][5].at[k - 2], rz_s.at[gi, k], re_r.at[gi, k - 2], (dp, zof(1)))

    def z_start(gi, k):
        if k == 1:
            z_out(gi, 1).start()
        if k > 1:

            @pl.when(ismid == 0)
            def _():
                z_hop(gi, k).start()

    def z_join(gi, k):
        b, r0, half, n, _to, mid_buf = groups[gi]

        @pl.when(ismid == 1)
        def _():
            z_hop(gi, k).wait_recv()
            add_rows(buf, (b, c, k), r0 + half * x, n, YH * y, YH, mid_buf, (k - 2,))
            z_out(gi, k).start()

    def zf_rows(k, xx):
        return buf.at[2, c, k, pl.ds(XH * (xx + 1) - ZF, ZF), :]

    def zf_out(k, xx):
        to = 0 if k == 1 else 1
        return remote(zf_rows(k, xx), zr.at[to, xx], zf_s.at[k, xx], zf_r.at[to, xx], (dp, zof(k)))

    def zf_hop(k, xx):
        return remote(zf_rows(k, xx), ze.at[k - 2, xx], zf_s.at[k, xx], zfe_r.at[k - 2, xx], (dp, zof(1)))

    def zf_start(k):
        if k == 1:
            for xx in range(2):
                zf_out(1, xx).start()
        if k > 1:

            @pl.when(ismid == 0)
            def _():
                for xx in range(2):
                    zf_hop(k, xx).start()

    def zf_join(_gi, k):
        @pl.when(ismid == 1)
        def _():
            for xx in range(2):
                zf_hop(k, xx).wait_recv()
                add_rows(buf, (2, c, k), XH * (xx + 1) - ZF, ZF, 0, D, ze, (k - 2, xx))
                zf_out(k, xx).start()

    def zf_sum():
        for xx in range(2):
            for slot in range(2):
                zf_out(1 + slot, xx).wait_recv()
                add_rows(buf, (2, c, 0), XH * (xx + 1) - ZF, ZF, 0, D, zr, (slot, xx))
        for q in rs_p1(k_first()):
            q.start()

    def fin_part(gi, r, n, c0, w):
        r0 = groups[gi][1]
        return fin.at[0 if gi == 0 else 1, c, blk(r0 + r, n, 16), blk(c0, w, 128)]

    def own_part(gi, r, n):
        b, r0 = groups[gi][:2]
        return buf.at[b, c, 0, blk(r0 + r, n, 16), blk(YH * y, YH, 128)]

    def fin_p1(gi):
        half = groups[gi][2]
        q = half // 2
        return [
            remote(
                own_part(gi, half * x + q * i, q), fin_part(gi, half * x + q * i, q, YH * y, YH),
                f1_s.at[gi, i], f1_r.at[gi, i], dev,
            )
            for i, dev in enumerate((dev_x, dev_y))
        ]

    def fin_local(gi):
        half = groups[gi][2]
        return pltpu.make_async_copy(
            own_part(gi, half * x, half), fin_part(gi, half * x, half, YH * y, YH), fl.at[gi]
        )

    def fin_p2(gi):
        half = groups[gi][2]
        q = half // 2
        cps = []
        for xx in range(2):
            ref = fin_part(gi, half * xx, q, YH * y, YH)
            cps.append(remote(ref, ref, f2_s.at[gi, xx], f2_r.at[gi, xx], dev_y))
        ref = fin_part(gi, half * x + q, q, 0, D)
        cps.append(remote(ref, ref, f2_s.at[gi, 2], f2_r.at[gi, 2], dev_x))
        return cps

    def fin_c(gi):
        ref = fin_part(gi, 0, 2 * groups[gi][2], 0, D)
        return remote(ref, ref, fc_s.at[gi], fc_r.at[gi], dev_c)

    def fin_0(gi):
        b, r0, half, n, part, _mid = groups[gi]
        for k in (1, 2):
            z_out(gi, k).wait_recv()
        for slot in range(2):
            add_rows(buf, (b, c, 0), r0 + half * x, n, YH * y, YH, part, (slot,))
        for q in fin_p1(gi):
            q.start()
        fin_local(gi).start()
        for k in (1, 2, 3):
            z_out(gi, k).wait_send()
            if gi == 0:
                for xx in range(2):
                    zf_out(k, xx).wait_send()

    def fin_1(gi):
        for q in fin_p1(gi):
            q.wait_recv()
        fin_local(gi).wait()
        for q in fin_p2(gi):
            q.start()
        for q in fin_p1(gi):
            q.wait_send()

    def fin_2(gi):
        for q in fin_p2(gi):
            q.wait_recv()
        fin_c(gi).start()
        for q in fin_p2(gi):
            q.wait_send()

    def fin_3(gi):
        fin_c(gi).wait_recv()
        fin_c(gi).wait_send()

    def g_copy(i):
        xs, xo = blk(GX * x, GX, 16), blk(GX * (1 - x), GX, 16)
        ys, yo = blk(YH * y, YH, 128), blk(YH * (1 - y), YH, 128)
        src, dst, dev = {
            0: lambda: (gg.at[:, 1 - c], gcr, dev_c),
            1: lambda: (gg.at[:, c, xo, :], gxr, dev_x),
            2: lambda: (gg.at[:, c, xs, yo], gyr, dev_y),
            3: lambda: (gout.at[:, c, xs, ys], gout.at[:, c, xs, ys], dev_y),
            4: lambda: (gout.at[:, c, xs, :], gout.at[:, c, xs, :], dev_x),
            5: lambda: (gout.at[:, c], gout.at[:, c], dev_c),
        }[i]()
        return remote(src, dst, g_s.at[i], g_r.at[i], dev)

    def g_z(slot, rslot):
        src = gg.at[zof(slot), c, blk(GX * x, GX, 16), blk(YH * y, YH, 128)]
        return remote(src, gzr.at[rslot - 1], gz_s.at[slot], gz_r.at[rslot], (dp, zof(slot)))

    def g_za(slot, rslot):
        src = gg.at[z, c, blk(GX * x, GX, 16), blk(YH * y, YH, 128)]
        dst = gout.at[z, c, blk(GX * x, GX, 16), blk(YH * y, YH, 128)]
        return remote(src, dst, ga_s.at[slot], ga_r.at[rslot], (dp, zof(slot)))

    def g_local():
        src = gg.at[z, c, blk(GX * x, GX, 16), blk(YH * y, YH, 128)]
        dst = gout.at[z, c, blk(GX * x, GX, 16), blk(YH * y, YH, 128)]
        return pltpu.make_async_copy(src, dst, gl.at[0])

    def g_step(i):
        xs, ys = blk(GX * x, GX, 16), blk(YH * y, YH, 128)
        if i == 0:
            g_copy(0).start()
        if i == 1:
            g_copy(0).wait_recv()
            for q in range(4):
                add_rows(gg, (q, c), 0, 2 * GX, 0, D, gcr, (q,))
            g_copy(1).start()
            g_copy(0).wait_send()
        if i == 2:
            g_copy(1).wait_recv()
            for q in range(4):
                add_rows(gg, (q, c), GX * x, GX, 0, D, gxr, (q,))
            g_copy(2).start()
            g_copy(1).wait_send()
        if i == 3:
            g_copy(2).wait_recv()
            for q in range(4):
                add_rows(gg, (q, c), GX * x, GX, YH * y, YH, gyr, (q,))
            for slot in range(1, 4):
                g_z(slot, seen_as(slot)).start()
            g_copy(2).wait_send()
        if i == 4:
            for slot in range(1, 4):
                g_z(slot, slot).wait_recv()
            t = gg[z, c, xs, ys].astype(f32)
            for slot in range(3):
                t = t + gzr[slot].astype(f32)
            gg[z, c, xs, ys] = t.astype(bf16)
            g_local().start()
            for slot in range(1, 4):
                g_za(slot, seen_as(slot)).start()
            for slot in range(1, 4):
                g_z(slot, slot).wait_send()
        if i == 5:
            for slot in range(1, 4):
                g_za(slot, slot).wait_recv()
            g_local().wait()
            g_copy(3).start()
            for slot in range(1, 4):
                g_za(slot, slot).wait_send()
        if i == 6:
            g_copy(3).wait_recv()
            g_copy(4).start()
            g_copy(3).wait_send()
        if i == 7:
            g_copy(4).wait_recv()
            g_copy(5).start()
            g_copy(4).wait_send()
        if i == 8:
            g_copy(5).wait_recv()
            g_copy(5).wait_send()

    def v_copy(i):
        return remote(vs.at[i], vr.at[i], v_s.at[i], v_r.at[i], (dev_c, dev_x, dev_y)[i])

    def v_z(slot, zz_dst, rslot):
        return remote(vz.at[z], vz.at[zz_dst], vz_s.at[slot], vz_r.at[rslot], (dp, zof(slot)))

    def v_step(i):
        if i == 0:
            v_copy(0).start()
        if i in (1, 2):
            v_copy(i - 1).wait_recv()
            vs[i] = vs[i - 1] + vr[i - 1]
            v_copy(i).start()
            v_copy(i - 1).wait_send()
        if i == 3:
            v_copy(2).wait_recv()
            vz[z] = vs[2] + vr[2]
            for slot in range(1, 4):
                v_z(slot, z, seen_as(slot)).start()
            v_copy(2).wait_send()
        if i == 4:
            for slot in range(1, 4):
                v_z(slot, z, slot).wait_recv()
            vec_ref[...] = (vz[0] + vz[1]) + (vz[2] + vz[3])
            for slot in range(1, 4):
                v_z(slot, z, slot).wait_send()

    def kind(n):
        if n == "z0":
            return k_first()
        return k_ffn(n) if n < 4 else k_out() if n == 4 else k_qkv(n - 5)

    def first(n):
        if n == "z0":
            zf_sum()
        else:
            rs_1(kind(n), lambda: zf_start(n) if n < 4 else None)

    def third(n):
        if n == "z0":
            rs_3(kind(n))
        elif n < 4:
            rs_3(kind(n), lambda: z_start(0, n))
        elif n == 4:
            rs_3(kind(n), lambda: [z_start(1, q) for q in range(1, 4)])
        else:
            rs_3(kind(n), lambda: z_start(2, 8 - n))

    events = {
        "zs": ag_zsend, "zw": ag_forward, "agp": ag_piece, "ag1": ag_1, "ag2": ag_2, "ag3": ag_3,
        "rs0": lambda n: rs_0(kind(n)), "rs1": first, "rs2": lambda n: rs_2(kind(n)), "rs3": third,
        "zza": z_join, "zfa": zf_join, "g": g_step, "v": v_step, "fin0": fin_0, "fin1": fin_1, "fin2": fin_2, "fin3": fin_3,
    }

    def after(name, k=None, p=None):
        if k is None:
            for ev in AFTER.get(name, ()):
                events[ev[0]](*ev[1:])
            return
        for kk in range(4):
            for pp in range(1 if p is None else 4):
                found = AFTER.get(name[0] + str(kk) + name[1:] + ("" if p is None else str(pp)), ())
                if found:

                    @pl.when((k == kk) if p is None else (k == kk) & (p == pp))
                    def _():
                        for ev in found:
                            events[ev[0]](*ev[1:])

    TR = 128
    again = again_ref[...].astype(f32).reshape(1, D)
    fgain = fgain_ref[...].astype(f32).reshape(1, D)
    gbias = gbias_ref[...].astype(f32).reshape(1, D)

    pl.semaphore_wait(bar, 6)
    for cp in local[:4]:
        cp.wait()
    ag_zsend(0)

    after("start")

    key_id = lax.broadcasted_iota(jnp.int32, (SLOTS, SLOTS), 0)
    query_id = lax.broadcasted_iota(jnp.int32, (SLOTS, SLOTS), 1)
    key_kind = jnp.where(key_id < LANG, 1, 0)
    query_kind = jnp.where(query_id < LANG, 1, 0)
    for p in range(pages):
        row = marks_ref[pl.ds(pages * z + p, 1), :]
        real = jnp.broadcast_to(jnp.where(row > 0, 0.0, NEG), (SLOTS, SLOTS)).T
        bias_ref[0, p] = jnp.where(key_kind == query_kind, real, NEG).astype(bf16)
        bias_ref[1, p] = jnp.where(key_kind == query_kind, NEG, real).astype(bf16)

    ins[0].wait()

    @pl.loop(0, R // TR)
    def _(i):
        rows = blk(i * TR, TR, 16)
        u, _inv = standardize(x_ref[rows, :].astype(f32))
        h[rows, :] = (u * again).astype(bf16)
        sc[rows, :] = jnp.zeros((TR, D), f32)
        mid[rows, :] = jnp.zeros((TR, D), f32)
        gh[rows, :] = jnp.zeros((TR, D), f32)

    vs[...] = jnp.zeros_like(vs)
    for cp in local[4:] + ins[1:]:
        cp.wait()
    after("norm")

    @pl.loop(0, 4)
    def _(k):
        zz = zof(k)

        @pl.when(k > 0)
        def _():
            ag_done(0, k)

        for at in range(2):
            qkv[at, k] = mm(buf[0, at, zz, 0:QR, :], h[...], "nt").astype(bf16)
        after("Aq", k)

        @pl.loop(0, pages)
        def _(p):
            cols = blk(p * SLOTS, SLOTS, 128)
            units = [(at, hh) for at in range(2) for hh in range(heads)]
            scores = []
            for at, hh in units:
                qt = qkv[at, k, HEAD * hh : HEAD * (hh + 1), cols]
                kt = qkv[at, k, F + HEAD * hh : F + HEAD * (hh + 1), cols]
                scores.append(mm(kt, qt, "tn"))
            probs = []
            for (at, hh), st in zip(units, scores):
                st = st * HEAD ** (-0.5) + bias_ref[at, p].astype(f32)
                top = jnp.max(st, axis=0, keepdims=True)
                ex = jnp.exp(st - top)
                tot = jnp.sum(ex, axis=0, keepdims=True)
                probs.append((ex * (1.0 / tot)).astype(bf16))
                lse[at, k, hh : hh + 1, cols] = top + jnp.log(tot)
            for (at, hh), pt in zip(units, probs):
                vt = qkv[at, k, 2 * F + HEAD * hh : 2 * F + HEAD * (hh + 1), cols]
                o[at, k, HEAD * hh : HEAD * (hh + 1), cols] = mm(vt, pt, "nn").astype(bf16)
            after("Ap", k, p)

        @pl.loop(0, 2)
        def _(p):
            cols = blk(p * 256, 256, 128)
            for at, dst in ((0, sc), (1, mid)):
                dst[cols, :] += mm(o[at, k, :, cols], buf[0, at, zz, QR:CH, :], "tn")

        after("As", k)

        @pl.when(k == 0)
        def _():
            @pl.loop(0, R // 256)
            def _(i):
                rows = blk(i * 256, 256, 16)
                aa[rows, :] = jax.nn.sigmoid(mm(h[rows, :], gate_ref[...], "nn") + gbias)

            after("gate")

    ag_zsend_wait(0)

    @pl.loop(0, R // TR)
    def _(i):
        rows = blk(i * TR, TR, 16)
        a = aa[rows, :]
        sv, cv = sc[rows, :], mid[rows, :]
        mv = x_ref[rows, :].astype(f32) + a * sv + (1.0 - a) * cv
        sc[rows, :] = sv - cv
        mid[rows, :] = mv
        acc[rows, :] = mv
        u, _inv = standardize(mv)
        h2[rows, :] = (u * fgain).astype(bf16)

    after("join")

    @pl.loop(0, 4)
    def _(k):
        zz = zof(k)

        @pl.when(k > 0)
        def _():
            ag_done(1, k)

        MT = 256

        @pl.loop(0, 2 * (R // MT))
        def _(i):
            rows = blk((i // 2) * MT, MT, 16)
            cols = blk((i % 2) * XH, XH, 128)
            w = mm(h2[rows, :], buf[1, 0, zz, :, cols], "nn")
            ge = mm(og_ref[rows, :], buf[1, 1, zz, blk((i % 2) * XH, XH, 16), :], "nt")
            w2 = w * w
            th = jnp.tanh(GC * w * (1.0 + GK * w2))
            half = 0.5 * (1.0 + th)
            eb[rows, cols] = (w * half).astype(bf16)
            dg = half + 0.5 * w * (1.0 - th * th) * (GC * (1.0 + 3.0 * GK * w2))
            wb[rows, cols] = (dg * ge).astype(bf16)

        after("Fa", k)

        @pl.loop(0, R // MT)
        def _(i):
            rows = blk(i * MT, MT, 16)
            acc[rows, :] += mm(eb[rows, :], buf[1, 1, zz], "nn")
            gh[rows, :] += mm(wb[rows, :], buf[1, 0, zz], "nt")

        after("Fb", k)

        @pl.loop(0, CH // 384)
        def _(i):
            cols = blk(i * 384, 384, 128)
            buf[2, 1, k, blk(i * 384, 384, 16), :] = mm(eb[:, cols], og_ref[...], "tn").astype(bf16)
            buf[2, 0, k, blk(i * 384, 384, 16), :] = mm(h2[:, cols], wb[...], "tn").astype(bf16)

        after("Fc", k)

    ag_zsend_wait(1)

    TS = 128
    zero_row = jnp.zeros((1, D), f32)

    def mid_back(i, sums):
        gain_sum, bias_sum = sums
        rows = blk(i * TS, TS, 16)
        h2[rows, :] = acc[rows, :].astype(bf16)
        u, inv = standardize(mid[rows, :])
        gy = gh[rows, :]
        gain_sum = gain_sum + jnp.sum(gy * u, axis=0, keepdims=True)
        sy = gy * fgain
        m1 = jnp.mean(sy, axis=1, keepdims=True)
        m2 = jnp.mean(sy * u, axis=1, keepdims=True)
        gm = og_ref[rows, :].astype(f32) + inv * (sy - m1 - u * m2)
        acc[rows, :] = gm
        a = aa[rows, :]
        eb[rows, :] = (a * gm).astype(bf16)
        wb[rows, :] = ((1.0 - a) * gm).astype(bf16)
        gzv = (gm * sc[rows, :] * a * (1.0 - a)).astype(bf16)
        gz[rows, :] = gzv
        bias_sum = bias_sum + jnp.sum(gzv.astype(f32), axis=0, keepdims=True)
        return gain_sum, bias_sum

    gain_sum, bias_sum = lax.fori_loop(0, R // TS, mid_back, (zero_row, zero_row))
    vs[0, 1:2, :] = bias_sum
    vs[0, 2:3, :] = gain_sum
    out_copy = pltpu.make_async_copy(h2, out_hbm, io.at[3])
    out_copy.start()
    after("mid2")
    gate_again = buf.at[2, 1 - c, 1]
    gate_load = pltpu.make_async_copy(gate_hbm, gate_again, io.at[5])
    gate_load.start()

    for k in range(4):
        for at, gref in ((0, eb), (1, wb)):
            buf[1, at, k, QR:CH, :] = mm(o[at, k], gref[...], "nn").astype(bf16)
    after("outmm")
    for i in range(4):
        t = mm(h[:, F * i : F * (i + 1)], gz[...], "tn").astype(bf16)
        gg[i, 0] = t[: F // 2]
        gg[i, 1] = t[F // 2 :]
    after("ggrad")

    x_again = wb
    x_load = pltpu.make_async_copy(x_hbm, x_again, io.at[6])

    @pl.loop(0, 4)
    def _(i):
        k = 3 - i
        zz = zof(k)
        for at, gref in ((0, eb), (1, wb)):
            o[at, k] = mm(buf[0, at, zz, QR:CH, :], gref[...], "nt").astype(bf16)

        @pl.when(i == 3)
        def _():
            x_load.start()

        after("Bo", i)

        @pl.loop(0, pages)
        def _(p):
            cols = blk(p * SLOTS, SLOTS, 128)
            units = [(at, hh) for at in range(2) for hh in range(heads)]
            for grp in (units,):
                rd = []
                for at, hh in grp:
                    qs = slice(HEAD * hh, HEAD * (hh + 1))
                    ks = slice(F + HEAD * hh, F + HEAD * (hh + 1))
                    vsl = slice(2 * F + HEAD * hh, 2 * F + HEAD * (hh + 1))
                    qt, kt, vt, go = qkv[at, k, qs, cols], qkv[at, k, ks, cols], qkv[at, k, vsl, cols], o[at, k, qs, cols]
                    rd.append((at, hh, qs, ks, vsl, qt, kt, vt, go, mm(kt, qt, "tn"), mm(vt, go, "tn")))
                ps = []
                for at, hh, qs, ks, vsl, qt, kt, vt, go, st, gpt in rd:
                    pt = jnp.exp(st * HEAD ** (-0.5) + bias_ref[at, p].astype(f32) - lse[at, k, hh : hh + 1, cols])
                    pg = pt * gpt
                    gst = (pg - pt * jnp.sum(pg, axis=0, keepdims=True)).astype(bf16)
                    ps.append((pt.astype(bf16), gst))
                for (at, hh, qs, ks, vsl, qt, kt, vt, go, st, gpt), (pb, gst) in zip(rd, ps):
                    qkv[at, k, vsl, cols] = mm(go, pb, "nt").astype(bf16)
                    qkv[at, k, qs, cols] = (mm(kt, gst, "nn") * HEAD ** (-0.5)).astype(bf16)
                    qkv[at, k, ks, cols] = (mm(qt, gst, "nt") * HEAD ** (-0.5)).astype(bf16)
            after("Bp", i, p)

        for at in range(2):
            for q in range(3):
                part = slice(F * q, F * (q + 1))
                buf[1, at, k, part, :] = mm(qkv[at, k, part, :], h[...], "nn").astype(bf16)
        after("Bg", i)

        @pl.loop(0, 2)
        def _(p):
            cols = blk(p * 256, 256, 128)
            t = mm(qkv[0, k, :, cols], buf[0, 0, zz, 0:QR, :], "tn") + mm(qkv[1, k, :, cols], buf[0, 1, zz, 0:QR, :], "tn")

            @pl.when(i == 0)
            def _():
                gh[cols, :] = t

            @pl.when(i > 0)
            def _():
                gh[cols, :] += t

        after("Bh", i)

    gate_load.wait()

    @pl.loop(0, R // 256)
    def _(i):
        rows = blk(i * 256, 256, 16)
        gh[rows, :] += mm(gz[rows, :], gate_again[...], "nt")

    def first_back(i, gain_sum):
        rows = blk(i * TS, TS, 16)
        u, inv = standardize(x_again[rows, :].astype(f32))
        gy = gh[rows, :]
        gain_sum = gain_sum + jnp.sum(gy * u, axis=0, keepdims=True)
        sy = gy * again
        m1 = jnp.mean(sy, axis=1, keepdims=True)
        m2 = jnp.mean(sy * u, axis=1, keepdims=True)
        eb[rows, :] = (acc[rows, :] + inv * (sy - m1 - u * m2)).astype(bf16)
        return gain_sum

    x_load.wait()
    vs[0, 0:1, :] = lax.fori_loop(0, R // TS, first_back, zero_row)
    tg_copy = pltpu.make_async_copy(eb, tg_hbm, io.at[4])
    tg_copy.start()
    after("tail")
    out_copy.wait()
    tg_copy.wait()


def widen_kernel(
    out_in, tg_in, fin, gout, vec_in,
    out_o, tg_o, ag_o, sq_o, cq_o, so_o, co_o, gw_o, gb_o, fg_o, up_o, dn_o,
    narrow, wide, whole, sem_in, sem_out, sem_pass,
):
    F = so_o.shape[0]
    QR = 3 * F
    passes = []
    for i, (src, dst) in enumerate(((out_in, out_o), (tg_in, tg_o))):
        load = pltpu.make_async_copy(src, whole.at[i], sem_pass.at[i])
        passes.append((load, pltpu.make_async_copy(whole.at[i], dst, sem_pass.at[2 + i])))
    CH = 4 * F
    jobs = []
    for i, (src, dsts) in enumerate(
        (
            (gout, ((0, gw_o),)), (fin.at[0, 0], ((0, up_o),)), (fin.at[0, 1], ((0, dn_o),)),
            (fin.at[1, 0], ((0, sq_o), (QR, so_o))), (fin.at[1, 1], ((0, cq_o), (QR, co_o))),
        )
    ):
        load = pltpu.make_async_copy(src, narrow.at[pl.ds(CH * i, CH)], sem_in.at[i])
        saves = [
            pltpu.make_async_copy(wide.at[pl.ds(CH * i + r0, dst.shape[0])], dst, sem_out.at[i, q])
            for q, (r0, dst) in enumerate(dsts)
        ]
        load.start()
        jobs.append((load, saves))
    for load, _ in passes:
        load.start()
    ag_o[...] = vec_in[0, :]
    gb_o[...] = vec_in[1, :]
    fg_o[...] = vec_in[2, :]
    for i, (load, saves) in enumerate(jobs):
        load.wait()

        @pl.loop(0, CH // 64)
        def _(q):
            rows = blk(CH * i + 64 * q, 64, 16)
            wide[rows, :] = narrow[rows, :].astype(f32)

        for cp in saves:
            cp.start()
    for load, save in passes:
        load.wait()
        save.start()
    for _, saves in jobs:
        for cp in saves:
            cp.wait()
    for _, save in passes:
        save.wait()


def body(
    tokens, region_mask, attn_gain, self_qkv, cross_qkv, self_out, cross_out, gate_weight, gate_bias,
    ffn_gain, up_weight, down_weight, out_grad, *, outer,
):
    R, D = tokens.shape
    F = self_out.shape[0]
    QR = 3 * F
    CH = QR + F
    pages = R // SLOTS

    vm = pl.BlockSpec(memory_space=pltpu.VMEM)
    hb = pl.BlockSpec(memory_space=pl.ANY)
    dma = pltpu.SemaphoreType.DMA
    XH, YH, GX, OR, ZF = CH // 2, D // 2, D // 16, F // 4, CH // 6
    scratch = [
        pltpu.VMEM((3, 2, 4, CH, D), bf16),
        pltpu.VMEM((4, CH, D), bf16),
        pltpu.VMEM((4, QR // 4, D), bf16),
        pltpu.VMEM((4, 2, QR // 4, YH), bf16),
        pltpu.VMEM((4, QR // 4, YH), bf16),
        pltpu.VMEM((4, QR // 4, YH), bf16),
        pltpu.VMEM((4, F, D), bf16),
        pltpu.VMEM((4, OR, D), bf16),
        pltpu.VMEM((2, 4, OR, YH), bf16),
        pltpu.VMEM((4, OR, YH), bf16),
        pltpu.VMEM((4, OR, YH), bf16),
        pltpu.VMEM((2, XH - ZF, YH), bf16),
        pltpu.VMEM((2, F // 2, YH), bf16),
        pltpu.VMEM((2, QR // 2, YH), bf16),
        pltpu.VMEM((2, XH - ZF, YH), bf16),
        pltpu.VMEM((2, F // 2, YH), bf16),
        pltpu.VMEM((2, QR // 2, YH), bf16),
        pltpu.VMEM((2, 2, ZF, D), bf16),
        pltpu.VMEM((2, 2, ZF, D), bf16),
        pltpu.VMEM((ZF // 2, D), bf16),
        pltpu.VMEM((2, ZF // 2, YH), bf16),
        pltpu.VMEM((ZF // 2, YH), bf16),
        pltpu.VMEM((ZF // 2, YH), bf16),
        pltpu.VMEM((4, 2, 2 * GX, D), bf16),
        pltpu.VMEM((4, 2 * GX, D), bf16),
        pltpu.VMEM((4, GX, D), bf16),
        pltpu.VMEM((4, GX, YH), bf16),
        pltpu.VMEM((3, GX, YH), bf16),
        pltpu.VMEM((3, 8, D), f32),
        pltpu.VMEM((3, 8, D), f32),
        pltpu.VMEM((4, 8, D), f32),
        pltpu.VMEM((R, D), bf16),
        pltpu.VMEM((2, pages, SLOTS, SLOTS), bf16),
        pltpu.VMEM((R, D), bf16),
        pltpu.VMEM((2, 4, QR, R), bf16),
        pltpu.VMEM((2, 4, F, R), bf16),
        pltpu.VMEM((2, 4, 8, R), f32),
        pltpu.VMEM((R, D), f32),
        pltpu.VMEM((R, D), f32),
        pltpu.VMEM((R, D), f32),
        pltpu.VMEM((R, D), bf16),
        pltpu.VMEM((R, D), f32),
        pltpu.VMEM((R, D), f32),
        pltpu.VMEM((R, D), bf16),
        pltpu.VMEM((R, D), bf16),
        dma((7,)),
        dma((6,)), dma((4, 2)), dma((4, 2)), dma((4, 2)), dma((4, 2)), dma((2, 5)), dma((2, 4)), dma((2, 4, 2)), dma((2, 4, 2)), dma((2, 4, 3)), dma((2, 4, 3)),
        dma((2, 4)), dma((2, 4)),
        dma((9,)), dma((9,)), dma((10, 3)), dma((10, 3)), dma((10, 2)), dma((10, 2)), dma((3, 4)), dma((3, 2)),
        dma((3, 2)), dma((4, 2)), dma((2, 2)), dma((2, 2)),
        dma((3, 2)), dma((3, 2)), dma((3, 3)), dma((3, 3)), dma((3,)), dma((3,)), dma((3,)),
        dma((6,)), dma((6,)), dma((4,)), dma((4,)), dma((4,)), dma((4,)), dma((1,)),
        dma((3,)), dma((3,)), dma((4,)), dma((4,)),
    ]
    mid_out = pl.pallas_call(
        layer_kernel,
        out_shape=(
            jax.ShapeDtypeStruct((R, D), bf16),
            jax.ShapeDtypeStruct((R, D), bf16),
            jax.ShapeDtypeStruct((2, 2, CH, D), bf16),
            jax.ShapeDtypeStruct((4, 2, 2 * GX, D), bf16),
            jax.ShapeDtypeStruct((8, D), f32),
        ),
        in_specs=[hb] * 3 + [vm] * 4 + [hb] * 6,
        out_specs=(hb, hb, hb, hb, vm),
        scratch_shapes=scratch,
        compiler_params=pltpu.CompilerParams(
            collective_id=1, has_side_effects=True, vmem_limit_bytes=64 * 2**20 - 2**17
        ),
    )(
        tokens, out_grad, gate_weight, region_mask, attn_gain, ffn_gain, gate_bias,
        self_qkv.reshape(QR, D), cross_qkv.reshape(QR, D), self_out, cross_out, up_weight, down_weight,
    )
    out, tg, fin, gout, vec = mid_out
    total = 4 * CH + D
    wide = lambda *shape: jax.ShapeDtypeStruct(shape, f32)
    res = pl.pallas_call(
        widen_kernel,
        out_shape=(
            jax.ShapeDtypeStruct((R, D), bf16), jax.ShapeDtypeStruct((R, D), bf16),
            wide(D), wide(QR, D), wide(QR, D), wide(F, D), wide(F, D), wide(D, D), wide(D), wide(D),
            wide(CH, D), wide(CH, D),
        ),
        in_specs=[hb] * 4 + [vm],
        out_specs=(hb, hb, vm, hb, hb, hb, hb, hb, vm, vm, hb, hb),
        scratch_shapes=[
            pltpu.VMEM((total, D), bf16), pltpu.VMEM((total, D), f32), pltpu.VMEM((2, R, D), bf16),
            dma((5,)), dma((5, 2)), dma((4,)),
        ],
        compiler_params=pltpu.CompilerParams(vmem_limit_bytes=60 * 2**20),
    )(out, tg, fin, gout.reshape(D, D), vec)
    out, tg, again, sq, cq, so, co, gw, gb, fg, up, dn = res
    grads = (again, sq.reshape(3, F, D), cq.reshape(3, F, D), so, co, gw, gb, fg, up, dn)
    if outer > 1:
        first = (lax.axis_index("dp") % 8 == 0).astype(f32)
        grads = lax.psum(tuple(g * first for g in grads), "dp")
    return (out, tg) + tuple(grads)


def solution(mesh):
    rows = P(("dp", "mp"), None)
    weights = (P(), P(None, "mp", None), P(None, "mp", None), P("mp", None), P("mp", None), P(), P(), P(), P(None, "mp"), P("mp", None))
    return jax.shard_map(
        functools.partial(body, outer=mesh.shape["dp"] // 8),
        mesh=mesh,
        in_specs=(rows, P("dp", None)) + weights + (rows,),
        out_specs=(rows, rows) + weights,
        check_vma=False,
    )
```

```python
import functools

import jax
import jax.numpy as jnp
from jax import lax
from jax.experimental import pallas as pl
from jax.experimental.pallas import tpu as pltpu
from jax.sharding import PartitionSpec as P

HEAD = 64
LANG = 96
SLOTS = 128
EPS = 1e-5
NEG = -1e30
GC = 0.7978845608028654
GK = 0.044715
f32 = jnp.float32
bf16 = jnp.bfloat16
MESH = pl.DeviceIdType.MESH

AFTER = {
    "norm": (("agp", 0),),
    "A0q": (("agp", 1),),
    "A0p1": (("agp", 2),),
    "A0p2": (("agp", 3), ("zw", 0, 1), ("zw", 0, 2), ("ag2", 0), ("ag1", 1), ("zw", 0, 3),),
    "gate": (("zs", 1), ("ag2", 1), ("ag3", 0),),
    "A1p0": (("zw", 1, 1),),
    "A1p1": (("ag1", 2), ("ag3", 1), ("zw", 1, 2), ("ag1", 3), ("ag2", 2),),
    "A1p3": (("zw", 1, 3),),
    "A2p2": (("ag1", 4),),
    "A2p3": (("ag2", 3),),
    "A2s": (("ag3", 2), ("ag1", 5), ("ag2", 4),),
    "F0a": (("ag3", 3),),
    "F0c": (("ag2", 5), ("rs0", 0),),
    "F1b": (("ag3", 4),),
    "F1c": (("rs0", 1), ("rs1", 0),),
    "F2a": (("rs1", 1), ("ag3", 5),),
    "F2c": (("rs0", 2),),
    "F3a": (("rs2", 0), ("rs1", 2),),
    "F3c": (("rs0", 3), ("rs2", 1),),
    "mid2": (("rs1", 3),),
    "outmm": (("rs0", 4),),
    "B0o": (("rs2", 2),),
    "B0p1": (("rs1", 4), ("g", 0),),
    "B0p2": (("zfa", 0, 2),),
    "B0g": (("g", 1), ("rs0", 5), ("rs2", 3),),
    "B1o": (("rs3", 0),),
    "B1p0": (("rs3", 1), ("rs1", 5), ("rs3", 2),),
    "B1p1": (("zfa", 0, 3),),
    "B1g": (("rs0", 6), ("rs2", 4),),
    "B1h": (("rs3", 3), ("rs1", 6), ("rs2", 5), ("g", 2),),
    "B2p1": (("zza", 0, 2),),
    "B2g": (("rs0", 7), ("rs1", "z0"), ("rs3", 4),),
    "B2h": (("rs1", 7),),
    "B3o": (("zza", 0, 3),),
    "B3p0": (("g", 3), ("rs3", 5), ("rs2", 6), ("rs2", "z0"),),
    "B3g": (("rs0", 8), ("rs2", 7), ("zza", 1, 3), ("g", 4), ("rs3", 6), ("rs1", 8), ("zza", 2, 3), ("rs3", "z0"), ("fin0", 0),),
    "tail": (("rs3", 7), ("zza", 1, 2), ("v", 0), ("g", 5), ("rs2", 8), ("zza", 2, 2), ("v", 1), ("fin1", 0), ("rs3", 8), ("fin0", 2), ("v", 2), ("g", 6), ("fin0", 1), ("fin1", 2), ("v", 3), ("g", 7), ("fin1", 1), ("fin2", 0), ("fin2", 2), ("fin2", 1), ("v", 4), ("fin3", 0), ("g", 8), ("fin3", 2), ("fin3", 1),),
}


def mm(lhs, rhs, form):
    dims = {"nn": ((1,), (0,)), "nt": ((1,), (1,)), "tn": ((0,), (0,))}[form]
    return lax.dot_general(lhs, rhs, (dims, ((), ())), preferred_element_type=f32)


def blk(start, size, align):
    return pl.ds(pl.multiple_of(start, align), size)


def standardize(rows):
    centre = jnp.mean(rows, axis=1, keepdims=True)
    offset = rows - centre
    spread = jnp.mean(offset * offset, axis=1, keepdims=True)
    inv = lax.rsqrt(spread + EPS)
    return offset * inv, inv


def layer_kernel(
    x_hbm, og_hbm, gate_hbm, marks_ref, again_ref, fgain_ref, gbias_ref,
    sq_ref, cq_ref, so_ref, co_ref, up_ref, dn_ref,
    out_hbm, tg_hbm, fin, gout, vec_ref,
    buf, crecv, p1a, p1b, p2a, p2b, cr_o, p1a_o, p1b_o, p2a_o, p2b_o,
    z_f, z_o, z_q, e_f, e_o, e_q, zr, ze, p1a_z, p1b_z, p2a_z, p2b_z, gg, gcr, gxr, gyr, gzr, vs, vr, vz,
    og_ref, bias_ref, h, qkv, o, lse, sc, aa, mid, h2, acc, gh, eb, wb,
    io, loc, ap_s, ap_r, a0_s, a0_r, az_s, az_r, a1_s, a1_r, a2_s, a2_r, ac_s, ac_r,
    rc_s, rc_r, r1_s, r1_r, r2_s, r2_r, rz_s, rz_r, re_r, zf_s, zf_r, zfe_r,
    f1_s, f1_r, f2_s, f2_r, fc_s, fc_r, fl,
    g_s, g_r, gz_s, gz_r, ga_s, ga_r, gl, v_s, v_r, vz_s, vz_r,
):
    R, D = x_hbm.shape
    gate_ref = buf.at[2, 0, 0]
    x_ref = eb
    gz = og_ref
    CH = buf.shape[3]
    XH, YH = CH // 2, D // 2
    ZF = zr.shape[2]
    AR = XH // 2
    QR = sq_ref.shape[0]
    F = QR // 3
    heads = F // HEAD
    pages = R // SLOTS
    GX = gg.shape[2] // 2

    dp = lax.axis_index("dp")
    z = lax.axis_index("mp")
    c = dp % 2
    x = (dp // 2) % 2
    y = (dp // 4) % 2
    s = z // 2
    ismid = (z + s) % 2
    dev_c = (dp + 1 - 2 * c, z)
    dev_x = (dp + 2 - 4 * x, z)
    dev_y = (dp + 4 - 8 * y, z)

    def zof(slot):
        b0, b1 = slot % 2, slot // 2
        near = (1 - b0) * z + b0 * (4 * s + 1 - z)
        far = (1 - b0) * (2 - s) + b0 * (3 - 3 * s)
        return (1 - b1) * near + b1 * far

    def seen_as(slot):
        is1 = 1 - slot // 2
        return is1 + (1 - is1) * (3 - ismid)

    def remote(src, dst, ss, rs, dev):
        return pltpu.make_async_remote_copy(
            src_ref=src, dst_ref=dst, send_sem=ss, recv_sem=rs, device_id=dev, device_id_type=MESH
        )

    bar = pltpu.get_barrier_semaphore()
    partners = (dev_c, dev_x, dev_y, (dp, zof(1)), (dp, zof(2)), (dp, zof(3)))
    for dev in partners:
        pl.semaphore_signal(bar, inc=1, device_id=dev, device_id_type=MESH)

    ins = [
        pltpu.make_async_copy(src, dst, io.at[i])
        for i, (src, dst) in enumerate(((x_hbm, x_ref), (gate_hbm, gate_ref), (og_hbm, og_ref)))
    ]
    ins[0].start()
    local = []
    for i, (src, g, cc, r0) in enumerate(
        (
            (sq_ref, 0, 0, 0), (so_ref, 0, 0, QR), (cq_ref, 0, 1, 0), (co_ref, 0, 1, QR),
            (up_ref, 1, 0, 0), (dn_ref, 1, 1, 0),
        )
    ):
        cp = pltpu.make_async_copy(src, buf.at[g, cc, z, pl.ds(r0, src.shape[0]), :], loc.at[i])
        cp.start()
        local.append(cp)
    ins[1].start()
    ins[2].start()

    def wpart(g, cc, zz, r0, nr, c0, nc):
        return buf.at[g, cc, zz, blk(r0, nr, 16), blk(c0, nc, 128)]

    def wquarter(g, zz):
        return wpart(g, c, zz, XH * x, XH, YH * y, YH)

    def z_copy(g, zz, slot_to, sidx, rslot):
        ref = wquarter(g, zz)
        return remote(ref, ref, az_s.at[g, sidx], az_r.at[g, rslot], (dp, zof(slot_to)))

    PIECES = 4

    def piece(zz, q):
        n = AR // PIECES
        out = []
        for i in range(2):
            ref = wpart(0, c, zz, XH * x + AR * i + n * q, n, YH * y, YH)
            out.append(remote(ref, ref, ap_s.at[q, i], ap_r.at[q, i], (dp, zof(1))))
        return out

    def piece_p1(zz, xx, yy, q):
        n = AR // PIECES
        ra = wpart(0, c, zz, XH * xx + n * q, n, YH * y, YH)
        rb = wpart(0, c, zz, XH * x + AR + n * q, n, YH * yy, YH)
        return (
            remote(ra, ra, a0_s.at[q, 0], a0_r.at[q, 0], dev_x), remote(rb, rb, a0_s.at[q, 1], a0_r.at[q, 1], dev_y)
        )

    def ag_piece(q):
        for cp in piece(zof(1), q):
            cp.wait_recv()
        for cp in piece_p1(zof(1), x, y, q):
            cp.start()

    def ag_zsend(g):
        if g == 0:
            for q in range(PIECES):
                for cp in piece(z, q):
                    cp.start()
        else:
            z_copy(g, z, 1, 0, 1).start()

        @pl.when(ismid == 1)
        def _():
            z_copy(g, z, 2, 1, 2).start()

    def ag_zsend_wait(g):
        if g == 0:
            for q in range(PIECES):
                for cp in piece(z, q):
                    cp.wait_send()
        else:
            z_copy(g, z, 1, 0, 1).wait_send()

        @pl.when(ismid == 1)
        def _():
            for i in range(1, 5):
                z_copy(g, z, 1, i, 1).wait_send()

    def ag_p1(g, j):
        zz = zof(j)
        ra = wpart(g, c, zz, XH * x, AR, YH * y, YH)
        rb = wpart(g, c, zz, XH * x + AR, AR, YH * y, YH)
        ia = wpart(g, c, zz, XH * (1 - x), AR, YH * y, YH)
        ib = wpart(g, c, zz, XH * x + AR, AR, YH * (1 - y), YH)
        return (
            (remote(ra, ra, a1_s.at[g, j, 0], a1_r.at[g, j, 0], dev_x),
             remote(rb, rb, a1_s.at[g, j, 1], a1_r.at[g, j, 1], dev_y)),
            (remote(ia, ia, a1_s.at[g, j, 0], a1_r.at[g, j, 0], dev_x),
             remote(ib, ib, a1_s.at[g, j, 1], a1_r.at[g, j, 1], dev_y)),
        )

    def ag_p2(g, j):
        zz = zof(j)
        outs, ins = [], []
        for xx in range(2):
            ra = wpart(g, c, zz, XH * xx, AR, YH * y, YH)
            ia = wpart(g, c, zz, XH * xx, AR, YH * (1 - y), YH)
            outs.append(remote(ra, ra, a2_s.at[g, j, xx], a2_r.at[g, j, xx], dev_y))
            ins.append(remote(ia, ia, a2_s.at[g, j, xx], a2_r.at[g, j, xx], dev_y))
        rb = wpart(g, c, zz, XH * x + AR, AR, 0, D)
        ib = wpart(g, c, zz, XH * (1 - x) + AR, AR, 0, D)
        outs.append(remote(rb, rb, a2_s.at[g, j, 2], a2_r.at[g, j, 2], dev_x))
        ins.append(remote(ib, ib, a2_s.at[g, j, 2], a2_r.at[g, j, 2], dev_x))
        return outs, ins

    def ag_c(g, j):
        zz = zof(j)
        mine, theirs = buf.at[g, c, zz], buf.at[g, 1 - c, zz]
        return (
            remote(mine, mine, ac_s.at[g, j], ac_r.at[g, j], dev_c),
            remote(theirs, theirs, ac_s.at[g, j], ac_r.at[g, j], dev_c),
        )

    def ag_forward(g, j):
        @pl.when(ismid == 1)
        def _():
            if g == 1 or j > 1:
                z_copy(g, zof(j), 1, 0, j).wait_recv()
            if j == 1:
                z_copy(g, zof(1), 2, 2, 3).start()
            else:
                z_copy(g, zof(j), 1, j + 1, j).start()

    def ag_1(t):
        g, j = t // 3, t % 3 + 1

        @pl.when(ismid == 0)
        def _():
            z_copy(g, zof(j), 1, 0, j).wait_recv()

        for cp in ag_p1(g, j)[0]:
            cp.start()

    def ag_2(t):
        g, j = t // 3, t % 3 + 1
        if t == 0:
            outs = [cp for q in range(PIECES) for cp in piece_p1(zof(1), x, y, q)]
            arrivals = [cp for q in range(PIECES) for cp in piece_p1(zof(1), 1 - x, 1 - y, q)]
        else:
            outs, arrivals = ag_p1(g, j)
        for cp in arrivals:
            cp.wait_recv()
        for cp in ag_p2(g, j)[0]:
            cp.start()
        for cp in outs:
            cp.wait_send()

    def ag_3(t):
        g, j = t // 3, t % 3 + 1
        outs, arrivals = ag_p2(g, j)
        for cp in arrivals:
            cp.wait_recv()
        ag_c(g, j)[0].start()
        for cp in outs:
            cp.wait_send()

    def ag_done(g, j):
        mine, theirs = ag_c(g, j)
        theirs.wait_recv()
        mine.wait_send()

    def add_rows(dst, dst_idx, r0, nr, c0, nc, src, src_idx):
        step = next(n for n in (64, 48) if nr % n == 0)

        @pl.loop(0, nr // step)
        def _(i):
            rows = blk(r0 + i * step, step, 16)
            cols = blk(c0, nc, 128)
            d = dst[(*dst_idx, rows, cols)].astype(f32)
            t = src[(*src_idx, blk(i * step, step, 16), slice(None))].astype(f32)
            dst[(*dst_idx, rows, cols)] = (d + t).astype(bf16)

    def single(b, nr, ha, kq, slot, sem):
        def reg(cc, r0, n, c0, w):
            return buf.at[b, cc, kq, blk(r0, n, 16), blk(c0, w, 128)]

        def add(r0, n, c0, w, src, idx):
            add_rows(buf, (b, c, kq), r0, n, c0, w, src, idx)

        return dict(
            reg=reg, add=add, nr=nr, ha=ha, off=0, sem=sem,
            cr=(crecv, (slot,), pl.ds(0, nr)), a1=(p1a, (slot,), pl.ds(0, ha)),
            b1=[(p1b, (slot, xx), pl.ds(0, ha)) for xx in range(2)],
            a2=(p2a, (slot,), pl.ds(0, ha)), b2=(p2b, (slot,), pl.ds(0, ha)),
        )

    def k_ffn(k):
        return single(2, CH, (XH - ZF) // 2, k, k, k)

    def k_first():
        kd = k_ffn(0)
        every = slice(None)
        kd.update(
            off=XH - ZF, ha=ZF // 2, sem=9, a1=(p1a_z, (), every), b1=[(p1b_z, (xx,), every) for xx in range(2)],
            a2=(p2a_z, (), every), b2=(p2b_z, (), every),
        )
        return kd

    def k_qkv(i):
        return single(1, QR, QR // 4, 3 - i, i, 5 + i)

    def k_out():
        def reg(cc, r0, n, c0, w):
            return buf.at[1, cc, :, blk(QR + r0, n, 16), blk(c0, w, 128)]

        def add(r0, n, c0, w, src, idx):
            for q in range(4):
                add_rows(buf, (1, c, q), QR + r0, n, c0, w, src, (*idx, q))

        every = slice(None)
        return dict(
            reg=reg, add=add, nr=F, ha=F // 4, off=0, sem=4,
            cr=(cr_o, (), every), a1=(p1a_o, (), every), b1=[(p1b_o, (xx,), every) for xx in range(2)],
            a2=(p2a_o, (), every), b2=(p2b_o, (), every),
        )

    def land(part):
        ref, idx, rows = part
        return ref.at[(*idx, rows)]

    def rs_c(kd):
        n = kd["sem"]
        return remote(kd["reg"](1 - c, 0, kd["nr"], 0, D), land(kd["cr"]), rc_s.at[n], rc_r.at[n], dev_c)

    def rs_p1(kd):
        n, half, ha, reg, off = kd["sem"], kd["nr"] // 2, kd["ha"], kd["reg"], kd["off"]
        cps = [remote(reg(c, half * (1 - x) + off, ha, 0, D), land(kd["a1"]), r1_s.at[n, 0], r1_r.at[n, 0], dev_x)]
        for xx in range(2):
            src = reg(c, half * xx + off + ha, ha, YH * (1 - y), YH)
            cps.append(remote(src, land(kd["b1"][xx]), r1_s.at[n, 1 + xx], r1_r.at[n, 1 + xx], dev_y))
        return cps

    def rs_p2(kd):
        n, half, ha, reg, off = kd["sem"], kd["nr"] // 2, kd["ha"], kd["reg"], kd["off"]
        return [
            remote(reg(c, half * x + off, ha, YH * (1 - y), YH), land(kd["a2"]), r2_s.at[n, 0], r2_r.at[n, 0], dev_y),
            remote(
                reg(c, half * (1 - x) + off + ha, ha, YH * y, YH), land(kd["b2"]), r2_s.at[n, 1], r2_r.at[n, 1], dev_x
            ),
        ]

    def rs_0(kd):
        rs_c(kd).start()

    def rs_1(kd, between=None):
        cp = rs_c(kd)
        cp.wait_recv()
        kd["add"](0, kd["nr"], 0, D, kd["cr"][0], kd["cr"][1])
        if between is not None:
            between()
        for q in rs_p1(kd):
            q.start()
        cp.wait_send()

    def rs_2(kd):
        half, ha, off = kd["nr"] // 2, kd["ha"], kd["off"]
        cps = rs_p1(kd)
        for q in cps:
            q.wait_recv()
        kd["add"](half * x + off, ha, 0, D, kd["a1"][0], kd["a1"][1])
        for xx in range(2):
            kd["add"](half * xx + off + ha, ha, YH * y, YH, kd["b1"][xx][0], kd["b1"][xx][1])
        for q in rs_p2(kd):
            q.start()
        for q in cps:
            q.wait_send()

    def rs_3(kd, after=None):
        half, ha, off = kd["nr"] // 2, kd["ha"], kd["off"]
        cps = rs_p2(kd)
        for q in cps:
            q.wait_recv()
        kd["add"](half * x + off, ha, YH * y, YH, kd["a2"][0], kd["a2"][1])
        kd["add"](half * x + off + ha, ha, YH * y, YH, kd["b2"][0], kd["b2"][1])
        if after is not None:
            after()
        for q in cps:
            q.wait_send()

    groups = (
        (2, 0, XH, XH - ZF, z_f, e_f),
        (1, QR, F // 2, F // 2, z_o, e_o),
        (1, 0, QR // 2, QR // 2, z_q, e_q),
    )

    def z_part(gi, k):
        b, r0, half, n = groups[gi][:4]
        return buf.at[b, c, k, blk(r0 + half * x, n, 16), blk(YH * y, YH, 128)]

    def z_out(gi, k):
        return remote(z_part(gi, k), groups[gi][4].at[0 if k == 1 else 1], rz_s.at[gi, k], rz_r.at[gi, 0 if k == 1 else 1], (dp, zof(k)))

    def z_hop(gi, k):
        return remote(z_part(gi, k), groups[gi][5].at[k - 2], rz_s.at[gi, k], re_r.at[gi, k - 2], (dp, zof(1)))

    def z_start(gi, k):
        if k == 1:
            z_out(gi, 1).start()
        if k > 1:

            @pl.when(ismid == 0)
            def _():
                z_hop(gi, k).start()

    def z_join(gi, k):
        b, r0, half, n, _to, mid_buf = groups[gi]

        @pl.when(ismid == 1)
        def _():
            z_hop(gi, k).wait_recv()
            add_rows(buf, (b, c, k), r0 + half * x, n, YH * y, YH, mid_buf, (k - 2,))
            z_out(gi, k).start()

    def zf_rows(k, xx):
        return buf.at[2, c, k, pl.ds(XH * (xx + 1) - ZF, ZF), :]

    def zf_out(k, xx):
        to = 0 if k == 1 else 1
        return remote(zf_rows(k, xx), zr.at[to, xx], zf_s.at[k, xx], zf_r.at[to, xx], (dp, zof(k)))

    def zf_hop(k, xx):
        return remote(zf_rows(k, xx), ze.at[k - 2, xx], zf_s.at[k, xx], zfe_r.at[k - 2, xx], (dp, zof(1)))

    def zf_start(k):
        if k == 1:
            for xx in range(2):
                zf_out(1, xx).start()
        if k > 1:

            @pl.when(ismid == 0)
            def _():
                for xx in range(2):
                    zf_hop(k, xx).start()

    def zf_join(_gi, k):
        @pl.when(ismid == 1)
        def _():
            for xx in range(2):
                zf_hop(k, xx).wait_recv()
                add_rows(buf, (2, c, k), XH * (xx + 1) - ZF, ZF, 0, D, ze, (k - 2, xx))
                zf_out(k, xx).start()

    def zf_sum():
        for xx in range(2):
            for slot in range(2):
                zf_out(1 + slot, xx).wait_recv()
                add_rows(buf, (2, c, 0), XH * (xx + 1) - ZF, ZF, 0, D, zr, (slot, xx))
        for q in rs_p1(k_first()):
            q.start()

    def fin_part(gi, r, n, c0, w):
        r0 = groups[gi][1]
        return fin.at[0 if gi == 0 else 1, c, blk(r0 + r, n, 16), blk(c0, w, 128)]

    def own_part(gi, r, n):
        b, r0 = groups[gi][:2]
        return buf.at[b, c, 0, blk(r0 + r, n, 16), blk(YH * y, YH, 128)]

    def fin_p1(gi):
        half = groups[gi][2]
        q = half // 2
        return [
            remote(
                own_part(gi, half * x + q * i, q), fin_part(gi, half * x + q * i, q, YH * y, YH),
                f1_s.at[gi, i], f1_r.at[gi, i], dev,
            )
            for i, dev in enumerate((dev_x, dev_y))
        ]

    def fin_local(gi):
        half = groups[gi][2]
        return pltpu.make_async_copy(
            own_part(gi, half * x, half), fin_part(gi, half * x, half, YH * y, YH), fl.at[gi]
        )

    def fin_p2(gi):
        half = groups[gi][2]
        q = half // 2
        cps = []
        for xx in range(2):
            ref = fin_part(gi, half * xx, q, YH * y, YH)
            cps.append(remote(ref, ref, f2_s.at[gi, xx], f2_r.at[gi, xx], dev_y))
        ref = fin_part(gi, half * x + q, q, 0, D)
        cps.append(remote(ref, ref, f2_s.at[gi, 2], f2_r.at[gi, 2], dev_x))
        return cps

    def fin_c(gi):
        ref = fin_part(gi, 0, 2 * groups[gi][2], 0, D)
        return remote(ref, ref, fc_s.at[gi], fc_r.at[gi], dev_c)

    def fin_0(gi):
        b, r0, half, n, part, _mid = groups[gi]
        for k in (1, 2):
            z_out(gi, k).wait_recv()
        for slot in range(2):
            add_rows(buf, (b, c, 0), r0 + half * x, n, YH * y, YH, part, (slot,))
        for q in fin_p1(gi):
            q.start()
        fin_local(gi).start()
        for k in (1, 2, 3):
            z_out(gi, k).wait_send()
            if gi == 0:
                for xx in range(2):
                    zf_out(k, xx).wait_send()

    def fin_1(gi):
        for q in fin_p1(gi):
            q.wait_recv()
        fin_local(gi).wait()
        for q in fin_p2(gi):
            q.start()
        for q in fin_p1(gi):
            q.wait_send()

    def fin_2(gi):
        for q in fin_p2(gi):
            q.wait_recv()
        fin_c(gi).start()
        for q in fin_p2(gi):
            q.wait_send()

    def fin_3(gi):
        fin_c(gi).wait_recv()
        fin_c(gi).wait_send()

    def g_copy(i):
        xs, xo = blk(GX * x, GX, 16), blk(GX * (1 - x), GX, 16)
        ys, yo = blk(YH * y, YH, 128), blk(YH * (1 - y), YH, 128)
        src, dst, dev = {
            0: lambda: (gg.at[:, 1 - c], gcr, dev_c),
            1: lambda: (gg.at[:, c, xo, :], gxr, dev_x),
            2: lambda: (gg.at[:, c, xs, yo], gyr, dev_y),
            3: lambda: (gout.at[:, c, xs, ys], gout.at[:, c, xs, ys], dev_y),
            4: lambda: (gout.at[:, c, xs, :], gout.at[:, c, xs, :], dev_x),
            5: lambda: (gout.at[:, c], gout.at[:, c], dev_c),
        }[i]()
        return remote(src, dst, g_s.at[i], g_r.at[i], dev)

    def g_z(slot, rslot):
        src = gg.at[zof(slot), c, blk(GX * x, GX, 16), blk(YH * y, YH, 128)]
        return remote(src, gzr.at[rslot - 1], gz_s.at[slot], gz_r.at[rslot], (dp, zof(slot)))

    def g_za(slot, rslot):
        src = gg.at[z, c, blk(GX * x, GX, 16), blk(YH * y, YH, 128)]
        dst = gout.at[z, c, blk(GX * x, GX, 16), blk(YH * y, YH, 128)]
        return remote(src, dst, ga_s.at[slot], ga_r.at[rslot], (dp, zof(slot)))

    def g_local():
        src = gg.at[z, c, blk(GX * x, GX, 16), blk(YH * y, YH, 128)]
        dst = gout.at[z, c, blk(GX * x, GX, 16), blk(YH * y, YH, 128)]
        return pltpu.make_async_copy(src, dst, gl.at[0])

    def g_step(i):
        xs, ys = blk(GX * x, GX, 16), blk(YH * y, YH, 128)
        if i == 0:
            g_copy(0).start()
        if i == 1:
            g_copy(0).wait_recv()
            for q in range(4):
                add_rows(gg, (q, c), 0, 2 * GX, 0, D, gcr, (q,))
            g_copy(1).start()
            g_copy(0).wait_send()
        if i == 2:
            g_copy(1).wait_recv()
            for q in range(4):
                add_rows(gg, (q, c), GX * x, GX, 0, D, gxr, (q,))
            g_copy(2).start()
            g_copy(1).wait_send()
        if i == 3:
            g_copy(2).wait_recv()
            for q in range(4):
                add_rows(gg, (q, c), GX * x, GX, YH * y, YH, gyr, (q,))
            for slot in range(1, 4):
                g_z(slot, seen_as(slot)).start()
            g_copy(2).wait_send()
        if i == 4:
            for slot in range(1, 4):
                g_z(slot, slot).wait_recv()
            t = gg[z, c, xs, ys].astype(f32)
            for slot in range(3):
                t = t + gzr[slot].astype(f32)
            gg[z, c, xs, ys] = t.astype(bf16)
            g_local().start()
            for slot in range(1, 4):
                g_za(slot, seen_as(slot)).start()
            for slot in range(1, 4):
                g_z(slot, slot).wait_send()
        if i == 5:
            for slot in range(1, 4):
                g_za(slot, slot).wait_recv()
            g_local().wait()
            g_copy(3).start()
            for slot in range(1, 4):
                g_za(slot, slot).wait_send()
        if i == 6:
            g_copy(3).wait_recv()
            g_copy(4).start()
            g_copy(3).wait_send()
        if i == 7:
            g_copy(4).wait_recv()
            g_copy(5).start()
            g_copy(4).wait_send()
        if i == 8:
            g_copy(5).wait_recv()
            g_copy(5).wait_send()

    def v_copy(i):
        return remote(vs.at[i], vr.at[i], v_s.at[i], v_r.at[i], (dev_c, dev_x, dev_y)[i])

    def v_z(slot, zz_dst, rslot):
        return remote(vz.at[z], vz.at[zz_dst], vz_s.at[slot], vz_r.at[rslot], (dp, zof(slot)))

    def v_step(i):
        if i == 0:
            v_copy(0).start()
        if i in (1, 2):
            v_copy(i - 1).wait_recv()
            vs[i] = vs[i - 1] + vr[i - 1]
            v_copy(i).start()
            v_copy(i - 1).wait_send()
        if i == 3:
            v_copy(2).wait_recv()
            vz[z] = vs[2] + vr[2]
            for slot in range(1, 4):
                v_z(slot, z, seen_as(slot)).start()
            v_copy(2).wait_send()
        if i == 4:
            for slot in range(1, 4):
                v_z(slot, z, slot).wait_recv()
            vec_ref[...] = (vz[0] + vz[1]) + (vz[2] + vz[3])
            for slot in range(1, 4):
                v_z(slot, z, slot).wait_send()

    def kind(n):
        if n == "z0":
            return k_first()
        return k_ffn(n) if n < 4 else k_out() if n == 4 else k_qkv(n - 5)

    def first(n):
        if n == "z0":
            zf_sum()
        else:
            rs_1(kind(n), lambda: zf_start(n) if n < 4 else None)

    def third(n):
        if n == "z0":
            rs_3(kind(n))
        elif n < 4:
            rs_3(kind(n), lambda: z_start(0, n))
        elif n == 4:
            rs_3(kind(n), lambda: [z_start(1, q) for q in range(1, 4)])
        else:
            rs_3(kind(n), lambda: z_start(2, 8 - n))

    events = {
        "zs": ag_zsend, "zw": ag_forward, "agp": ag_piece, "ag1": ag_1, "ag2": ag_2, "ag3": ag_3,
        "rs0": lambda n: rs_0(kind(n)), "rs1": first, "rs2": lambda n: rs_2(kind(n)), "rs3": third,
        "zza": z_join, "zfa": zf_join, "g": g_step, "v": v_step, "fin0": fin_0, "fin1": fin_1, "fin2": fin_2, "fin3": fin_3,
    }

    def after(name, k=None, p=None):
        if k is None:
            for ev in AFTER.get(name, ()):
                events[ev[0]](*ev[1:])
            return
        for kk in range(4):
            for pp in range(1 if p is None else 4):
                found = AFTER.get(name[0] + str(kk) + name[1:] + ("" if p is None else str(pp)), ())
                if found:

                    @pl.when((k == kk) if p is None else (k == kk) & (p == pp))
                    def _():
                        for ev in found:
                            events[ev[0]](*ev[1:])

    TR = 128
    again = again_ref[...].astype(f32).reshape(1, D)
    fgain = fgain_ref[...].astype(f32).reshape(1, D)
    gbias = gbias_ref[...].astype(f32).reshape(1, D)

    pl.semaphore_wait(bar, 6)
    for cp in local[:4]:
        cp.wait()
    ag_zsend(0)

    after("start")

    key_id = lax.broadcasted_iota(jnp.int32, (SLOTS, SLOTS), 0)
    query_id = lax.broadcasted_iota(jnp.int32, (SLOTS, SLOTS), 1)
    key_kind = jnp.where(key_id < LANG, 1, 0)
    query_kind = jnp.where(query_id < LANG, 1, 0)
    for p in range(pages):
        row = marks_ref[pl.ds(pages * z + p, 1), :]
        real = jnp.broadcast_to(jnp.where(row > 0, 0.0, NEG), (SLOTS, SLOTS)).T
        bias_ref[0, p] = jnp.where(key_kind == query_kind, real, NEG).astype(bf16)
        bias_ref[1, p] = jnp.where(key_kind == query_kind, NEG, real).astype(bf16)

    ins[0].wait()

    @pl.loop(0, R // TR)
    def _(i):
        rows = blk(i * TR, TR, 16)
        u, _inv = standardize(x_ref[rows, :].astype(f32))
        h[rows, :] = (u * again).astype(bf16)
        sc[rows, :] = jnp.zeros((TR, D), f32)
        mid[rows, :] = jnp.zeros((TR, D), f32)
        gh[rows, :] = jnp.zeros((TR, D), f32)

    vs[...] = jnp.zeros_like(vs)
    for cp in local[4:] + ins[1:]:
        cp.wait()
    after("norm")

    @pl.loop(0, 4)
    def _(k):
        zz = zof(k)

        @pl.when(k > 0)
        def _():
            ag_done(0, k)

        for at in range(2):
            qkv[at, k] = mm(buf[0, at, zz, 0:QR, :], h[...], "nt").astype(bf16)
        after("Aq", k)

        @pl.loop(0, pages)
        def _(p):
            cols = blk(p * SLOTS, SLOTS, 128)
            units = [(at, hh) for at in range(2) for hh in range(heads)]
            scores = []
            for at, hh in units:
                qt = qkv[at, k, HEAD * hh : HEAD * (hh + 1), cols]
                kt = qkv[at, k, F + HEAD * hh : F + HEAD * (hh + 1), cols]
                scores.append(mm(kt, qt, "tn"))
            probs = []
            for (at, hh), st in zip(units, scores):
                st = st * HEAD ** (-0.5) + bias_ref[at, p].astype(f32)
                top = jnp.max(st, axis=0, keepdims=True)
                ex = jnp.exp(st - top)
                tot = jnp.sum(ex, axis=0, keepdims=True)
                probs.append((ex * (1.0 / tot)).astype(bf16))
                lse[at, k, hh : hh + 1, cols] = top + jnp.log(tot)
            for (at, hh), pt in zip(units, probs):
                vt = qkv[at, k, 2 * F + HEAD * hh : 2 * F + HEAD * (hh + 1), cols]
                o[at, k, HEAD * hh : HEAD * (hh + 1), cols] = mm(vt, pt, "nn").astype(bf16)
            after("Ap", k, p)

        @pl.loop(0, 2)
        def _(p):
            cols = blk(p * 256, 256, 128)
            for at, dst in ((0, sc), (1, mid)):
                dst[cols, :] += mm(o[at, k, :, cols], buf[0, at, zz, QR:CH, :], "tn")

        after("As", k)

        @pl.when(k == 0)
        def _():
            @pl.loop(0, R // 256)
            def _(i):
                rows = blk(i * 256, 256, 16)
                aa[rows, :] = jax.nn.sigmoid(mm(h[rows, :], gate_ref[...], "nn") + gbias)

            after("gate")

    ag_zsend_wait(0)

    @pl.loop(0, R // TR)
    def _(i):
        rows = blk(i * TR, TR, 16)
        a = aa[rows, :]
        sv, cv = sc[rows, :], mid[rows, :]
        mv = x_ref[rows, :].astype(f32) + a * sv + (1.0 - a) * cv
        sc[rows, :] = sv - cv
        mid[rows, :] = mv
        acc[rows, :] = mv
        u, _inv = standardize(mv)
        h2[rows, :] = (u * fgain).astype(bf16)

    after("join")

    @pl.loop(0, 4)
    def _(k):
        zz = zof(k)

        @pl.when(k > 0)
        def _():
            ag_done(1, k)

        MT = 256

        @pl.loop(0, 2 * (R // MT))
        def _(i):
            rows = blk((i // 2) * MT, MT, 16)
            cols = blk((i % 2) * XH, XH, 128)
            w = mm(h2[rows, :], buf[1, 0, zz, :, cols], "nn")
            ge = mm(og_ref[rows, :], buf[1, 1, zz, blk((i % 2) * XH, XH, 16), :], "nt")
            w2 = w * w
            th = jnp.tanh(GC * w * (1.0 + GK * w2))
            half = 0.5 * (1.0 + th)
            eb[rows, cols] = (w * half).astype(bf16)
            dg = half + 0.5 * w * (1.0 - th * th) * (GC * (1.0 + 3.0 * GK * w2))
            wb[rows, cols] = (dg * ge).astype(bf16)

        after("Fa", k)

        @pl.loop(0, R // MT)
        def _(i):
            rows = blk(i * MT, MT, 16)
            acc[rows, :] += mm(eb[rows, :], buf[1, 1, zz], "nn")
            gh[rows, :] += mm(wb[rows, :], buf[1, 0, zz], "nt")

        after("Fb", k)

        @pl.loop(0, CH // 384)
        def _(i):
            cols = blk(i * 384, 384, 128)
            buf[2, 1, k, blk(i * 384, 384, 16), :] = mm(eb[:, cols], og_ref[...], "tn").astype(bf16)
            buf[2, 0, k, blk(i * 384, 384, 16), :] = mm(h2[:, cols], wb[...], "tn").astype(bf16)

        after("Fc", k)

    ag_zsend_wait(1)

    TS = 128
    zero_row = jnp.zeros((1, D), f32)

    def mid_back(i, sums):
        gain_sum, bias_sum = sums
        rows = blk(i * TS, TS, 16)
        h2[rows, :] = acc[rows, :].astype(bf16)
        u, inv = standardize(mid[rows, :])
        gy = gh[rows, :]
        gain_sum = gain_sum + jnp.sum(gy * u, axis=0, keepdims=True)
        sy = gy * fgain
        m1 = jnp.mean(sy, axis=1, keepdims=True)
        m2 = jnp.mean(sy * u, axis=1, keepdims=True)
        gm = og_ref[rows, :].astype(f32) + inv * (sy - m1 - u * m2)
        acc[rows, :] = gm
        a = aa[rows, :]
        eb[rows, :] = (a * gm).astype(bf16)
        wb[rows, :] = ((1.0 - a) * gm).astype(bf16)
        gzv = (gm * sc[rows, :] * a * (1.0 - a)).astype(bf16)
        gz[rows, :] = gzv
        bias_sum = bias_sum + jnp.sum(gzv.astype(f32), axis=0, keepdims=True)
        return gain_sum, bias_sum

    gain_sum, bias_sum = lax.fori_loop(0, R // TS, mid_back, (zero_row, zero_row))
    vs[0, 1:2, :] = bias_sum
    vs[0, 2:3, :] = gain_sum
    out_copy = pltpu.make_async_copy(h2, out_hbm, io.at[3])
    out_copy.start()
    after("mid2")
    gate_again = buf.at[2, 1 - c, 1]
    gate_load = pltpu.make_async_copy(gate_hbm, gate_again, io.at[5])
    gate_load.start()

    for k in range(4):
        for at, gref in ((0, eb), (1, wb)):
            buf[1, at, k, QR:CH, :] = mm(o[at, k], gref[...], "nn").astype(bf16)
    after("outmm")
    for i in range(4):
        t = mm(h[:, F * i : F * (i + 1)], gz[...], "tn").astype(bf16)
        gg[i, 0] = t[: F // 2]
        gg[i, 1] = t[F // 2 :]
    after("ggrad")

    x_again = wb
    x_load = pltpu.make_async_copy(x_hbm, x_again, io.at[6])

    @pl.loop(0, 4)
    def _(i):
        k = 3 - i
        zz = zof(k)
        for at, gref in ((0, eb), (1, wb)):
            o[at, k] = mm(buf[0, at, zz, QR:CH, :], gref[...], "nt").astype(bf16)

        @pl.when(i == 3)
        def _():
            x_load.start()

        after("Bo", i)

        @pl.loop(0, pages)
        def _(p):
            cols = blk(p * SLOTS, SLOTS, 128)
            units = [(at, hh) for at in range(2) for hh in range(heads)]
            for grp in (units,):
                rd = []
                for at, hh in grp:
                    qs = slice(HEAD * hh, HEAD * (hh + 1))
                    ks = slice(F + HEAD * hh, F + HEAD * (hh + 1))
                    vsl = slice(2 * F + HEAD * hh, 2 * F + HEAD * (hh + 1))
                    qt, kt, vt, go = qkv[at, k, qs, cols], qkv[at, k, ks, cols], qkv[at, k, vsl, cols], o[at, k, qs, cols]
                    rd.append((at, hh, qs, ks, vsl, qt, kt, vt, go, mm(kt, qt, "tn"), mm(vt, go, "tn")))
                ps = []
                for at, hh, qs, ks, vsl, qt, kt, vt, go, st, gpt in rd:
                    pt = jnp.exp(st * HEAD ** (-0.5) + bias_ref[at, p].astype(f32) - lse[at, k, hh : hh + 1, cols])
                    pg = pt * gpt
                    gst = (pg - pt * jnp.sum(pg, axis=0, keepdims=True)).astype(bf16)
                    ps.append((pt.astype(bf16), gst))
                for (at, hh, qs, ks, vsl, qt, kt, vt, go, st, gpt), (pb, gst) in zip(rd, ps):
                    qkv[at, k, vsl, cols] = mm(go, pb, "nt").astype(bf16)
                    qkv[at, k, qs, cols] = (mm(kt, gst, "nn") * HEAD ** (-0.5)).astype(bf16)
                    qkv[at, k, ks, cols] = (mm(qt, gst, "nt") * HEAD ** (-0.5)).astype(bf16)
            after("Bp", i, p)

        for at in range(2):
            for q in range(3):
                part = slice(F * q, F * (q + 1))
                buf[1, at, k, part, :] = mm(qkv[at, k, part, :], h[...], "nn").astype(bf16)
        after("Bg", i)

        @pl.loop(0, 2)
        def _(p):
            cols = blk(p * 256, 256, 128)
            t = mm(qkv[0, k, :, cols], buf[0, 0, zz, 0:QR, :], "tn") + mm(qkv[1, k, :, cols], buf[0, 1, zz, 0:QR, :], "tn")

            @pl.when(i == 0)
            def _():
                gh[cols, :] = t

            @pl.when(i > 0)
            def _():
                gh[cols, :] += t

        after("Bh", i)

    gate_load.wait()

    @pl.loop(0, R // 256)
    def _(i):
        rows = blk(i * 256, 256, 16)
        gh[rows, :] += mm(gz[rows, :], gate_again[...], "nt")

    def first_back(i, gain_sum):
        rows = blk(i * TS, TS, 16)
        u, inv = standardize(x_again[rows, :].astype(f32))
        gy = gh[rows, :]
        gain_sum = gain_sum + jnp.sum(gy * u, axis=0, keepdims=True)
        sy = gy * again
        m1 = jnp.mean(sy, axis=1, keepdims=True)
        m2 = jnp.mean(sy * u, axis=1, keepdims=True)
        eb[rows, :] = (acc[rows, :] + inv * (sy - m1 - u * m2)).astype(bf16)
        return gain_sum

    x_load.wait()
    vs[0, 0:1, :] = lax.fori_loop(0, R // TS, first_back, zero_row)
    tg_copy = pltpu.make_async_copy(eb, tg_hbm, io.at[4])
    tg_copy.start()
    after("tail")
    out_copy.wait()
    tg_copy.wait()


def widen_kernel(
    out_in, tg_in, fin, gout, vec_in,
    out_o, tg_o, ag_o, sq_o, cq_o, so_o, co_o, gw_o, gb_o, fg_o, up_o, dn_o,
    narrow, wide, whole, sem_in, sem_out, sem_pass,
):
    F = so_o.shape[0]
    QR = 3 * F
    passes = []
    for i, (src, dst) in enumerate(((out_in, out_o), (tg_in, tg_o))):
        load = pltpu.make_async_copy(src, whole.at[i], sem_pass.at[i])
        passes.append((load, pltpu.make_async_copy(whole.at[i], dst, sem_pass.at[2 + i])))
    CH = 4 * F
    jobs = []
    for i, (src, dsts) in enumerate(
        (
            (gout, ((0, gw_o),)), (fin.at[0, 0], ((0, up_o),)), (fin.at[0, 1], ((0, dn_o),)),
            (fin.at[1, 0], ((0, sq_o), (QR, so_o))), (fin.at[1, 1], ((0, cq_o), (QR, co_o))),
        )
    ):
        load = pltpu.make_async_copy(src, narrow.at[pl.ds(CH * i, CH)], sem_in.at[i])
        saves = [
            pltpu.make_async_copy(wide.at[pl.ds(CH * i + r0, dst.shape[0])], dst, sem_out.at[i, q])
            for q, (r0, dst) in enumerate(dsts)
        ]
        load.start()
        jobs.append((load, saves))
    for load, _ in passes:
        load.start()
    ag_o[...] = vec_in[0, :]
    gb_o[...] = vec_in[1, :]
    fg_o[...] = vec_in[2, :]
    for i, (load, saves) in enumerate(jobs):
        load.wait()

        @pl.loop(0, CH // 64)
        def _(q):
            rows = blk(CH * i + 64 * q, 64, 16)
            wide[rows, :] = narrow[rows, :].astype(f32)

        for cp in saves:
            cp.start()
    for load, save in passes:
        load.wait()
        save.start()
    for _, saves in jobs:
        for cp in saves:
            cp.wait()
    for _, save in passes:
        save.wait()


def body(
    tokens, region_mask, attn_gain, self_qkv, cross_qkv, self_out, cross_out, gate_weight, gate_bias,
    ffn_gain, up_weight, down_weight, out_grad, *, outer,
):
    R, D = tokens.shape
    F = self_out.shape[0]
    QR = 3 * F
    CH = QR + F
    pages = R // SLOTS

    vm = pl.BlockSpec(memory_space=pltpu.VMEM)
    hb = pl.BlockSpec(memory_space=pl.ANY)
    dma = pltpu.SemaphoreType.DMA
    XH, YH, GX, OR, ZF = CH // 2, D // 2, D // 16, F // 4, CH // 6
    scratch = [
        pltpu.VMEM((3, 2, 4, CH, D), bf16),
        pltpu.VMEM((4, CH, D), bf16),
        pltpu.VMEM((4, QR // 4, D), bf16),
        pltpu.VMEM((4, 2, QR // 4, YH), bf16),
        pltpu.VMEM((4, QR // 4, YH), bf16),
        pltpu.VMEM((4, QR // 4, YH), bf16),
        pltpu.VMEM((4, F, D), bf16),
        pltpu.VMEM((4, OR, D), bf16),
        pltpu.VMEM((2, 4, OR, YH), bf16),
        pltpu.VMEM((4, OR, YH), bf16),
        pltpu.VMEM((4, OR, YH), bf16),
        pltpu.VMEM((2, XH - ZF, YH), bf16),
        pltpu.VMEM((2, F // 2, YH), bf16),
        pltpu.VMEM((2, QR // 2, YH), bf16),
        pltpu.VMEM((2, XH - ZF, YH), bf16),
        pltpu.VMEM((2, F // 2, YH), bf16),
        pltpu.VMEM((2, QR // 2, YH), bf16),
        pltpu.VMEM((2, 2, ZF, D), bf16),
        pltpu.VMEM((2, 2, ZF, D), bf16),
        pltpu.VMEM((ZF // 2, D), bf16),
        pltpu.VMEM((2, ZF // 2, YH), bf16),
        pltpu.VMEM((ZF // 2, YH), bf16),
        pltpu.VMEM((ZF // 2, YH), bf16),
        pltpu.VMEM((4, 2, 2 * GX, D), bf16),
        pltpu.VMEM((4, 2 * GX, D), bf16),
        pltpu.VMEM((4, GX, D), bf16),
        pltpu.VMEM((4, GX, YH), bf16),
        pltpu.VMEM((3, GX, YH), bf16),
        pltpu.VMEM((3, 8, D), f32),
        pltpu.VMEM((3, 8, D), f32),
        pltpu.VMEM((4, 8, D), f32),
        pltpu.VMEM((R, D), bf16),
        pltpu.VMEM((2, pages, SLOTS, SLOTS), bf16),
        pltpu.VMEM((R, D), bf16),
        pltpu.VMEM((2, 4, QR, R), bf16),
        pltpu.VMEM((2, 4, F, R), bf16),
        pltpu.VMEM((2, 4, 8, R), f32),
        pltpu.VMEM((R, D), f32),
        pltpu.VMEM((R, D), f32),
        pltpu.VMEM((R, D), f32),
        pltpu.VMEM((R, D), bf16),
        pltpu.VMEM((R, D), f32),
        pltpu.VMEM((R, D), f32),
        pltpu.VMEM((R, D), bf16),
        pltpu.VMEM((R, D), bf16),
        dma((7,)),
        dma((6,)), dma((4, 2)), dma((4, 2)), dma((4, 2)), dma((4, 2)), dma((2, 5)), dma((2, 4)), dma((2, 4, 2)), dma((2, 4, 2)), dma((2, 4, 3)), dma((2, 4, 3)),
        dma((2, 4)), dma((2, 4)),
        dma((9,)), dma((9,)), dma((10, 3)), dma((10, 3)), dma((10, 2)), dma((10, 2)), dma((3, 4)), dma((3, 2)),
        dma((3, 2)), dma((4, 2)), dma((2, 2)), dma((2, 2)),
        dma((3, 2)), dma((3, 2)), dma((3, 3)), dma((3, 3)), dma((3,)), dma((3,)), dma((3,)),
        dma((6,)), dma((6,)), dma((4,)), dma((4,)), dma((4,)), dma((4,)), dma((1,)),
        dma((3,)), dma((3,)), dma((4,)), dma((4,)),
    ]
    mid_out = pl.pallas_call(
        layer_kernel,
        out_shape=(
            jax.ShapeDtypeStruct((R, D), bf16),
            jax.ShapeDtypeStruct((R, D), bf16),
            jax.ShapeDtypeStruct((2, 2, CH, D), bf16),
            jax.ShapeDtypeStruct((4, 2, 2 * GX, D), bf16),
            jax.ShapeDtypeStruct((8, D), f32),
        ),
        in_specs=[hb] * 3 + [vm] * 4 + [hb] * 6,
        out_specs=(hb, hb, hb, hb, vm),
        scratch_shapes=scratch,
        compiler_params=pltpu.CompilerParams(
            collective_id=1, has_side_effects=True, vmem_limit_bytes=64 * 2**20 - 2**17
        ),
    )(
        tokens, out_grad, gate_weight, region_mask, attn_gain, ffn_gain, gate_bias,
        self_qkv.reshape(QR, D), cross_qkv.reshape(QR, D), self_out, cross_out, up_weight, down_weight,
    )
    out, tg, fin, gout, vec = mid_out
    total = 4 * CH + D
    wide = lambda *shape: jax.ShapeDtypeStruct(shape, f32)
    res = pl.pallas_call(
        widen_kernel,
        out_shape=(
            jax.ShapeDtypeStruct((R, D), bf16), jax.ShapeDtypeStruct((R, D), bf16),
            wide(D), wide(QR, D), wide(QR, D), wide(F, D), wide(F, D), wide(D, D), wide(D), wide(D),
            wide(CH, D), wide(CH, D),
        ),
        in_specs=[hb] * 4 + [vm],
        out_specs=(hb, hb, vm, hb, hb, hb, hb, hb, vm, vm, hb, hb),
        scratch_shapes=[
            pltpu.VMEM((total, D), bf16), pltpu.VMEM((total, D), f32), pltpu.VMEM((2, R, D), bf16),
            dma((5,)), dma((5, 2)), dma((4,)),
        ],
        compiler_params=pltpu.CompilerParams(vmem_limit_bytes=60 * 2**20),
    )(out, tg, fin, gout.reshape(D, D), vec)
    out, tg, again, sq, cq, so, co, gw, gb, fg, up, dn = res
    grads = (again, sq.reshape(3, F, D), cq.reshape(3, F, D), so, co, gw, gb, fg, up, dn)
    if outer > 1:
        first = (lax.axis_index("dp") % 8 == 0).astype(f32)
        grads = lax.psum(tuple(g * first for g in grads), "dp")
    return (out, tg) + tuple(grads)


def solution(mesh):
    rows = P(("dp", "mp"), None)
    weights = (P(), P(None, "mp", None), P(None, "mp", None), P("mp", None), P("mp", None), P(), P(), P(), P(None, "mp"), P("mp", None))
    return jax.shard_map(
        functools.partial(body, outer=mesh.shape["dp"] // 8),
        mesh=mesh,
        in_specs=(rows, P("dp", None)) + weights + (rows,),
        out_specs=(rows, rows) + weights,
        check_vma=False,
    )
```

```python
import functools

import jax
import jax.numpy as jnp
from jax import lax
from jax.experimental import pallas as pl
from jax.experimental.pallas import tpu as pltpu
from jax.sharding import PartitionSpec as P

HEAD = 64
LANG = 96
SLOTS = 128
EPS = 1e-5
NEG = -1e30
GC = 0.7978845608028654
GK = 0.044715
f32 = jnp.float32
bf16 = jnp.bfloat16
MESH = pl.DeviceIdType.MESH

AFTER = {
    "norm": (("agp", 0),),
    "A0q": (("agp", 1),),
    "A0p1": (("agp", 2),),
    "A0p2": (("agp", 3), ("zw", 0, 1), ("zw", 0, 2), ("ag2", 0), ("ag1", 1), ("zw", 0, 3),),
    "gate": (("zs", 1), ("ag2", 1), ("ag3", 0),),
    "A1p0": (("zw", 1, 1),),
    "A1p1": (("ag1", 2), ("ag3", 1), ("zw", 1, 2), ("ag1", 3), ("ag2", 2),),
    "A1p3": (("zw", 1, 3),),
    "A2p2": (("ag1", 4),),
    "A2p3": (("ag2", 3),),
    "A2s": (("ag3", 2), ("ag1", 5), ("ag2", 4),),
    "F0a": (("ag3", 3),),
    "F0c": (("ag2", 5), ("rs0", 0),),
    "F1b": (("ag3", 4),),
    "F1c": (("rs0", 1), ("rs1", 0),),
    "F2a": (("rs1", 1), ("ag3", 5),),
    "F2c": (("rs0", 2),),
    "F3a": (("rs2", 0), ("rs1", 2),),
    "F3c": (("rs0", 3), ("rs2", 1),),
    "mid2": (("rs1", 3),),
    "outmm": (("rs0", 4),),
    "B0o": (("rs2", 2),),
    "B0p1": (("rs1", 4), ("g", 0),),
    "B0p2": (("zfa", 0, 2),),
    "B0g": (("g", 1), ("rs0", 5), ("rs2", 3),),
    "B1o": (("rs3", 0),),
    "B1p0": (("rs3", 1), ("rs1", 5), ("rs3", 2),),
    "B1p1": (("zfa", 0, 3),),
    "B1g": (("rs0", 6), ("rs2", 4),),
    "B1h": (("rs3", 3), ("rs1", 6), ("rs2", 5), ("g", 2),),
    "B2p1": (("zza", 0, 2),),
    "B2g": (("rs0", 7), ("rs1", "z0"), ("rs3", 4),),
    "B2h": (("rs1", 7),),
    "B3o": (("zza", 0, 3),),
    "B3p0": (("g", 3), ("rs3", 5), ("rs2", 6), ("rs2", "z0"),),
    "B3g": (("rs0", 8), ("rs2", 7), ("zza", 1, 3), ("g", 4), ("rs3", 6), ("rs1", 8), ("zza", 2, 3), ("rs3", "z0"), ("fin0", 0),),
    "tail": (("rs3", 7), ("zza", 1, 2), ("v", 0), ("g", 5), ("rs2", 8), ("zza", 2, 2), ("v", 1), ("fin1", 0), ("rs3", 8), ("fin0", 2), ("v", 2), ("g", 6), ("fin0", 1), ("fin1", 2), ("v", 3), ("g", 7), ("fin1", 1), ("fin2", 0), ("fin2", 2), ("fin2", 1), ("v", 4), ("fin3", 0), ("g", 8), ("fin3", 2), ("fin3", 1),),
}


def mm(lhs, rhs, form):
    dims = {"nn": ((1,), (0,)), "nt": ((1,), (1,)), "tn": ((0,), (0,))}[form]
    return lax.dot_general(lhs, rhs, (dims, ((), ())), preferred_element_type=f32)


def blk(start, size, align):
    return pl.ds(pl.multiple_of(start, align), size)


def standardize(rows):
    centre = jnp.mean(rows, axis=1, keepdims=True)
    offset = rows - centre
    spread = jnp.mean(offset * offset, axis=1, keepdims=True)
    inv = lax.rsqrt(spread + EPS)
    return offset * inv, inv


def layer_kernel(
    x_hbm, og_hbm, gate_hbm, marks_ref, again_ref, fgain_ref, gbias_ref,
    sq_ref, cq_ref, so_ref, co_ref, up_ref, dn_ref,
    out_hbm, tg_hbm, fin, gout, vec_ref,
    buf, crecv, p1a, p1b, p2a, p2b, cr_o, p1a_o, p1b_o, p2a_o, p2b_o,
    z_f, z_o, z_q, e_f, e_o, e_q, zr, ze, p1a_z, p1b_z, p2a_z, p2b_z, gg, gcr, gxr, gyr, gzr, vs, vr, vz,
    og_ref, bias_ref, h, qkv, o, lse, sc, aa, mid, h2, acc, gh, eb, wb,
    io, loc, ap_s, ap_r, a0_s, a0_r, az_s, az_r, a1_s, a1_r, a2_s, a2_r, ac_s, ac_r,
    rc_s, rc_r, r1_s, r1_r, r2_s, r2_r, rz_s, rz_r, re_r, zf_s, zf_r, zfe_r,
    f1_s, f1_r, f2_s, f2_r, fc_s, fc_r, fl,
    g_s, g_r, gz_s, gz_r, ga_s, ga_r, gl, v_s, v_r, vz_s, vz_r,
):
    R, D = x_hbm.shape
    gate_ref = buf.at[2, 0, 0]
    x_ref = eb
    gz = og_ref
    CH = buf.shape[3]
    XH, YH = CH // 2, D // 2
    ZF = zr.shape[2]
    AR = XH // 2
    QR = sq_ref.shape[0]
    F = QR // 3
    heads = F // HEAD
    pages = R // SLOTS
    GX = gg.shape[2] // 2

    dp = lax.axis_index("dp")
    z = lax.axis_index("mp")
    c = dp % 2
    x = (dp // 2) % 2
    y = (dp // 4) % 2
    s = z // 2
    ismid = (z + s) % 2
    dev_c = (dp + 1 - 2 * c, z)
    dev_x = (dp + 2 - 4 * x, z)
    dev_y = (dp + 4 - 8 * y, z)

    def zof(slot):
        b0, b1 = slot % 2, slot // 2
        near = (1 - b0) * z + b0 * (4 * s + 1 - z)
        far = (1 - b0) * (2 - s) + b0 * (3 - 3 * s)
        return (1 - b1) * near + b1 * far

    def seen_as(slot):
        is1 = 1 - slot // 2
        return is1 + (1 - is1) * (3 - ismid)

    def remote(src, dst, ss, rs, dev):
        return pltpu.make_async_remote_copy(
            src_ref=src, dst_ref=dst, send_sem=ss, recv_sem=rs, device_id=dev, device_id_type=MESH
        )

    bar = pltpu.get_barrier_semaphore()
    partners = (dev_c, dev_x, dev_y, (dp, zof(1)), (dp, zof(2)), (dp, zof(3)))
    for dev in partners:
        pl.semaphore_signal(bar, inc=1, device_id=dev, device_id_type=MESH)

    ins = [
        pltpu.make_async_copy(src, dst, io.at[i])
        for i, (src, dst) in enumerate(((x_hbm, x_ref), (gate_hbm, gate_ref), (og_hbm, og_ref)))
    ]
    ins[0].start()
    local = []
    for i, (src, g, cc, r0) in enumerate(
        (
            (sq_ref, 0, 0, 0), (so_ref, 0, 0, QR), (cq_ref, 0, 1, 0), (co_ref, 0, 1, QR),
            (up_ref, 1, 0, 0), (dn_ref, 1, 1, 0),
        )
    ):
        cp = pltpu.make_async_copy(src, buf.at[g, cc, z, pl.ds(r0, src.shape[0]), :], loc.at[i])
        cp.start()
        local.append(cp)
    ins[1].start()
    ins[2].start()

    def wpart(g, cc, zz, r0, nr, c0, nc):
        return buf.at[g, cc, zz, blk(r0, nr, 16), blk(c0, nc, 128)]

    def wquarter(g, zz):
        return wpart(g, c, zz, XH * x, XH, YH * y, YH)

    def z_copy(g, zz, slot_to, sidx, rslot):
        ref = wquarter(g, zz)
        return remote(ref, ref, az_s.at[g, sidx], az_r.at[g, rslot], (dp, zof(slot_to)))

    PIECES = 4

    def piece(zz, q):
        n = AR // PIECES
        out = []
        for i in range(2):
            ref = wpart(0, c, zz, XH * x + AR * i + n * q, n, YH * y, YH)
            out.append(remote(ref, ref, ap_s.at[q, i], ap_r.at[q, i], (dp, zof(1))))
        return out

    def piece_p1(zz, xx, yy, q):
        n = AR // PIECES
        ra = wpart(0, c, zz, XH * xx + n * q, n, YH * y, YH)
        rb = wpart(0, c, zz, XH * x + AR + n * q, n, YH * yy, YH)
        return (
            remote(ra, ra, a0_s.at[q, 0], a0_r.at[q, 0], dev_x), remote(rb, rb, a0_s.at[q, 1], a0_r.at[q, 1], dev_y)
        )

    def ag_piece(q):
        for cp in piece(zof(1), q):
            cp.wait_recv()
        for cp in piece_p1(zof(1), x, y, q):
            cp.start()

    def ag_zsend(g):
        if g == 0:
            for q in range(PIECES):
                for cp in piece(z, q):
                    cp.start()
        else:
            z_copy(g, z, 1, 0, 1).start()

        @pl.when(ismid == 1)
        def _():
            z_copy(g, z, 2, 1, 2).start()

    def ag_zsend_wait(g):
        if g == 0:
            for q in range(PIECES):
                for cp in piece(z, q):
                    cp.wait_send()
        else:
            z_copy(g, z, 1, 0, 1).wait_send()

        @pl.when(ismid == 1)
        def _():
            for i in range(1, 5):
                z_copy(g, z, 1, i, 1).wait_send()

    def ag_p1(g, j):
        zz = zof(j)
        ra = wpart(g, c, zz, XH * x, AR, YH * y, YH)
        rb = wpart(g, c, zz, XH * x + AR, AR, YH * y, YH)
        ia = wpart(g, c, zz, XH * (1 - x), AR, YH * y, YH)
        ib = wpart(g, c, zz, XH * x + AR, AR, YH * (1 - y), YH)
        return (
            (remote(ra, ra, a1_s.at[g, j, 0], a1_r.at[g, j, 0], dev_x),
             remote(rb, rb, a1_s.at[g, j, 1], a1_r.at[g, j, 1], dev_y)),
            (remote(ia, ia, a1_s.at[g, j, 0], a1_r.at[g, j, 0], dev_x),
             remote(ib, ib, a1_s.at[g, j, 1], a1_r.at[g, j, 1], dev_y)),
        )

    def ag_p2(g, j):
        zz = zof(j)
        outs, ins = [], []
        for xx in range(2):
            ra = wpart(g, c, zz, XH * xx, AR, YH * y, YH)
            ia = wpart(g, c, zz, XH * xx, AR, YH * (1 - y), YH)
            outs.append(remote(ra, ra, a2_s.at[g, j, xx], a2_r.at[g, j, xx], dev_y))
            ins.append(remote(ia, ia, a2_s.at[g, j, xx], a2_r.at[g, j, xx], dev_y))
        rb = wpart(g, c, zz, XH * x + AR, AR, 0, D)
        ib = wpart(g, c, zz, XH * (1 - x) + AR, AR, 0, D)
        outs.append(remote(rb, rb, a2_s.at[g, j, 2], a2_r.at[g, j, 2], dev_x))
        ins.append(remote(ib, ib, a2_s.at[g, j, 2], a2_r.at[g, j, 2], dev_x))
        return outs, ins

    def ag_c(g, j):
        zz = zof(j)
        mine, theirs = buf.at[g, c, zz], buf.at[g, 1 - c, zz]
        return (
            remote(mine, mine, ac_s.at[g, j], ac_r.at[g, j], dev_c),
            remote(theirs, theirs, ac_s.at[g, j], ac_r.at[g, j], dev_c),
        )

    def ag_forward(g, j):
        @pl.when(ismid == 1)
        def _():
            if g == 1 or j > 1:
                z_copy(g, zof(j), 1, 0, j).wait_recv()
            if j == 1:
                z_copy(g, zof(1), 2, 2, 3).start()
            else:
                z_copy(g, zof(j), 1, j + 1, j).start()

    def ag_1(t):
        g, j = t // 3, t % 3 + 1

        @pl.when(ismid == 0)
        def _():
            z_copy(g, zof(j), 1, 0, j).wait_recv()

        for cp in ag_p1(g, j)[0]:
            cp.start()

    def ag_2(t):
        g, j = t // 3, t % 3 + 1
        if t == 0:
            outs = [cp for q in range(PIECES) for cp in piece_p1(zof(1), x, y, q)]
            arrivals = [cp for q in range(PIECES) for cp in piece_p1(zof(1), 1 - x, 1 - y, q)]
        else:
            outs, arrivals = ag_p1(g, j)
        for cp in arrivals:
            cp.wait_recv()
        for cp in ag_p2(g, j)[0]:
            cp.start()
        for cp in outs:
            cp.wait_send()

    def ag_3(t):
        g, j = t // 3, t % 3 + 1
        outs, arrivals = ag_p2(g, j)
        for cp in arrivals:
            cp.wait_recv()
        ag_c(g, j)[0].start()
        for cp in outs:
            cp.wait_send()

    def ag_done(g, j):
        mine, theirs = ag_c(g, j)
        theirs.wait_recv()
        mine.wait_send()

    def add_rows(dst, dst_idx, r0, nr, c0, nc, src, src_idx):
        step = next(n for n in (64, 48) if nr % n == 0)

        @pl.loop(0, nr // step)
        def _(i):
            rows = blk(r0 + i * step, step, 16)
            cols = blk(c0, nc, 128)
            d = dst[(*dst_idx, rows, cols)].astype(f32)
            t = src[(*src_idx, blk(i * step, step, 16), slice(None))].astype(f32)
            dst[(*dst_idx, rows, cols)] = (d + t).astype(bf16)

    def single(b, nr, ha, kq, slot, sem):
        def reg(cc, r0, n, c0, w):
            return buf.at[b, cc, kq, blk(r0, n, 16), blk(c0, w, 128)]

        def add(r0, n, c0, w, src, idx):
            add_rows(buf, (b, c, kq), r0, n, c0, w, src, idx)

        return dict(
            reg=reg, add=add, nr=nr, ha=ha, off=0, sem=sem,
            cr=(crecv, (slot,), pl.ds(0, nr)), a1=(p1a, (slot,), pl.ds(0, ha)),
            b1=[(p1b, (slot, xx), pl.ds(0, ha)) for xx in range(2)],
            a2=(p2a, (slot,), pl.ds(0, ha)), b2=(p2b, (slot,), pl.ds(0, ha)),
        )

    def k_ffn(k):
        return single(2, CH, (XH - ZF) // 2, k, k, k)

    def k_first():
        kd = k_ffn(0)
        every = slice(None)
        kd.update(
            off=XH - ZF, ha=ZF // 2, sem=9, a1=(p1a_z, (), every), b1=[(p1b_z, (xx,), every) for xx in range(2)],
            a2=(p2a_z, (), every), b2=(p2b_z, (), every),
        )
        return kd

    def k_qkv(i):
        return single(1, QR, QR // 4, 3 - i, i, 5 + i)

    def k_out():
        def reg(cc, r0, n, c0, w):
            return buf.at[1, cc, :, blk(QR + r0, n, 16), blk(c0, w, 128)]

        def add(r0, n, c0, w, src, idx):
            for q in range(4):
                add_rows(buf, (1, c, q), QR + r0, n, c0, w, src, (*idx, q))

        every = slice(None)
        return dict(
            reg=reg, add=add, nr=F, ha=F // 4, off=0, sem=4,
            cr=(cr_o, (), every), a1=(p1a_o, (), every), b1=[(p1b_o, (xx,), every) for xx in range(2)],
            a2=(p2a_o, (), every), b2=(p2b_o, (), every),
        )

    def land(part):
        ref, idx, rows = part
        return ref.at[(*idx, rows)]

    def rs_c(kd):
        n = kd["sem"]
        return remote(kd["reg"](1 - c, 0, kd["nr"], 0, D), land(kd["cr"]), rc_s.at[n], rc_r.at[n], dev_c)

    def rs_p1(kd):
        n, half, ha, reg, off = kd["sem"], kd["nr"] // 2, kd["ha"], kd["reg"], kd["off"]
        cps = [remote(reg(c, half * (1 - x) + off, ha, 0, D), land(kd["a1"]), r1_s.at[n, 0], r1_r.at[n, 0], dev_x)]
        for xx in range(2):
            src = reg(c, half * xx + off + ha, ha, YH * (1 - y), YH)
            cps.append(remote(src, land(kd["b1"][xx]), r1_s.at[n, 1 + xx], r1_r.at[n, 1 + xx], dev_y))
        return cps

    def rs_p2(kd):
        n, half, ha, reg, off = kd["sem"], kd["nr"] // 2, kd["ha"], kd["reg"], kd["off"]
        return [
            remote(reg(c, half * x + off, ha, YH * (1 - y), YH), land(kd["a2"]), r2_s.at[n, 0], r2_r.at[n, 0], dev_y),
            remote(
                reg(c, half * (1 - x) + off + ha, ha, YH * y, YH), land(kd["b2"]), r2_s.at[n, 1], r2_r.at[n, 1], dev_x
            ),
        ]

    def rs_0(kd):
        rs_c(kd).start()

    def rs_1(kd, between=None):
        cp = rs_c(kd)
        cp.wait_recv()
        kd["add"](0, kd["nr"], 0, D, kd["cr"][0], kd["cr"][1])
        if between is not None:
            between()
        for q in rs_p1(kd):
            q.start()
        cp.wait_send()

    def rs_2(kd):
        half, ha, off = kd["nr"] // 2, kd["ha"], kd["off"]
        cps = rs_p1(kd)
        for q in cps:
            q.wait_recv()
        kd["add"](half * x + off, ha, 0, D, kd["a1"][0], kd["a1"][1])
        for xx in range(2):
            kd["add"](half * xx + off + ha, ha, YH * y, YH, kd["b1"][xx][0], kd["b1"][xx][1])
        for q in rs_p2(kd):
            q.start()
        for q in cps:
            q.wait_send()

    def rs_3(kd, after=None):
        half, ha, off = kd["nr"] // 2, kd["ha"], kd["off"]
        cps = rs_p2(kd)
        for q in cps:
            q.wait_recv()
        kd["add"](half * x + off, ha, YH * y, YH, kd["a2"][0], kd["a2"][1])
        kd["add"](half * x + off + ha, ha, YH * y, YH, kd["b2"][0], kd["b2"][1])
        if after is not None:
            after()
        for q in cps:
            q.wait_send()

    groups = (
        (2, 0, XH, XH - ZF, z_f, e_f),
        (1, QR, F // 2, F // 2, z_o, e_o),
        (1, 0, QR // 2, QR // 2, z_q, e_q),
    )

    def z_part(gi, k):
        b, r0, half, n = groups[gi][:4]
        return buf.at[b, c, k, blk(r0 + half * x, n, 16), blk(YH * y, YH, 128)]

    def z_out(gi, k):
        return remote(z_part(gi, k), groups[gi][4].at[0 if k == 1 else 1], rz_s.at[gi, k], rz_r.at[gi, 0 if k == 1 else 1], (dp, zof(k)))

    def z_hop(gi, k):
        return remote(z_part(gi, k), groups[gi][5].at[k - 2], rz_s.at[gi, k], re_r.at[gi, k - 2], (dp, zof(1)))

    def z_start(gi, k):
        if k == 1:
            z_out(gi, 1).start()
        if k > 1:

            @pl.when(ismid == 0)
            def _():
                z_hop(gi, k).start()

    def z_join(gi, k):
        b, r0, half, n, _to, mid_buf = groups[gi]

        @pl.when(ismid == 1)
        def _():
            z_hop(gi, k).wait_recv()
            add_rows(buf, (b, c, k), r0 + half * x, n, YH * y, YH, mid_buf, (k - 2,))
            z_out(gi, k).start()

    def zf_rows(k, xx):
        return buf.at[2, c, k, pl.ds(XH * (xx + 1) - ZF, ZF), :]

    def zf_out(k, xx):
        to = 0 if k == 1 else 1
        return remote(zf_rows(k, xx), zr.at[to, xx], zf_s.at[k, xx], zf_r.at[to, xx], (dp, zof(k)))

    def zf_hop(k, xx):
        return remote(zf_rows(k, xx), ze.at[k - 2, xx], zf_s.at[k, xx], zfe_r.at[k - 2, xx], (dp, zof(1)))

    def zf_start(k):
        if k == 1:
            for xx in range(2):
                zf_out(1, xx).start()
        if k > 1:

            @pl.when(ismid == 0)
            def _():
                for xx in range(2):
                    zf_hop(k, xx).start()

    def zf_join(_gi, k):
        @pl.when(ismid == 1)
        def _():
            for xx in range(2):
                zf_hop(k, xx).wait_recv()
                add_rows(buf, (2, c, k), XH * (xx + 1) - ZF, ZF, 0, D, ze, (k - 2, xx))
                zf_out(k, xx).start()

    def zf_sum():
        for xx in range(2):
            for slot in range(2):
                zf_out(1 + slot, xx).wait_recv()
                add_rows(buf, (2, c, 0), XH * (xx + 1) - ZF, ZF, 0, D, zr, (slot, xx))
        for q in rs_p1(k_first()):
            q.start()

    def fin_part(gi, r, n, c0, w):
        r0 = groups[gi][1]
        return fin.at[0 if gi == 0 else 1, c, blk(r0 + r, n, 16), blk(c0, w, 128)]

    def own_part(gi, r, n):
        b, r0 = groups[gi][:2]
        return buf.at[b, c, 0, blk(r0 + r, n, 16), blk(YH * y, YH, 128)]

    def fin_p1(gi):
        half = groups[gi][2]
        q = half // 2
        return [
            remote(
                own_part(gi, half * x + q * i, q), fin_part(gi, half * x + q * i, q, YH * y, YH),
                f1_s.at[gi, i], f1_r.at[gi, i], dev,
            )
            for i, dev in enumerate((dev_x, dev_y))
        ]

    def fin_local(gi):
        half = groups[gi][2]
        return pltpu.make_async_copy(
            own_part(gi, half * x, half), fin_part(gi, half * x, half, YH * y, YH), fl.at[gi]
        )

    def fin_p2(gi):
        half = groups[gi][2]
        q = half // 2
        cps = []
        for xx in range(2):
            ref = fin_part(gi, half * xx, q, YH * y, YH)
            cps.append(remote(ref, ref, f2_s.at[gi, xx], f2_r.at[gi, xx], dev_y))
        ref = fin_part(gi, half * x + q, q, 0, D)
        cps.append(remote(ref, ref, f2_s.at[gi, 2], f2_r.at[gi, 2], dev_x))
        return cps

    def fin_c(gi):
        ref = fin_part(gi, 0, 2 * groups[gi][2], 0, D)
        return remote(ref, ref, fc_s.at[gi], fc_r.at[gi], dev_c)

    def fin_0(gi):
        b, r0, half, n, part, _mid = groups[gi]
        for k in (1, 2):
            z_out(gi, k).wait_recv()
        for slot in range(2):
            add_rows(buf, (b, c, 0), r0 + half * x, n, YH * y, YH, part, (slot,))
        for q in fin_p1(gi):
            q.start()
        fin_local(gi).start()
        for k in (1, 2, 3):
            z_out(gi, k).wait_send()
            if gi == 0:
                for xx in range(2):
                    zf_out(k, xx).wait_send()

    def fin_1(gi):
        for q in fin_p1(gi):
            q.wait_recv()
        fin_local(gi).wait()
        for q in fin_p2(gi):
            q.start()
        for q in fin_p1(gi):
            q.wait_send()

    def fin_2(gi):
        for q in fin_p2(gi):
            q.wait_recv()
        fin_c(gi).start()
        for q in fin_p2(gi):
            q.wait_send()

    def fin_3(gi):
        fin_c(gi).wait_recv()
        fin_c(gi).wait_send()

    def g_copy(i):
        xs, xo = blk(GX * x, GX, 16), blk(GX * (1 - x), GX, 16)
        ys, yo = blk(YH * y, YH, 128), blk(YH * (1 - y), YH, 128)
        src, dst, dev = {
            0: lambda: (gg.at[:, 1 - c], gcr, dev_c),
            1: lambda: (gg.at[z, c, xo, :], gxr, dev_x),
            2: lambda: (gg.at[z, c, xs, yo], gyr, dev_y),
            3: lambda: (gg.at[z, c, xs, ys], gout.at[z, c, xs, ys], dev_y),
            4: lambda: (gout.at[z, c, xs, :], gout.at[z, c, xs, :], dev_x),
            5: lambda: (gout.at[:, c], gout.at[:, c], dev_c),
        }[i]()
        return remote(src, dst, g_s.at[i], g_r.at[i], dev)

    def g_z(slot, rslot):
        return remote(
            gg.at[zof(slot), c], gzr.at[rslot - 1], gz_s.at[slot], gz_r.at[rslot], (dp, zof(slot))
        )

    def g_za(slot, rslot):
        return remote(gout.at[z, c], gout.at[z, c], ga_s.at[slot], ga_r.at[rslot], (dp, zof(slot)))

    def g_local():
        xs, ys = blk(GX * x, GX, 16), blk(YH * y, YH, 128)
        return pltpu.make_async_copy(gg.at[z, c, xs, ys], gout.at[z, c, xs, ys], gl.at[0])

    def g_step(i):
        if i == 0:
            g_copy(0).start()
        if i == 1:
            g_copy(0).wait_recv()
            for q in range(4):
                add_rows(gg, (q, c), 0, 2 * GX, 0, D, gcr, (q,))
            for slot in range(1, 4):
                g_z(slot, seen_as(slot)).start()
            g_copy(0).wait_send()
        if i == 2:
            for slot in range(1, 4):
                g_z(slot, slot).wait_recv()
            t = gg[z, c].astype(f32)
            for slot in range(3):
                t = t + gzr[slot].astype(f32)
            gg[z, c] = t.astype(bf16)
            g_copy(1).start()
            for slot in range(1, 4):
                g_z(slot, slot).wait_send()
        if i == 3:
            g_copy(1).wait_recv()
            add_rows(gg, (z, c), GX * x, GX, 0, D, gxr, ())
            g_copy(2).start()
            g_copy(1).wait_send()
        if i == 4:
            g_copy(2).wait_recv()
            add_rows(gg, (z, c), GX * x, GX, YH * y, YH, gyr, ())
            g_local().start()
            g_copy(3).start()
            g_copy(2).wait_send()
        if i == 5:
            g_copy(3).wait_recv()
            g_local().wait()
            g_copy(4).start()
            g_copy(3).wait_send()
        if i == 6:
            g_copy(4).wait_recv()
            for slot in range(1, 4):
                g_za(slot, seen_as(slot)).start()
            g_copy(4).wait_send()
        if i == 7:
            for slot in range(1, 4):
                g_za(slot, slot).wait_recv()
            g_copy(5).start()
            for slot in range(1, 4):
                g_za(slot, slot).wait_send()
        if i == 8:
            g_copy(5).wait_recv()
            g_copy(5).wait_send()

    def v_copy(i):
        return remote(vs.at[i], vr.at[i], v_s.at[i], v_r.at[i], (dev_c, dev_x, dev_y)[i])

    def v_z(slot, zz_dst, rslot):
        return remote(vz.at[z], vz.at[zz_dst], vz_s.at[slot], vz_r.at[rslot], (dp, zof(slot)))

    def v_step(i):
        if i == 0:
            v_copy(0).start()
        if i in (1, 2):
            v_copy(i - 1).wait_recv()
            vs[i] = vs[i - 1] + vr[i - 1]
            v_copy(i).start()
            v_copy(i - 1).wait_send()
        if i == 3:
            v_copy(2).wait_recv()
            vz[z] = vs[2] + vr[2]
            for slot in range(1, 4):
                v_z(slot, z, seen_as(slot)).start()
            v_copy(2).wait_send()
        if i == 4:
            for slot in range(1, 4):
                v_z(slot, z, slot).wait_recv()
            vec_ref[...] = (vz[0] + vz[1]) + (vz[2] + vz[3])
            for slot in range(1, 4):
                v_z(slot, z, slot).wait_send()

    def kind(n):
        if n == "z0":
            return k_first()
        return k_ffn(n) if n < 4 else k_out() if n == 4 else k_qkv(n - 5)

    def first(n):
        if n == "z0":
            zf_sum()
        else:
            rs_1(kind(n), lambda: zf_start(n) if n < 4 else None)

    def third(n):
        if n == "z0":
            rs_3(kind(n))
        elif n < 4:
            rs_3(kind(n), lambda: z_start(0, n))
        elif n == 4:
            rs_3(kind(n), lambda: [z_start(1, q) for q in range(1, 4)])
        else:
            rs_3(kind(n), lambda: z_start(2, 8 - n))

    events = {
        "zs": ag_zsend, "zw": ag_forward, "agp": ag_piece, "ag1": ag_1, "ag2": ag_2, "ag3": ag_3,
        "rs0": lambda n: rs_0(kind(n)), "rs1": first, "rs2": lambda n: rs_2(kind(n)), "rs3": third,
        "zza": z_join, "zfa": zf_join, "g": g_step, "v": v_step, "fin0": fin_0, "fin1": fin_1, "fin2": fin_2, "fin3": fin_3,
    }

    def after(name, k=None, p=None):
        if k is None:
            for ev in AFTER.get(name, ()):
                events[ev[0]](*ev[1:])
            return
        for kk in range(4):
            for pp in range(1 if p is None else 4):
                found = AFTER.get(name[0] + str(kk) + name[1:] + ("" if p is None else str(pp)), ())
                if found:

                    @pl.when((k == kk) if p is None else (k == kk) & (p == pp))
                    def _():
                        for ev in found:
                            events[ev[0]](*ev[1:])

    TR = 128
    again = again_ref[...].astype(f32).reshape(1, D)
    fgain = fgain_ref[...].astype(f32).reshape(1, D)
    gbias = gbias_ref[...].astype(f32).reshape(1, D)

    pl.semaphore_wait(bar, 6)
    for cp in local[:4]:
        cp.wait()
    ag_zsend(0)

    after("start")

    key_id = lax.broadcasted_iota(jnp.int32, (SLOTS, SLOTS), 0)
    query_id = lax.broadcasted_iota(jnp.int32, (SLOTS, SLOTS), 1)
    key_kind = jnp.where(key_id < LANG, 1, 0)
    query_kind = jnp.where(query_id < LANG, 1, 0)
    for p in range(pages):
        row = marks_ref[pl.ds(pages * z + p, 1), :]
        real = jnp.broadcast_to(jnp.where(row > 0, 0.0, NEG), (SLOTS, SLOTS)).T
        bias_ref[0, p] = jnp.where(key_kind == query_kind, real, NEG).astype(bf16)
        bias_ref[1, p] = jnp.where(key_kind == query_kind, NEG, real).astype(bf16)

    ins[0].wait()

    @pl.loop(0, R // TR)
    def _(i):
        rows = blk(i * TR, TR, 16)
        u, _inv = standardize(x_ref[rows, :].astype(f32))
        h[rows, :] = (u * again).astype(bf16)
        sc[rows, :] = jnp.zeros((TR, D), f32)
        mid[rows, :] = jnp.zeros((TR, D), f32)
        gh[rows, :] = jnp.zeros((TR, D), f32)

    vs[...] = jnp.zeros_like(vs)
    for cp in local[4:] + ins[1:]:
        cp.wait()
    after("norm")

    @pl.loop(0, 4)
    def _(k):
        zz = zof(k)

        @pl.when(k > 0)
        def _():
            ag_done(0, k)

        for at in range(2):
            qkv[at, k] = mm(buf[0, at, zz, 0:QR, :], h[...], "nt").astype(bf16)
        after("Aq", k)

        @pl.loop(0, pages)
        def _(p):
            cols = blk(p * SLOTS, SLOTS, 128)
            units = [(at, hh) for at in range(2) for hh in range(heads)]
            scores = []
            for at, hh in units:
                qt = qkv[at, k, HEAD * hh : HEAD * (hh + 1), cols]
                kt = qkv[at, k, F + HEAD * hh : F + HEAD * (hh + 1), cols]
                scores.append(mm(kt, qt, "tn"))
            probs = []
            for (at, hh), st in zip(units, scores):
                st = st * HEAD ** (-0.5) + bias_ref[at, p].astype(f32)
                top = jnp.max(st, axis=0, keepdims=True)
                ex = jnp.exp(st - top)
                tot = jnp.sum(ex, axis=0, keepdims=True)
                probs.append((ex * (1.0 / tot)).astype(bf16))
                lse[at, k, hh : hh + 1, cols] = top + jnp.log(tot)
            for (at, hh), pt in zip(units, probs):
                vt = qkv[at, k, 2 * F + HEAD * hh : 2 * F + HEAD * (hh + 1), cols]
                o[at, k, HEAD * hh : HEAD * (hh + 1), cols] = mm(vt, pt, "nn").astype(bf16)
            after("Ap", k, p)

        @pl.loop(0, 2)
        def _(p):
            cols = blk(p * 256, 256, 128)
            for at, dst in ((0, sc), (1, mid)):
                dst[cols, :] += mm(o[at, k, :, cols], buf[0, at, zz, QR:CH, :], "tn")

        after("As", k)

        @pl.when(k == 0)
        def _():
            @pl.loop(0, R // 256)
            def _(i):
                rows = blk(i * 256, 256, 16)
                aa[rows, :] = jax.nn.sigmoid(mm(h[rows, :], gate_ref[...], "nn") + gbias)

            after("gate")

    ag_zsend_wait(0)

    @pl.loop(0, R // TR)
    def _(i):
        rows = blk(i * TR, TR, 16)
        a = aa[rows, :]
        sv, cv = sc[rows, :], mid[rows, :]
        mv = x_ref[rows, :].astype(f32) + a * sv + (1.0 - a) * cv
        sc[rows, :] = sv - cv
        mid[rows, :] = mv
        acc[rows, :] = mv
        u, _inv = standardize(mv)
        h2[rows, :] = (u * fgain).astype(bf16)

    after("join")

    @pl.loop(0, 4)
    def _(k):
        zz = zof(k)

        @pl.when(k > 0)
        def _():
            ag_done(1, k)

        MT = 256

        @pl.loop(0, 2 * (R // MT))
        def _(i):
            rows = blk((i // 2) * MT, MT, 16)
            cols = blk((i % 2) * XH, XH, 128)
            w = mm(h2[rows, :], buf[1, 0, zz, :, cols], "nn")
            ge = mm(og_ref[rows, :], buf[1, 1, zz, blk((i % 2) * XH, XH, 16), :], "nt")
            w2 = w * w
            th = jnp.tanh(GC * w * (1.0 + GK * w2))
            half = 0.5 * (1.0 + th)
            eb[rows, cols] = (w * half).astype(bf16)
            dg = half + 0.5 * w * (1.0 - th * th) * (GC * (1.0 + 3.0 * GK * w2))
            wb[rows, cols] = (dg * ge).astype(bf16)

        after("Fa", k)

        @pl.loop(0, R // MT)
        def _(i):
            rows = blk(i * MT, MT, 16)
            acc[rows, :] += mm(eb[rows, :], buf[1, 1, zz], "nn")
            gh[rows, :] += mm(wb[rows, :], buf[1, 0, zz], "nt")

        after("Fb", k)

        @pl.loop(0, CH // 384)
        def _(i):
            cols = blk(i * 384, 384, 128)
            buf[2, 1, k, blk(i * 384, 384, 16), :] = mm(eb[:, cols], og_ref[...], "tn").astype(bf16)
            buf[2, 0, k, blk(i * 384, 384, 16), :] = mm(h2[:, cols], wb[...], "tn").astype(bf16)

        after("Fc", k)

    ag_zsend_wait(1)

    TS = 128
    zero_row = jnp.zeros((1, D), f32)

    def mid_back(i, sums):
        gain_sum, bias_sum = sums
        rows = blk(i * TS, TS, 16)
        h2[rows, :] = acc[rows, :].astype(bf16)
        u, inv = standardize(mid[rows, :])
        gy = gh[rows, :]
        gain_sum = gain_sum + jnp.sum(gy * u, axis=0, keepdims=True)
        sy = gy * fgain
        m1 = jnp.mean(sy, axis=1, keepdims=True)
        m2 = jnp.mean(sy * u, axis=1, keepdims=True)
        gm = og_ref[rows, :].astype(f32) + inv * (sy - m1 - u * m2)
        acc[rows, :] = gm
        a = aa[rows, :]
        eb[rows, :] = (a * gm).astype(bf16)
        wb[rows, :] = ((1.0 - a) * gm).astype(bf16)
        gzv = (gm * sc[rows, :] * a * (1.0 - a)).astype(bf16)
        gz[rows, :] = gzv
        bias_sum = bias_sum + jnp.sum(gzv.astype(f32), axis=0, keepdims=True)
        return gain_sum, bias_sum

    gain_sum, bias_sum = lax.fori_loop(0, R // TS, mid_back, (zero_row, zero_row))
    vs[0, 1:2, :] = bias_sum
    vs[0, 2:3, :] = gain_sum
    out_copy = pltpu.make_async_copy(h2, out_hbm, io.at[3])
    out_copy.start()
    after("mid2")
    gate_again = buf.at[2, 1 - c, 1]
    gate_load = pltpu.make_async_copy(gate_hbm, gate_again, io.at[5])
    gate_load.start()

    for k in range(4):
        for at, gref in ((0, eb), (1, wb)):
            buf[1, at, k, QR:CH, :] = mm(o[at, k], gref[...], "nn").astype(bf16)
    after("outmm")
    for i in range(4):
        t = mm(h[:, F * i : F * (i + 1)], gz[...], "tn").astype(bf16)
        gg[i, 0] = t[: F // 2]
        gg[i, 1] = t[F // 2 :]
    after("ggrad")

    x_again = wb
    x_load = pltpu.make_async_copy(x_hbm, x_again, io.at[6])

    @pl.loop(0, 4)
    def _(i):
        k = 3 - i
        zz = zof(k)
        for at, gref in ((0, eb), (1, wb)):
            o[at, k] = mm(buf[0, at, zz, QR:CH, :], gref[...], "nt").astype(bf16)

        @pl.when(i == 3)
        def _():
            x_load.start()

        after("Bo", i)

        @pl.loop(0, pages)
        def _(p):
            cols = blk(p * SLOTS, SLOTS, 128)
            units = [(at, hh) for at in range(2) for hh in range(heads)]
            for grp in (units,):
                rd = []
                for at, hh in grp:
                    qs = slice(HEAD * hh, HEAD * (hh + 1))
                    ks = slice(F + HEAD * hh, F + HEAD * (hh + 1))
                    vsl = slice(2 * F + HEAD * hh, 2 * F + HEAD * (hh + 1))
                    qt, kt, vt, go = qkv[at, k, qs, cols], qkv[at, k, ks, cols], qkv[at, k, vsl, cols], o[at, k, qs, cols]
                    rd.append((at, hh, qs, ks, vsl, qt, kt, vt, go, mm(kt, qt, "tn"), mm(vt, go, "tn")))
                ps = []
                for at, hh, qs, ks, vsl, qt, kt, vt, go, st, gpt in rd:
                    pt = jnp.exp(st * HEAD ** (-0.5) + bias_ref[at, p].astype(f32) - lse[at, k, hh : hh + 1, cols])
                    pg = pt * gpt
                    gst = (pg - pt * jnp.sum(pg, axis=0, keepdims=True)).astype(bf16)
                    ps.append((pt.astype(bf16), gst))
                for (at, hh, qs, ks, vsl, qt, kt, vt, go, st, gpt), (pb, gst) in zip(rd, ps):
                    qkv[at, k, vsl, cols] = mm(go, pb, "nt").astype(bf16)
                    qkv[at, k, qs, cols] = (mm(kt, gst, "nn") * HEAD ** (-0.5)).astype(bf16)
                    qkv[at, k, ks, cols] = (mm(qt, gst, "nt") * HEAD ** (-0.5)).astype(bf16)
            after("Bp", i, p)

        for at in range(2):
            for q in range(3):
                part = slice(F * q, F * (q + 1))
                buf[1, at, k, part, :] = mm(qkv[at, k, part, :], h[...], "nn").astype(bf16)
        after("Bg", i)

        @pl.loop(0, 2)
        def _(p):
            cols = blk(p * 256, 256, 128)
            t = mm(qkv[0, k, :, cols], buf[0, 0, zz, 0:QR, :], "tn") + mm(qkv[1, k, :, cols], buf[0, 1, zz, 0:QR, :], "tn")

            @pl.when(i == 0)
            def _():
                gh[cols, :] = t

            @pl.when(i > 0)
            def _():
                gh[cols, :] += t

        after("Bh", i)

    gate_load.wait()

    @pl.loop(0, R // 256)
    def _(i):
        rows = blk(i * 256, 256, 16)
        gh[rows, :] += mm(gz[rows, :], gate_again[...], "nt")

    def first_back(i, gain_sum):
        rows = blk(i * TS, TS, 16)
        u, inv = standardize(x_again[rows, :].astype(f32))
        gy = gh[rows, :]
        gain_sum = gain_sum + jnp.sum(gy * u, axis=0, keepdims=True)
        sy = gy * again
        m1 = jnp.mean(sy, axis=1, keepdims=True)
        m2 = jnp.mean(sy * u, axis=1, keepdims=True)
        eb[rows, :] = (acc[rows, :] + inv * (sy - m1 - u * m2)).astype(bf16)
        return gain_sum

    x_load.wait()
    vs[0, 0:1, :] = lax.fori_loop(0, R // TS, first_back, zero_row)
    tg_copy = pltpu.make_async_copy(eb, tg_hbm, io.at[4])
    tg_copy.start()
    after("tail")
    out_copy.wait()
    tg_copy.wait()


def widen_kernel(
    out_in, tg_in, fin, gout, vec_in,
    out_o, tg_o, ag_o, sq_o, cq_o, so_o, co_o, gw_o, gb_o, fg_o, up_o, dn_o,
    narrow, wide, whole, sem_in, sem_out, sem_pass,
):
    F = so_o.shape[0]
    QR = 3 * F
    passes = []
    for i, (src, dst) in enumerate(((out_in, out_o), (tg_in, tg_o))):
        load = pltpu.make_async_copy(src, whole.at[i], sem_pass.at[i])
        passes.append((load, pltpu.make_async_copy(whole.at[i], dst, sem_pass.at[2 + i])))
    CH = 4 * F
    jobs = []
    for i, (src, dsts) in enumerate(
        (
            (gout, ((0, gw_o),)), (fin.at[0, 0], ((0, up_o),)), (fin.at[0, 1], ((0, dn_o),)),
            (fin.at[1, 0], ((0, sq_o), (QR, so_o))), (fin.at[1, 1], ((0, cq_o), (QR, co_o))),
        )
    ):
        load = pltpu.make_async_copy(src, narrow.at[pl.ds(CH * i, CH)], sem_in.at[i])
        saves = [
            pltpu.make_async_copy(wide.at[pl.ds(CH * i + r0, dst.shape[0])], dst, sem_out.at[i, q])
            for q, (r0, dst) in enumerate(dsts)
        ]
        load.start()
        jobs.append((load, saves))
    for load, _ in passes:
        load.start()
    ag_o[...] = vec_in[0, :]
    gb_o[...] = vec_in[1, :]
    fg_o[...] = vec_in[2, :]
    for i, (load, saves) in enumerate(jobs):
        load.wait()

        @pl.loop(0, CH // 64)
        def _(q):
            rows = blk(CH * i + 64 * q, 64, 16)
            wide[rows, :] = narrow[rows, :].astype(f32)

        for cp in saves:
            cp.start()
    for load, save in passes:
        load.wait()
        save.start()
    for _, saves in jobs:
        for cp in saves:
            cp.wait()
    for _, save in passes:
        save.wait()


def body(
    tokens, region_mask, attn_gain, self_qkv, cross_qkv, self_out, cross_out, gate_weight, gate_bias,
    ffn_gain, up_weight, down_weight, out_grad, *, outer,
):
    R, D = tokens.shape
    F = self_out.shape[0]
    QR = 3 * F
    CH = QR + F
    pages = R // SLOTS

    vm = pl.BlockSpec(memory_space=pltpu.VMEM)
    hb = pl.BlockSpec(memory_space=pl.ANY)
    dma = pltpu.SemaphoreType.DMA
    XH, YH, GX, OR, ZF = CH // 2, D // 2, D // 16, F // 4, CH // 6
    scratch = [
        pltpu.VMEM((3, 2, 4, CH, D), bf16),
        pltpu.VMEM((4, CH, D), bf16),
        pltpu.VMEM((4, QR // 4, D), bf16),
        pltpu.VMEM((4, 2, QR // 4, YH), bf16),
        pltpu.VMEM((4, QR // 4, YH), bf16),
        pltpu.VMEM((4, QR // 4, YH), bf16),
        pltpu.VMEM((4, F, D), bf16),
        pltpu.VMEM((4, OR, D), bf16),
        pltpu.VMEM((2, 4, OR, YH), bf16),
        pltpu.VMEM((4, OR, YH), bf16),
        pltpu.VMEM((4, OR, YH), bf16),
        pltpu.VMEM((2, XH - ZF, YH), bf16),
        pltpu.VMEM((2, F // 2, YH), bf16),
        pltpu.VMEM((2, QR // 2, YH), bf16),
        pltpu.VMEM((2, XH - ZF, YH), bf16),
        pltpu.VMEM((2, F // 2, YH), bf16),
        pltpu.VMEM((2, QR // 2, YH), bf16),
        pltpu.VMEM((2, 2, ZF, D), bf16),
        pltpu.VMEM((2, 2, ZF, D), bf16),
        pltpu.VMEM((ZF // 2, D), bf16),
        pltpu.VMEM((2, ZF // 2, YH), bf16),
        pltpu.VMEM((ZF // 2, YH), bf16),
        pltpu.VMEM((ZF // 2, YH), bf16),
        pltpu.VMEM((4, 2, 2 * GX, D), bf16),
        pltpu.VMEM((4, 2 * GX, D), bf16),
        pltpu.VMEM((GX, D), bf16),
        pltpu.VMEM((GX, YH), bf16),
        pltpu.VMEM((3, 2 * GX, D), bf16),
        pltpu.VMEM((3, 8, D), f32),
        pltpu.VMEM((3, 8, D), f32),
        pltpu.VMEM((4, 8, D), f32),
        pltpu.VMEM((R, D), bf16),
        pltpu.VMEM((2, pages, SLOTS, SLOTS), bf16),
        pltpu.VMEM((R, D), bf16),
        pltpu.VMEM((2, 4, QR, R), bf16),
        pltpu.VMEM((2, 4, F, R), bf16),
        pltpu.VMEM((2, 4, 8, R), f32),
        pltpu.VMEM((R, D), f32),
        pltpu.VMEM((R, D), f32),
        pltpu.VMEM((R, D), f32),
        pltpu.VMEM((R, D), bf16),
        pltpu.VMEM((R, D), f32),
        pltpu.VMEM((R, D), f32),
        pltpu.VMEM((R, D), bf16),
        pltpu.VMEM((R, D), bf16),
        dma((7,)),
        dma((6,)), dma((4, 2)), dma((4, 2)), dma((4, 2)), dma((4, 2)), dma((2, 5)), dma((2, 4)), dma((2, 4, 2)), dma((2, 4, 2)), dma((2, 4, 3)), dma((2, 4, 3)),
        dma((2, 4)), dma((2, 4)),
        dma((9,)), dma((9,)), dma((10, 3)), dma((10, 3)), dma((10, 2)), dma((10, 2)), dma((3, 4)), dma((3, 2)),
        dma((3, 2)), dma((4, 2)), dma((2, 2)), dma((2, 2)),
        dma((3, 2)), dma((3, 2)), dma((3, 3)), dma((3, 3)), dma((3,)), dma((3,)), dma((3,)),
        dma((6,)), dma((6,)), dma((4,)), dma((4,)), dma((4,)), dma((4,)), dma((1,)),
        dma((3,)), dma((3,)), dma((4,)), dma((4,)),
    ]
    mid_out = pl.pallas_call(
        layer_kernel,
        out_shape=(
            jax.ShapeDtypeStruct((R, D), bf16),
            jax.ShapeDtypeStruct((R, D), bf16),
            jax.ShapeDtypeStruct((2, 2, CH, D), bf16),
            jax.ShapeDtypeStruct((4, 2, 2 * GX, D), bf16),
            jax.ShapeDtypeStruct((8, D), f32),
        ),
        in_specs=[hb] * 3 + [vm] * 4 + [hb] * 6,
        out_specs=(hb, hb, hb, hb, vm),
        scratch_shapes=scratch,
        compiler_params=pltpu.CompilerParams(
            collective_id=1, has_side_effects=True, vmem_limit_bytes=64 * 2**20 - 2**17
        ),
    )(
        tokens, out_grad, gate_weight, region_mask, attn_gain, ffn_gain, gate_bias,
        self_qkv.reshape(QR, D), cross_qkv.reshape(QR, D), self_out, cross_out, up_weight, down_weight,
    )
    out, tg, fin, gout, vec = mid_out
    total = 4 * CH + D
    wide = lambda *shape: jax.ShapeDtypeStruct(shape, f32)
    res = pl.pallas_call(
        widen_kernel,
        out_shape=(
            jax.ShapeDtypeStruct((R, D), bf16), jax.ShapeDtypeStruct((R, D), bf16),
            wide(D), wide(QR, D), wide(QR, D), wide(F, D), wide(F, D), wide(D, D), wide(D), wide(D),
            wide(CH, D), wide(CH, D),
        ),
        in_specs=[hb] * 4 + [vm],
        out_specs=(hb, hb, vm, hb, hb, hb, hb, hb, vm, vm, hb, hb),
        scratch_shapes=[
            pltpu.VMEM((total, D), bf16), pltpu.VMEM((total, D), f32), pltpu.VMEM((2, R, D), bf16),
            dma((5,)), dma((5, 2)), dma((4,)),
        ],
        compiler_params=pltpu.CompilerParams(vmem_limit_bytes=60 * 2**20),
    )(out, tg, fin, gout.reshape(D, D), vec)
    out, tg, again, sq, cq, so, co, gw, gb, fg, up, dn = res
    grads = (again, sq.reshape(3, F, D), cq.reshape(3, F, D), so, co, gw, gb, fg, up, dn)
    if outer > 1:
        first = (lax.axis_index("dp") % 8 == 0).astype(f32)
        grads = lax.psum(tuple(g * first for g in grads), "dp")
    return (out, tg) + tuple(grads)


def solution(mesh):
    rows = P(("dp", "mp"), None)
    weights = (P(), P(None, "mp", None), P(None, "mp", None), P("mp", None), P("mp", None), P(), P(), P(), P(None, "mp"), P("mp", None))
    return jax.shard_map(
        functools.partial(body, outer=mesh.shape["dp"] // 8),
        mesh=mesh,
        in_specs=(rows, P("dp", None)) + weights + (rows,),
        out_specs=(rows, rows) + weights,
        check_vma=False,
    )
```
